32 devices in a mesh: edge: 16 (over z, y, x), gate: 2 (over core).
Axes of the slice: x: 2, y: 2, z: 4, core: 2. Of those that a mesh axis runs over, the one named last changes fastest.
Arguments:
- node_state: bfloat16 [4096, 128], P('edge', 'gate'), may hold values from -4 to 4
- edge_feat: bfloat16 [16, 65536], P(None, 'edge'), may hold values from -5 to 5
- source: int32 [65536], P('edge'), may hold values from 0 to 4095, as said below
- target: int32 [65536], P('edge'), may hold values from 0 to 4095, as said below
- edge_mask: int32 [65536], P('edge'), may hold values 0 or 1
- node_mask: int32 [4096], P('edge'), may hold values 0 or 1
- net_first: bfloat16 [16, 128], replicated, may hold values from -1.5 to 1.5
- net_first_bias: bfloat16 [128], replicated, may hold values from -3 to 3
- net_second: bfloat16 [128, 16384], P(None, 'gate'), may hold values from -0.046875 to 0.046875
- net_second_bias: bfloat16 [16384], P('gate'), may hold values from -0.29882812 to 0.29882812
- gru_input: bfloat16 [3, 128, 128], P(None, None, 'gate'), may hold values from -0.5 to 0.5
- gru_hidden: bfloat16 [3, 128, 128], P(None, None, 'gate'), may hold values from -0.5 to 0.5
- gru_input_bias: bfloat16 [3, 128], P(None, 'gate'), may hold values from -2 to 2
- gru_hidden_bias: bfloat16 [3, 128], P(None, 'gate'), may hold values from -2 to 2
- cotangent: bfloat16 [4096, 128], P('edge', 'gate'), may hold values from -5 to 5
Outputs:
- new_state: bfloat16 [4096, 128], P('edge', 'gate')
- grad_state: float32 [4096, 128], P('edge', 'gate')
- grad_feat: float32 [16, 65536], P(None, 'edge')
- grad_first: float32 [16, 128], replicated
- grad_first_bias: float32 [128], replicated
- grad_second: float32 [128, 16384], P(None, 'gate')
- grad_second_bias: float32 [16384], P('gate')
- grad_input: float32 [3, 128, 128], P(None, None, 'gate')
- grad_hidden: float32 [3, 128, 128], P(None, None, 'gate')
- grad_input_bias: float32 [3, 128], P(None, 'gate')
- grad_hidden_bias: float32 [3, 128], P(None, 'gate')
The draws below stay inside these ranges and needn't reach their ends.
Inputs may be any that keep to these rules, and one draw needn't show every extreme that they name: `target`: edge e goes into one of the nodes b * 256 to (b + 1) * 256 - 1, with b = e // 4096; the first edge of each such block of edges goes into that block's first node. source[e] = max(target[e] - r, 0) with r of 1 to 64; the first edge of each block of 4096 edges has r = 64.
All inputs are finite; a program needn't handle non-finite values. No bound on the sum of `edge_mask` or of `node_mask` on one device may be relied on, other than what follows from the above.
Results may differ from the reference program's by a relative error of at most 0.04.
Values may be sent and summed in bfloat16 or wider, within the bound.
A program may use at most 128 MiB of HBM per device.

```python
import math
import jax
import jax.numpy as jnp
from jax import lax

H = 128
NETH = 128
FEAT = 16
NODE_DEV = 256
BORDER = 64
EDGE_DEV = 4096
NODES = 4096
EDGES = 65536


def edge_pairs(key):
    edge_index = jnp.arange(EDGES, dtype=jnp.int32)
    device_row = edge_index // EDGE_DEV
    first_edge = edge_index % EDGE_DEV == 0
    local_node = jax.random.randint(jax.random.fold_in(key, 11), (EDGES,), 0, NODE_DEV, dtype=jnp.int32)
    reach_back = jax.random.randint(jax.random.fold_in(key, 12), (EDGES,), 1, BORDER + 1, dtype=jnp.int32)
    local_node = jnp.where(first_edge, 0, local_node)
    reach_back = jnp.where(first_edge, BORDER, reach_back)
    target_node = device_row * NODE_DEV + local_node
    source_node = jnp.maximum(target_node - reach_back, 0)
    return (source_node.astype(jnp.int32), target_node.astype(jnp.int32))


def draw_source(key, part):
    return edge_pairs(key)[0]


def draw_target(key, part):
    return edge_pairs(key)[1]


def plant(array, rng, smallest, largest):
    dims = array.shape
    spot = [jax.random.randint(jax.random.fold_in(rng, axis), (), 0, dims[axis]) for axis in range(len(dims))]
    array = array.at[tuple(spot)].set(smallest)
    longest = dims.index(max(dims))
    spot[longest] = (spot[longest] + 1) % dims[longest]
    return array.at[tuple(spot)].set(largest)


def level_of(rng, shape, shards, smallest, high):
    level = 1.0
    for dim, blocks in shards:
        steps = jax.random.uniform(jax.random.fold_in(jax.random.fold_in(rng, 6), dim), (blocks,), jnp.float32, smallest / len(shards), high / len(shards))
        level = level * jnp.repeat(jnp.exp(steps), shape[dim] // blocks).reshape((-1,) + (1,) * (len(shape) - 1 - dim))
    return level


def noise(rng, dims, width, bound, split=(), held_as=jnp.bfloat16):
    entries = jax.random.normal(rng, dims, jnp.float32) * width
    if len(split) > 0:
        entries = level_of(rng, dims, split, -0.22, 0.18) * entries
    return jnp.clip(entries, min=-bound, max=bound).astype(held_as)


def setup_inputs(seed: int = 0) -> dict:
    keys = jax.random.split(jax.random.key(seed), 16)
    node_state = noise(keys[0], (NODES, H), 1.0, 4.0, ((0, 16), (1, 2)))
    edge_feat = noise(keys[1], (FEAT, EDGES), 1.0, 5.0, ((1, 16),))
    source = draw_source(jax.random.fold_in(keys[15], 71), 0)
    target = draw_target(jax.random.fold_in(keys[15], 71), 0)
    edge_mask = plant((jax.random.randint(keys[4], (EDGES,), 0, 8) < 7).astype(jnp.int32), jax.random.fold_in(keys[4], 1), 0, 1)
    node_mask = plant((jax.random.randint(keys[5], (NODES,), 0, 8) < 7).astype(jnp.int32), jax.random.fold_in(keys[5], 1), 0, 1)
    net_first = noise(keys[6], (FEAT, NETH), FEAT ** -0.5, 1.5)
    net_first_bias = noise(keys[7], (NETH,), 0.5, 3.0)
    net_second = noise(keys[8], (NETH, H * H), (NETH * H) ** -0.5, 0.046875, ((1, 2),))
    net_second_bias = noise(keys[9], (H * H,), 0.05, 0.29882812, ((0, 2),))
    gru_input = noise(keys[10], (3, H, H), H ** -0.5, 0.5, ((2, 2),))
    gru_hidden = noise(keys[11], (3, H, H), H ** -0.5, 0.5, ((2, 2),))
    gru_input_bias = noise(keys[12], (3, H), 0.3, 2.0, ((1, 2),))
    gru_hidden_bias = noise(keys[13], (3, H), 0.3, 2.0, ((1, 2),))
    cotangent = noise(keys[14], (NODES, H), 1.0, 5.0, ((0, 16), (1, 2)))
    return {"node_state": node_state, "edge_feat": edge_feat, "source": source, "target": target, "edge_mask": edge_mask, "node_mask": node_mask, "net_first": net_first, "net_first_bias": net_first_bias, "net_second": net_second, "net_second_bias": net_second_bias, "gru_input": gru_input, "gru_hidden": gru_hidden, "gru_input_bias": gru_input_bias, "gru_hidden_bias": gru_hidden_bias, "cotangent": cotangent}


@jax.custom_vjp
def low(v):
    return lax.optimization_barrier(v.astype(jnp.bfloat16)).astype(jnp.float32)

@jax.custom_vjp
def low_back(v):
    return v

def low_keep(v):
    return (low(v), None)

def low_pass(kept, grad):
    return (grad,)

def back_keep(v):
    return (v, None)

def back_low(kept, grad):
    return (low(grad),)
low.defvjp(low_keep, low_pass)
low_back.defvjp(back_keep, back_low)

def reference(node_state, edge_feat, source, target, edge_mask, node_mask, net_first, net_first_bias, net_second, net_second_bias, gru_input, gru_hidden, gru_input_bias, gru_hidden_bias, cotangent):
    highest = lax.Precision.HIGHEST
    block_rows = math.gcd(EDGES, 2048)
    block_count = EDGES // block_rows
    source_rows = source.reshape(block_count, block_rows)
    target_rows = target.reshape(block_count, block_rows)
    mask_rows = edge_mask.astype(jnp.float32).reshape(block_count, block_rows)
    node_keep = node_mask.astype(jnp.float32)[:, None]
    feat_blocks = edge_feat.astype(jnp.float32).reshape(FEAT, block_count, block_rows).transpose(1, 0, 2)

    def forward(states, feat_all, first_weight, first_bias, second_weight, second_bias, input_weight, hidden_weight, input_bias, hidden_bias):

        def edge_step(summed, block_items):
            feat_blk, source_blk, target_blk, mask_blk = block_items
            pre_act = low_back(jnp.dot(feat_blk.T, first_weight, precision=highest, preferred_element_type=jnp.float32) + first_bias)
            hidden = low(jax.nn.silu(pre_act))
            matrices = low(low_back(jnp.dot(hidden, second_weight, precision=highest, preferred_element_type=jnp.float32) + second_bias))
            matrices = matrices.reshape(block_rows, H, H)
            sources = states[source_blk]
            message = jnp.einsum('eoi,ei->eo', matrices, sources, precision=highest)
            message = low(low_back(message)) * mask_blk[:, None]
            return (summed + jax.ops.segment_sum(message, target_blk, num_segments=NODES), None)
        summed, _ = lax.scan(jax.checkpoint(edge_step), jnp.zeros((NODES, H), jnp.float32), (feat_all, source_rows, target_rows, mask_rows))
        incoming = low(summed)
        input_pre = low_back(jnp.einsum('nc,kcj->knj', incoming, input_weight, precision=highest) + input_bias[:, None, :])
        hidden_pre = low_back(jnp.einsum('nc,kcj->knj', states, hidden_weight, precision=highest) + hidden_bias[:, None, :])
        reset_gate = jax.nn.sigmoid(input_pre[0] + hidden_pre[0])
        update_gate = jax.nn.sigmoid(input_pre[1] + hidden_pre[1])
        candidate = jnp.tanh(input_pre[2] + reset_gate * hidden_pre[2])
        return node_keep * ((1.0 - update_gate) * candidate + update_gate * states)
    inputs_list = (node_state.astype(jnp.float32), feat_blocks, net_first.astype(jnp.float32), net_first_bias.astype(jnp.float32), net_second.astype(jnp.float32), net_second_bias.astype(jnp.float32), gru_input.astype(jnp.float32), gru_hidden.astype(jnp.float32), gru_input_bias.astype(jnp.float32), gru_hidden_bias.astype(jnp.float32))
    output_state, pullback = jax.vjp(forward, *inputs_list)
    gradients = pullback(cotangent.astype(jnp.float32))
    grad_feat = gradients[1].transpose(1, 0, 2).reshape(FEAT, EDGES)
    return (output_state.astype(jnp.bfloat16), gradients[0], grad_feat, gradients[2], gradients[3], gradients[4], gradients[5], gradients[6], gradients[7], gradients[8], gradients[9])
```

```python
import functools

import jax
import jax.numpy as jnp
from jax import lax
from jax.experimental import pallas as pl
from jax.experimental.pallas import tpu as pltpu
from jax.sharding import PartitionSpec as P

BORDER = 64
GROUP = 16
HALF = 8
TILE = 256
LANES = 128
ROWS = 32
VMEM_LIMIT = 56 * 1024 * 1024

NN = ((1,), (0,))
NT = ((1,), (1,))
TN = ((0,), (0,))
F32 = jnp.float32
BF16 = jnp.bfloat16


def dot(left, right, dims=NN):
    return lax.dot_general(left, right, (dims, ((), ())), preferred_element_type=F32)


def iota(shape, dim):
    return lax.broadcasted_iota(jnp.int32, shape, dim)


def extended_first(first_ref, bias_ref):
    extra = jnp.where(iota((ROWS - 16, LANES), 0) == 2, bias_ref[...].astype(F32), 0.0)
    return jnp.concatenate([first_ref[...].astype(F32), extra], axis=0).astype(BF16)


def tile_masks(slot_row):
    place = slot_row.astype(jnp.int32) - 1
    low = jnp.logical_and(place >= 0, place < HALF)
    high = place >= HALF
    within = jnp.where(high, place - HALF, place)
    return low, high, within


def halves(hidden, low, high):
    return jnp.concatenate(
        [jnp.where(low, hidden, 0.0), jnp.where(high, hidden, 0.0)], axis=0
    ).astype(BF16)


def keep_within(values, within):
    rows, width = values.shape
    match = iota((HALF, width), 0) == within
    kept = jnp.where(match[None], values.reshape(rows // HALF, HALF, width), 0.0)
    return kept.reshape(rows, width).astype(BF16)


def target_hot(target_row, node_count):
    width = target_row.shape[1]
    return (iota((node_count, width), 0) + 1 == target_row.astype(jnp.int32)).astype(F32).astype(BF16)


def lane_hot(lane_ref, out_ref):
    chunks = lane_ref.shape[0]
    for c in range(chunks):
        row = lane_ref[c : c + 1, :].astype(jnp.int32)
        out_ref[:, c * LANES : (c + 1) * LANES] = (
            (iota((TILE, LANES), 0) == row).astype(F32).astype(BF16)
        )


def forward_kernel(
    source_ref, target_ref, mask_ref, feat_ref, state_ref, first_ref, first_bias_ref, second_ref, second_bias_ref,
    incoming_ref, tiles_ref, table_ref, tile_ref, lane_ref, meta_ref,
    counts_ref, spread_ref, hot_ref, bias_ref, total_ref, meta_smem, sem,
):
    chunks = source_ref.shape[0]
    node_count, half_width = incoming_ref.shape
    groups = table_ref.shape[0]
    first_node = lax.axis_index("edge") * node_count

    group_rows = []
    for c in range(chunks):
        slot = source_ref[c : c + 1, :] - first_node + BORDER
        group = lax.shift_right_logical(slot, 4)
        group_rows.append(group)
        counts_ref[c * ROWS : (c + 1) * ROWS, :] = (
            (iota((ROWS, LANES), 0) == group).astype(F32).astype(BF16)
        )
    above = jnp.where(
        iota((LANES, 2 * LANES), 0) < iota((LANES, 2 * LANES), 1), 1.0, 0.0
    ).astype(BF16)
    sums = dot(counts_ref[...], above)
    running = jnp.zeros((ROWS, LANES), F32)
    ranks = []
    for c in range(chunks):
        hot = counts_ref[c * ROWS : (c + 1) * ROWS, :].astype(F32)
        part = sums[c * ROWS : (c + 1) * ROWS]
        ranks.append(jnp.sum(hot * (part[:, :LANES] + running), axis=0, keepdims=True))
        running = running + part[:, LANES:]
    extra = jnp.floor(jnp.maximum(running - 1.0, 0.0) * (1.0 / TILE))
    before = (iota((ROWS, ROWS), 1) < iota((ROWS, ROWS), 0)).astype(F32).astype(BF16)
    extra_start = dot(before, extra.astype(BF16))
    extra_end = extra_start + extra
    upcoming = iota((ROWS, LANES), 1).astype(F32)
    extra_group = jnp.sum((extra_end <= upcoming).astype(F32), axis=0, keepdims=True)
    extra_group = jnp.minimum(extra_group, groups - 1.0)
    extra_count = jnp.sum(extra, axis=0, keepdims=True)
    row8 = iota((8, LANES), 0)
    meta_ref[...] = jnp.where(row8 == 0, extra_group, jnp.where(row8 == 1, extra_count, 0.0)).astype(jnp.int32)
    copy = pltpu.make_async_copy(meta_ref, meta_smem, sem)
    copy.start()

    row16 = iota((ROWS - 16, LANES), 0)
    for c in range(chunks):
        hot = counts_ref[c * ROWS : (c + 1) * ROWS, :].astype(F32)
        over = jnp.floor(ranks[c] * (1.0 / TILE))
        start = jnp.sum(hot * extra_start, axis=0, keepdims=True)
        group = group_rows[c].astype(F32)
        tile = jnp.where(over == 0.0, group, groups - 1.0 + start + over)
        lane = ranks[c] - TILE * over
        tile_ref[c : c + 1, :] = tile
        lane_ref[c : c + 1, :] = lane
        slot = source_ref[c : c + 1, :] - first_node + BORDER
        place = (slot - lax.shift_left(group_rows[c], 4) + 1).astype(F32)
        target = jnp.where(
            mask_ref[c : c + 1, :] > 0, target_ref[c : c + 1, :] - first_node + 1, 0
        ).astype(F32)
        more = jnp.where(row16 == 0, target, jnp.where(row16 == 1, place, jnp.where(row16 == 2, 1.0, 0.0)))
        values = jnp.concatenate([feat_ref[:, c * LANES : (c + 1) * LANES].astype(F32), more], axis=0)
        for t in range(groups):
            spread_ref[t * ROWS : (t + 1) * ROWS, c * LANES : (c + 1) * LANES] = jnp.where(
                tile == float(t), values, 0.0
            ).astype(BF16)
        spread_ref[groups * ROWS : (groups + 1) * ROWS, c * LANES : (c + 1) * LANES] = values.astype(BF16)
    lane_hot(lane_ref, hot_ref)
    moved = dot(spread_ref[: groups * ROWS, :], hot_ref[...], NT)
    tiles_ref[:groups] = moved.reshape(groups, ROWS, TILE).astype(BF16)
    copy.wait()
    extra_total = meta_smem[1, 0]

    def move_extra(u, carry):
        wanted = (groups + u).astype(F32)
        pieces = []
        for c in range(chunks):
            pieces.append(
                jnp.where(
                    tile_ref[c : c + 1, :] == wanted,
                    spread_ref[groups * ROWS : (groups + 1) * ROWS, c * LANES : (c + 1) * LANES].astype(F32),
                    0.0,
                ).astype(BF16)
            )
        tiles_ref[groups + u] = dot(jnp.concatenate(pieces, axis=1), hot_ref[...], NT).astype(BF16)
        return carry

    lax.fori_loop(0, extra_total, move_extra, 0)

    states = state_ref[...]

    def table_pair(p, carry):
        pair = second_ref[:, pl.ds(pl.multiple_of(p * 2 * LANES, 2 * LANES), 2 * LANES)]
        both = jnp.concatenate([pair[:, :LANES], pair[:, LANES:]], axis=0)
        product = dot(states, both, NT).reshape(groups, 2, HALF, 2 * LANES)
        for a in range(2):
            rows = jnp.concatenate([product[:, a, :, :LANES], product[:, a, :, LANES:]], axis=1)
            table_ref[:, pl.ds(pl.multiple_of(p * 16, 16), 16), a * LANES : (a + 1) * LANES] = rows.astype(BF16)
        return carry

    lax.fori_loop(0, half_width // 2, table_pair, 0, unroll=2)
    bias_ref[...] = dot(states, second_bias_ref[...], NT)

    first_t = extended_first(first_ref, first_bias_ref)
    fold = (iota((half_width, half_width * HALF), 1) // HALF == iota((half_width, half_width * HALF), 0)).astype(F32).astype(BF16)

    def messages(t, group):
        held = tiles_ref[t]
        low, high, within = tile_masks(held[17:18, :].astype(F32))
        pre = dot(first_t, held, TN)
        hidden = pre * jax.nn.sigmoid(pre)
        spread = dot(table_ref[group], halves(hidden, low, high))
        message = dot(fold, keep_within(spread, within))
        place = held[17:18, :].astype(jnp.int32) - 1
        slot_hot = (iota((GROUP, TILE), 0) == place).astype(F32).astype(BF16)
        bias = bias_ref[pl.ds(pl.multiple_of(group * GROUP, GROUP), GROUP), :].astype(BF16)
        message = (message + dot(bias, slot_hot, TN)).astype(BF16)
        hot = target_hot(held[16:17, :].astype(F32), node_count)
        total_ref[...] += dot(hot, message, NT)

    total_ref[...] = jnp.zeros_like(total_ref)

    def group_messages(g, carry):
        messages(g, g)
        return carry

    def extra_messages(u, carry):
        messages(groups + u, meta_smem[0, u])
        return carry

    lax.fori_loop(0, groups, group_messages, 0)
    lax.fori_loop(0, extra_total, extra_messages, 0)
    incoming_ref[...] = total_ref[...].astype(BF16)


def backward_kernel(
    meta_ref, grad_ref, state_ref, first_ref, first_bias_ref, second_ref, second_bias_ref, tiles_ref, table_ref,
    tile_ref, lane_ref,
    second_grad_ref, second_bias_grad_ref, source_grad_ref, feat_grad_ref, first_grad_ref,
    held_ref, sums_ref, part_ref, hot_ref, rows_ref,
):
    node_count, half_width = grad_ref.shape
    groups = table_ref.shape[0]
    chunks = tile_ref.shape[0]
    slots = groups * GROUP
    extra_total = meta_ref[1, 0]
    first_t = extended_first(first_ref, first_bias_ref)
    grad_t = grad_ref[...].astype(F32).T
    wide = jnp.broadcast_to(grad_t[:, None, :], (half_width, HALF, node_count)).reshape(half_width * HALF, node_count)
    grad_rows = jnp.concatenate([wide, grad_t], axis=0).astype(BF16)
    lane_hot(lane_ref, hot_ref)
    first_grad_ref[...] = jnp.zeros_like(first_grad_ref)

    def work(t, group):
        held = tiles_ref[t]
        low, high, within = tile_masks(held[17:18, :].astype(F32))
        pre = dot(first_t, held, TN)
        logistic = jax.nn.sigmoid(pre)
        hidden = halves(pre * logistic, low, high)
        hot = target_hot(held[16:17, :].astype(F32), node_count)
        picked = dot(grad_rows, hot)
        spread = keep_within(picked[: half_width * HALF], within)
        product = dot(spread, hidden, NT)
        place = held[17:18, :].astype(jnp.int32) - 1
        slot_hot = (iota((GROUP, TILE), 0) == place).astype(F32).astype(BF16)
        sums = dot(slot_hot, picked[half_width * HALF :].astype(BF16), NT)
        grad_hidden = dot(table_ref[group], spread, TN)
        grad_hidden = jnp.where(low, grad_hidden[:LANES], grad_hidden[LANES:])
        grad_pre = (grad_hidden * logistic * (1.0 + pre * (1.0 - logistic))).astype(BF16)
        part_ref[pl.ds(pl.multiple_of(t * 16, 16), 16), :] = dot(first_ref[...], grad_pre).astype(BF16)
        first_grad_ref[...] += dot(held, grad_pre, NT)
        return product, sums

    def group_work(g, carry):
        product, sums = work(g, g)
        held_ref[g] = product
        sums_ref[pl.ds(pl.multiple_of(g * GROUP, GROUP), GROUP), :] = sums
        return carry

    def extra_work(u, carry):
        group = meta_ref[0, u]
        product, sums = work(groups + u, group)
        held_ref[group] += product
        sums_ref[pl.ds(pl.multiple_of(group * GROUP, GROUP), GROUP), :] += sums
        return carry

    lax.fori_loop(0, groups, group_work, 0)
    lax.fori_loop(0, extra_total, extra_work, 0)

    for c in range(chunks):
        cols = slice(c * LANES, (c + 1) * LANES)
        back = dot(part_ref[: groups * 16, :], hot_ref[:, cols])
        tile = tile_ref[c : c + 1, :]
        total = jnp.zeros((16, LANES), F32)
        for t in range(groups):
            total = total + jnp.where(tile == float(t), back[t * 16 : (t + 1) * 16], 0.0)
        feat_grad_ref[:, cols] = total

    def extra_back(u, carry):
        wanted = (groups + u).astype(F32)
        part = part_ref[pl.ds(pl.multiple_of((groups + u) * 16, 16), 16), :]
        for c in range(chunks):
            cols = slice(c * LANES, (c + 1) * LANES)
            back = dot(part, hot_ref[:, cols])
            feat_grad_ref[:, cols] += jnp.where(tile_ref[c : c + 1, :] == wanted, back, 0.0)
        return carry

    lax.fori_loop(0, extra_total, extra_back, 0)

    states = state_ref[...].astype(F32).reshape(groups, 2, HALF, LANES)
    states = jnp.concatenate(
        [states[:, a].reshape(slots // 2, LANES) for a in range(2)], axis=0
    ).astype(BF16)
    rows_ref[...] = jnp.zeros_like(rows_ref)

    def pair_grads(p, carry):
        quarter = []
        for q in range(2):
            rows = held_ref[:, pl.ds(pl.multiple_of(p * 16 + q * HALF, HALF), HALF), :].reshape(slots // 2, 2 * LANES)
            rows = rows.astype(BF16)
            quarter.append(jnp.concatenate([rows[:, :LANES], rows[:, LANES:]], axis=0))
        cols = pl.ds(pl.multiple_of(p * 2 * LANES, 2 * LANES), 2 * LANES)
        pair = second_ref[:, cols]
        second_grad_ref[:, cols] = jnp.concatenate(
            [dot(quarter[0], states, TN), dot(quarter[1], states, TN)], axis=1
        ).astype(BF16)
        rows_ref[...] += dot(
            jnp.concatenate(quarter, axis=1), jnp.concatenate([pair[:, :LANES], pair[:, LANES:]], axis=0)
        )
        return carry

    lax.fori_loop(0, half_width // 2, pair_grads, 0)
    sums = sums_ref[...].astype(BF16)
    second_bias_grad_ref[...] = dot(sums, state_ref[...], TN)
    ordered = jnp.stack(
        [rows_ref[a * (slots // 2) : (a + 1) * (slots // 2), :].reshape(groups, HALF, LANES) for a in range(2)], axis=1
    ).reshape(slots, LANES)
    source_grad_ref[...] = ordered + dot(sums, second_bias_ref[...])


def passed_along(block, axis, distance):
    devices = range(lax.axis_size(axis))
    route = [(i - distance, i) for i in devices if i - distance in devices]
    return lax.ppermute(block, axis, route)


def per_device(
    node_state, edge_feat, source, target, edge_mask, node_mask, net_first, net_first_bias, net_second,
    net_second_bias, gru_input, gru_hidden, gru_input_bias, gru_hidden_bias, cotangent,
):
    node_count, half_width = node_state.shape
    edge_count = source.shape[0]
    width = 2 * half_width
    chunks = edge_count // LANES
    slots = BORDER + node_count
    groups = slots // GROUP
    tiles = groups + edge_count // TILE - 1
    full_state = lax.all_gather(node_state, "gate", axis=1, tiled=True)
    earlier = passed_along(full_state[node_count - BORDER :], "edge", 1)
    extended = jnp.concatenate([earlier, full_state], axis=0)
    params = pltpu.CompilerParams(vmem_limit_bytes=VMEM_LIMIT)
    first_bias = net_first_bias.reshape(1, width)
    second_bias = net_second_bias.reshape(half_width, width)
    shape = jax.ShapeDtypeStruct
    incoming, moved, table, tile_rows, lane_rows, meta = pl.pallas_call(
        forward_kernel,
        out_shape=(
            shape((node_count, half_width), BF16),
            shape((tiles, ROWS, TILE), BF16),
            shape((groups, half_width * HALF, 2 * width), BF16),
            shape((chunks, LANES), F32),
            shape((chunks, LANES), F32),
            shape((8, LANES), jnp.int32),
        ),
        scratch_shapes=[
            pltpu.VMEM((chunks * ROWS, LANES), BF16),
            pltpu.VMEM(((groups + 1) * ROWS, edge_count), BF16),
            pltpu.VMEM((TILE, edge_count), BF16),
            pltpu.VMEM((slots, half_width), F32),
            pltpu.VMEM((node_count, half_width), F32),
            pltpu.SMEM((8, LANES), jnp.int32),
            pltpu.SemaphoreType.DMA,
        ],
        compiler_params=params,
        name="forward_edges",
    )(
        source.reshape(chunks, LANES), target.reshape(chunks, LANES), edge_mask.reshape(chunks, LANES),
        edge_feat, extended, net_first, first_bias, net_second, second_bias,
    )

    message_full = lax.all_gather(incoming, "gate", axis=1, tiled=True)
    input_pre = (
        jnp.einsum("nc,kcj->knj", message_full, gru_input, preferred_element_type=F32)
        + gru_input_bias.astype(F32)[:, None, :]
    )
    hidden_pre = (
        jnp.einsum("nc,kcj->knj", full_state, gru_hidden, preferred_element_type=F32)
        + gru_hidden_bias.astype(F32)[:, None, :]
    )
    own_state = node_state.astype(F32)
    reset_gate = jax.nn.sigmoid(input_pre[0] + hidden_pre[0])
    update_gate = jax.nn.sigmoid(input_pre[1] + hidden_pre[1])
    candidate = jnp.tanh(input_pre[2] + reset_gate * hidden_pre[2])
    node_keep = node_mask.astype(F32)[:, None]
    new_state = (node_keep * ((1.0 - update_gate) * candidate + update_gate * own_state)).astype(BF16)
    grad_output = cotangent.astype(F32) * node_keep
    grad_own = grad_output * update_gate
    grad_cand_pre = grad_output * (1.0 - update_gate) * (1.0 - candidate * candidate)
    grad_update_pre = grad_output * (own_state - candidate) * update_gate * (1.0 - update_gate)
    grad_reset_pre = grad_cand_pre * hidden_pre[2] * reset_gate * (1.0 - reset_gate)
    grad_input_pre = jnp.stack([grad_reset_pre, grad_update_pre, grad_cand_pre]).astype(BF16)
    grad_hidden_pre = jnp.stack([grad_reset_pre, grad_update_pre, grad_cand_pre * reset_gate]).astype(BF16)
    input_weight_grad = jnp.einsum("nc,knj->kcj", message_full, grad_input_pre, preferred_element_type=F32)
    hidden_weight_grad = jnp.einsum("nc,knj->kcj", full_state, grad_hidden_pre, preferred_element_type=F32)
    input_bias_grad = jnp.sum(grad_input_pre.astype(F32), axis=1)
    hidden_bias_grad = jnp.sum(grad_hidden_pre.astype(F32), axis=1)
    input_partial = jnp.einsum("knj,kcj->nc", grad_input_pre, gru_input, preferred_element_type=F32)
    state_partial = jnp.einsum("knj,kcj->nc", grad_hidden_pre, gru_hidden, preferred_element_type=F32)
    message_grad = lax.psum_scatter(input_partial, "gate", scatter_dimension=1, tiled=True).astype(BF16)

    vmem = pl.BlockSpec(memory_space=pltpu.VMEM)
    second_grad, second_bias_grad, source_grads, feat_part, first_part = pl.pallas_call(
        backward_kernel,
        out_shape=(
            shape((width, half_width * width), BF16),
            shape((half_width, width), F32),
            shape((slots, width), F32),
            shape((16, edge_count), F32),
            shape((ROWS, width), F32),
        ),
        in_specs=[pl.BlockSpec(memory_space=pltpu.SMEM)] + [vmem] * 10,
        out_specs=(vmem,) * 5,
        scratch_shapes=[
            pltpu.VMEM((groups, half_width * HALF, 2 * width), F32),
            pltpu.VMEM((slots, half_width), F32),
            pltpu.VMEM((tiles * 16, TILE), BF16),
            pltpu.VMEM((TILE, edge_count), BF16),
            pltpu.VMEM((slots, width), F32),
        ],
        compiler_params=params,
        name="backward_edges",
    )(
        meta, message_grad, extended, net_first, first_bias, net_second, second_bias, moved, table, tile_rows, lane_rows,
    )

    grad_feat = lax.psum(feat_part, "gate")
    first_sum = lax.psum(first_part, ("edge", "gate"))
    returned = passed_along(source_grads[:BORDER].astype(BF16), "edge", -1).astype(F32)
    own_grads = source_grads[BORDER:] + state_partial
    own_grads = jnp.concatenate([own_grads[: node_count - BORDER], own_grads[node_count - BORDER :] + returned], axis=0)
    grad_state = (
        lax.psum_scatter(own_grads.astype(BF16), "gate", scatter_dimension=1, tiled=True).astype(F32) + grad_own
    )
    second_sum = lax.psum(second_grad, "edge").astype(F32)
    bias_sum, input_sum, hidden_sum, input_bias_sum, hidden_bias_sum = lax.psum(
        (second_bias_grad.reshape(half_width * width), input_weight_grad, hidden_weight_grad, input_bias_grad, hidden_bias_grad),
        "edge",
    )
    return (
        new_state, grad_state, grad_feat, first_sum[:16], first_sum[18], second_sum, bias_sum, input_sum, hidden_sum,
        input_bias_sum, hidden_bias_sum,
    )


def solution(mesh):
    return jax.shard_map(
        per_device,
        mesh=mesh,
        in_specs=(
            P("edge", "gate"), P(None, "edge"), P("edge"), P("edge"), P("edge"), P("edge"), P(), P(), P(None, "gate"),
            P("gate"), P(None, None, "gate"), P(None, None, "gate"), P(None, "gate"), P(None, "gate"), P("edge", "gate"),
        ),
        out_specs=(
            P("edge", "gate"), P("edge", "gate"), P(None, "edge"), P(), P(), P(None, "gate"), P("gate"),
            P(None, None, "gate"), P(None, None, "gate"), P(None, "gate"), P(None, "gate"),
        ),
        check_vma=False,
    )
```

```python
import functools

import jax
import jax.numpy as jnp
from jax import lax
from jax.experimental import pallas as pl
from jax.experimental.pallas import tpu as pltpu
from jax.sharding import PartitionSpec as P

BORDER = 64
GROUP = 16
HALF = 8
TILE = 256
LANES = 128
ROWS = 32
VMEM_LIMIT = 56 * 1024 * 1024

NN = ((1,), (0,))
NT = ((1,), (1,))
TN = ((0,), (0,))
F32 = jnp.float32
BF16 = jnp.bfloat16


def dot(left, right, dims=NN):
    return lax.dot_general(left, right, (dims, ((), ())), preferred_element_type=F32)


def iota(shape, dim):
    return lax.broadcasted_iota(jnp.int32, shape, dim)


def extended_first(first_ref, bias_ref):
    extra = jnp.where(iota((ROWS - 16, LANES), 0) == 2, bias_ref[...].astype(F32), 0.0)
    return jnp.concatenate([first_ref[...].astype(F32), extra], axis=0).astype(BF16)


def tile_masks(slot_row):
    place = slot_row.astype(jnp.int32) - 1
    low = jnp.logical_and(place >= 0, place < HALF)
    high = place >= HALF
    within = jnp.where(high, place - HALF, place)
    return low, high, within


def halves(hidden, low, high):
    return jnp.concatenate(
        [jnp.where(low, hidden, 0.0), jnp.where(high, hidden, 0.0)], axis=0
    ).astype(BF16)


def keep_within(values, within):
    rows, width = values.shape
    match = iota((HALF, width), 0) == within
    kept = jnp.where(match[None], values.reshape(rows // HALF, HALF, width), 0.0)
    return kept.reshape(rows, width).astype(BF16)


def target_hot(target_row, node_count):
    width = target_row.shape[1]
    return (iota((node_count, width), 0) + 1 == target_row.astype(jnp.int32)).astype(F32).astype(BF16)


def lane_hot(lane_ref, out_ref):
    chunks = lane_ref.shape[0]
    for c in range(chunks):
        row = lane_ref[c : c + 1, :].astype(jnp.int32)
        out_ref[:, c * LANES : (c + 1) * LANES] = (
            (iota((TILE, LANES), 0) == row).astype(F32).astype(BF16)
        )


def forward_kernel(
    source_ref, target_ref, mask_ref, feat_ref, state_ref, first_ref, first_bias_ref, second_ref, second_bias_ref,
    incoming_ref, tiles_ref, table_ref, tile_ref, lane_ref, meta_ref,
    counts_ref, spread_ref, hot_ref, bias_ref, total_ref, meta_smem, sem,
):
    chunks = source_ref.shape[0]
    node_count, half_width = incoming_ref.shape
    groups = table_ref.shape[0]
    first_node = lax.axis_index("edge") * node_count

    group_rows = []
    for c in range(chunks):
        slot = source_ref[c : c + 1, :] - first_node + BORDER
        group = lax.shift_right_logical(slot, 4)
        group_rows.append(group)
        counts_ref[c * ROWS : (c + 1) * ROWS, :] = (
            (iota((ROWS, LANES), 0) == group).astype(F32).astype(BF16)
        )
    above = jnp.where(
        iota((LANES, 2 * LANES), 0) < iota((LANES, 2 * LANES), 1), 1.0, 0.0
    ).astype(BF16)
    sums = dot(counts_ref[...], above)
    running = jnp.zeros((ROWS, LANES), F32)
    ranks = []
    for c in range(chunks):
        hot = counts_ref[c * ROWS : (c + 1) * ROWS, :].astype(F32)
        part = sums[c * ROWS : (c + 1) * ROWS]
        ranks.append(jnp.sum(hot * (part[:, :LANES] + running), axis=0, keepdims=True))
        running = running + part[:, LANES:]
    extra = jnp.floor(jnp.maximum(running - 1.0, 0.0) * (1.0 / TILE))
    before = (iota((ROWS, ROWS), 1) < iota((ROWS, ROWS), 0)).astype(F32).astype(BF16)
    extra_start = dot(before, extra.astype(BF16))
    extra_end = extra_start + extra
    upcoming = iota((ROWS, LANES), 1).astype(F32)
    extra_group = jnp.sum((extra_end <= upcoming).astype(F32), axis=0, keepdims=True)
    extra_group = jnp.minimum(extra_group, groups - 1.0)
    extra_count = jnp.sum(extra, axis=0, keepdims=True)
    row8 = iota((8, LANES), 0)
    meta_ref[...] = jnp.where(row8 == 0, extra_group, jnp.where(row8 == 1, extra_count, 0.0)).astype(jnp.int32)
    copy = pltpu.make_async_copy(meta_ref, meta_smem, sem)
    copy.start()

    row16 = iota((ROWS - 16, LANES), 0)
    for c in range(chunks):
        hot = counts_ref[c * ROWS : (c + 1) * ROWS, :].astype(F32)
        over = jnp.floor(ranks[c] * (1.0 / TILE))
        start = jnp.sum(hot * extra_start, axis=0, keepdims=True)
        group = group_rows[c].astype(F32)
        tile = jnp.where(over == 0.0, group, groups - 1.0 + start + over)
        lane = ranks[c] - TILE * over
        tile_ref[c : c + 1, :] = tile
        lane_ref[c : c + 1, :] = lane
        slot = source_ref[c : c + 1, :] - first_node + BORDER
        place = (slot - lax.shift_left(group_rows[c], 4) + 1).astype(F32)
        target = jnp.where(
            mask_ref[c : c + 1, :] > 0, target_ref[c : c + 1, :] - first_node + 1, 0
        ).astype(F32)
        more = jnp.where(row16 == 0, target, jnp.where(row16 == 1, place, jnp.where(row16 == 2, 1.0, 0.0)))
        values = jnp.concatenate([feat_ref[:, c * LANES : (c + 1) * LANES].astype(F32), more], axis=0)
        for t in range(groups):
            spread_ref[t * ROWS : (t + 1) * ROWS, c * LANES : (c + 1) * LANES] = jnp.where(
                tile == float(t), values, 0.0
            ).astype(BF16)
        spread_ref[groups * ROWS : (groups + 1) * ROWS, c * LANES : (c + 1) * LANES] = values.astype(BF16)
    lane_hot(lane_ref, hot_ref)
    moved = dot(spread_ref[: groups * ROWS, :], hot_ref[...], NT)
    tiles_ref[:groups] = moved.reshape(groups, ROWS, TILE).astype(BF16)
    copy.wait()
    extra_total = meta_smem[1, 0]

    def move_extra(u, carry):
        wanted = (groups + u).astype(F32)
        pieces = []
        for c in range(chunks):
            pieces.append(
                jnp.where(
                    tile_ref[c : c + 1, :] == wanted,
                    spread_ref[groups * ROWS : (groups + 1) * ROWS, c * LANES : (c + 1) * LANES].astype(F32),
                    0.0,
                ).astype(BF16)
            )
        tiles_ref[groups + u] = dot(jnp.concatenate(pieces, axis=1), hot_ref[...], NT).astype(BF16)
        return carry

    lax.fori_loop(0, extra_total, move_extra, 0)

    states = state_ref[...]

    def table_pair(p, carry):
        pair = second_ref[:, pl.ds(pl.multiple_of(p * 2 * LANES, 2 * LANES), 2 * LANES)]
        both = jnp.concatenate([pair[:, :LANES], pair[:, LANES:]], axis=0)
        product = dot(states, both, NT).reshape(groups, 2, HALF, 2 * LANES)
        for a in range(2):
            rows = jnp.concatenate([product[:, a, :, :LANES], product[:, a, :, LANES:]], axis=1)
            table_ref[:, pl.ds(pl.multiple_of(p * 16, 16), 16), a * LANES : (a + 1) * LANES] = rows.astype(BF16)
        return carry

    lax.fori_loop(0, half_width // 2, table_pair, 0, unroll=2)
    bias_ref[...] = dot(states, second_bias_ref[...], NT)

    first_t = extended_first(first_ref, first_bias_ref)
    fold = (iota((half_width, half_width * HALF), 1) // HALF == iota((half_width, half_width * HALF), 0)).astype(F32).astype(BF16)

    def messages(t, group):
        held = tiles_ref[t]
        low, high, within = tile_masks(held[17:18, :].astype(F32))
        pre = dot(first_t, held, TN)
        hidden = pre * jax.nn.sigmoid(pre)
        spread = dot(table_ref[group], halves(hidden, low, high))
        message = dot(fold, keep_within(spread, within))
        place = held[17:18, :].astype(jnp.int32) - 1
        slot_hot = (iota((GROUP, TILE), 0) == place).astype(F32).astype(BF16)
        bias = bias_ref[pl.ds(pl.multiple_of(group * GROUP, GROUP), GROUP), :].astype(BF16)
        message = (message + dot(bias, slot_hot, TN)).astype(BF16)
        hot = target_hot(held[16:17, :].astype(F32), node_count)
        total_ref[...] += dot(hot, message, NT)

    total_ref[...] = jnp.zeros_like(total_ref)

    def group_messages(g, carry):
        messages(g, g)
        return carry

    def extra_messages(u, carry):
        messages(groups + u, meta_smem[0, u])
        return carry

    lax.fori_loop(0, groups, group_messages, 0)
    lax.fori_loop(0, extra_total, extra_messages, 0)
    incoming_ref[...] = total_ref[...].astype(BF16)


def backward_kernel(
    meta_ref, grad_ref, state_ref, first_ref, first_bias_ref, second_ref, second_bias_ref, tiles_ref, table_ref,
    tile_ref, lane_ref,
    second_grad_ref, second_bias_grad_ref, source_grad_ref, feat_grad_ref, first_grad_ref,
    held_ref, sums_ref, part_ref, hot_ref, rows_ref,
):
    node_count, half_width = grad_ref.shape
    groups = table_ref.shape[0]
    chunks = tile_ref.shape[0]
    slots = groups * GROUP
    extra_total = meta_ref[1, 0]
    first_t = extended_first(first_ref, first_bias_ref)
    grad_t = grad_ref[...].astype(F32).T
    wide = jnp.broadcast_to(grad_t[:, None, :], (half_width, HALF, node_count)).reshape(half_width * HALF, node_count)
    grad_rows = jnp.concatenate([wide, grad_t], axis=0).astype(BF16)
    lane_hot(lane_ref, hot_ref)
    first_grad_ref[...] = jnp.zeros_like(first_grad_ref)

    def work(t, group):
        held = tiles_ref[t]
        low, high, within = tile_masks(held[17:18, :].astype(F32))
        pre = dot(first_t, held, TN)
        logistic = jax.nn.sigmoid(pre)
        hidden = halves(pre * logistic, low, high)
        hot = target_hot(held[16:17, :].astype(F32), node_count)
        picked = dot(grad_rows, hot)
        spread = keep_within(picked[: half_width * HALF], within)
        product = dot(spread, hidden, NT)
        place = held[17:18, :].astype(jnp.int32) - 1
        slot_hot = (iota((GROUP, TILE), 0) == place).astype(F32).astype(BF16)
        sums = dot(slot_hot, picked[half_width * HALF :].astype(BF16), NT)
        grad_hidden = dot(table_ref[group], spread, TN)
        grad_hidden = jnp.where(low, grad_hidden[:LANES], grad_hidden[LANES:])
        grad_pre = (grad_hidden * logistic * (1.0 + pre * (1.0 - logistic))).astype(BF16)
        part_ref[pl.ds(pl.multiple_of(t * 16, 16), 16), :] = dot(first_ref[...], grad_pre).astype(BF16)
        first_grad_ref[...] += dot(held, grad_pre, NT)
        return product, sums

    def group_work(g, carry):
        product, sums = work(g, g)
        held_ref[g] = product
        sums_ref[pl.ds(pl.multiple_of(g * GROUP, GROUP), GROUP), :] = sums
        return carry

    def extra_work(u, carry):
        group = meta_ref[0, u]
        product, sums = work(groups + u, group)
        held_ref[group] += product
        sums_ref[pl.ds(pl.multiple_of(group * GROUP, GROUP), GROUP), :] += sums
        return carry

    lax.fori_loop(0, groups, group_work, 0)
    lax.fori_loop(0, extra_total, extra_work, 0)

    for c in range(chunks):
        cols = slice(c * LANES, (c + 1) * LANES)
        back = dot(part_ref[: groups * 16, :], hot_ref[:, cols])
        tile = tile_ref[c : c + 1, :]
        total = jnp.zeros((16, LANES), F32)
        for t in range(groups):
            total = total + jnp.where(tile == float(t), back[t * 16 : (t + 1) * 16], 0.0)
        feat_grad_ref[:, cols] = total

    def extra_back(u, carry):
        wanted = (groups + u).astype(F32)
        part = part_ref[pl.ds(pl.multiple_of((groups + u) * 16, 16), 16), :]
        for c in range(chunks):
            cols = slice(c * LANES, (c + 1) * LANES)
            back = dot(part, hot_ref[:, cols])
            feat_grad_ref[:, cols] += jnp.where(tile_ref[c : c + 1, :] == wanted, back, 0.0)
        return carry

    lax.fori_loop(0, extra_total, extra_back, 0)

    states = state_ref[...].astype(F32).reshape(groups, 2, HALF, LANES)
    states = jnp.concatenate(
        [states[:, a].reshape(slots // 2, LANES) for a in range(2)], axis=0
    ).astype(BF16)
    rows_ref[...] = jnp.zeros_like(rows_ref)

    def pair_grads(p, carry):
        quarter = []
        for q in range(2):
            rows = held_ref[:, pl.ds(pl.multiple_of(p * 16 + q * HALF, HALF), HALF), :].reshape(slots // 2, 2 * LANES)
            rows = rows.astype(BF16)
            quarter.append(jnp.concatenate([rows[:, :LANES], rows[:, LANES:]], axis=0))
        cols = pl.ds(pl.multiple_of(p * 2 * LANES, 2 * LANES), 2 * LANES)
        pair = second_ref[:, cols]
        second_grad_ref[:, cols] = jnp.concatenate(
            [dot(quarter[0], states, TN), dot(quarter[1], states, TN)], axis=1
        ).astype(BF16)
        rows_ref[...] += dot(
            jnp.concatenate(quarter, axis=1), jnp.concatenate([pair[:, :LANES], pair[:, LANES:]], axis=0)
        )
        return carry

    lax.fori_loop(0, half_width // 2, pair_grads, 0)
    sums = sums_ref[...].astype(BF16)
    second_bias_grad_ref[...] = dot(sums, state_ref[...], TN)
    ordered = jnp.stack(
        [rows_ref[a * (slots // 2) : (a + 1) * (slots // 2), :].reshape(groups, HALF, LANES) for a in range(2)], axis=1
    ).reshape(slots, LANES)
    source_grad_ref[...] = ordered + dot(sums, second_bias_ref[...])


def mesh_signal(sem, peers):
    for peer in peers:
        pl.semaphore_signal(sem, inc=1, device_id=peer, device_id_type=pl.DeviceIdType.MESH)
    pl.semaphore_wait(sem, len(peers))


def node_kernel(
    incoming_ref, full_ref, state_ref, mask_ref, input_ref, hidden_ref, input_bias_ref, hidden_bias_ref, cotangent_ref,
    message_grad_ref, new_ref, own_ref, partial_ref, weights_ref, biases_ref,
    other_ref, send_ref, back_ref, send_sem, recv_sem,
):
    edge, gate = lax.axis_index("edge"), lax.axis_index("gate")
    partner = (edge, 1 - gate)
    half = state_ref.shape[1]
    mesh_signal(pltpu.get_barrier_semaphore(), [partner])
    swap = pltpu.make_async_remote_copy(
        incoming_ref, other_ref, send_sem.at[0], recv_sem.at[0], device_id=partner, device_id_type=pl.DeviceIdType.MESH
    )
    swap.start()
    full = full_ref[...]
    hidden_pre = [dot(full, hidden_ref[k]) + hidden_bias_ref[k : k + 1, :].astype(F32) for k in range(3)]
    keep = jnp.concatenate(
        [
            jnp.broadcast_to(mask_ref[c : c + 1, :], (8, LANES)).astype(F32).T[:, :1]
            for c in range(mask_ref.shape[0])
        ],
        axis=0,
    )
    own = state_ref[...].astype(F32)
    grad_output = cotangent_ref[...].astype(F32) * keep
    mine = incoming_ref[...]
    swap.wait()
    other = other_ref[...]
    is_first = gate == 0
    message = jnp.concatenate(
        [jnp.where(is_first, mine, other), jnp.where(is_first, other, mine)], axis=1
    )
    input_pre = [dot(message, input_ref[k]) + input_bias_ref[k : k + 1, :].astype(F32) for k in range(3)]
    reset = jax.nn.sigmoid(input_pre[0] + hidden_pre[0])
    update = jax.nn.sigmoid(input_pre[1] + hidden_pre[1])
    candidate = jnp.tanh(input_pre[2] + reset * hidden_pre[2])
    grad_cand = grad_output * (1.0 - update) * (1.0 - candidate * candidate)
    grad_update = grad_output * (own - candidate) * update * (1.0 - update)
    grad_reset = grad_cand * hidden_pre[2] * reset * (1.0 - reset)
    grad_input = [grad_reset.astype(BF16), grad_update.astype(BF16), grad_cand.astype(BF16)]
    grad_hidden = [grad_input[0], grad_input[1], (grad_cand * reset).astype(BF16)]

    def onto(first_row):
        rows = pl.ds(pl.multiple_of(first_row, half), half)
        return sum(dot(grad_input[k], input_ref[k, rows, :], NT) for k in range(3))

    send_ref[...] = onto((1 - gate) * half)
    back = pltpu.make_async_remote_copy(
        send_ref, back_ref, send_sem.at[1], recv_sem.at[1], device_id=partner, device_id_type=pl.DeviceIdType.MESH
    )
    back.start()
    new_ref[...] = (keep * ((1.0 - update) * candidate + update * own)).astype(BF16)
    own_ref[...] = grad_output * update
    partial_ref[...] = sum(dot(grad_hidden[k], hidden_ref[k], NT) for k in range(3))
    grads = [dot(message, grad_input[k], TN) for k in range(3)] + [dot(full, grad_hidden[k], TN) for k in range(3)]
    for k in range(3):
        weights_ref[:, k * LANES : (k + 1) * LANES] = jnp.concatenate(
            [grads[2 * k], grads[2 * k + 1]], axis=1
        ).astype(BF16)
    sums = [jnp.sum(g.astype(F32), axis=0, keepdims=True) for g in grad_input + grad_hidden]
    biases_ref[...] = jnp.concatenate(sums + [jnp.zeros((2, half), F32)], axis=0)
    kept = onto(gate * half)
    back.wait()
    message_grad_ref[...] = (kept + back_ref[...]).astype(BF16)


def spread_units(units, parts):
    parts = min(units, parts)
    sizes = [units // parts + (1 if i < units % parts else 0) for i in range(parts)]
    return [(sum(sizes[:i]), sizes[i]) for i in range(parts)]


def finish_kernel(
    digits, groups,
    second_ref, second_bias_ref, first_ref, weights_ref, biases_ref, feat_ref, source_ref, partial_ref, own_ref,
    total_ref, small_total_ref, feat_out_ref, state_out_ref,
    work_ref, land_refs, small_ref, first_land_ref, feat_land_ref, rows_send_ref, rows_land_ref, rim_send_ref, rim_land_ref,
    send_sem, recv_sem, side_send, side_recv,
):
    edge, gate = lax.axis_index("edge"), lax.axis_index("gate")
    count = 1 << digits
    partner = (edge, 1 - gate)
    before = (lax.rem(edge + count - 1, count), gate)
    after = (lax.rem(edge + 1, count), gate)
    peers = [(edge ^ (1 << d), gate) for d in range(digits)]
    bits = [lax.rem(lax.shift_right_logical(edge, d), 2) for d in range(digits)]
    width = second_ref.shape[1]
    unit = LANES << (digits - 3)
    orders = [[0, 1, 2], [1, 2, 0], [2, 0, 1]]
    rest = list(range(3, digits))
    chunks = [
        (second_ref, start * unit, start * unit, size * unit, orders[i % 3] + rest, i // 3)
        for i, (start, size) in enumerate(spread_units(width // unit, 3 * groups))
    ]
    chunks.append((small_ref, 0, width, small_ref.shape[1], orders[0] + rest, groups - 1))

    mesh_signal(pltpu.get_barrier_semaphore(), peers + [partner, before, after])

    def side(index, source, target, device):
        return pltpu.make_async_remote_copy(
            source, target, side_send.at[index], side_recv.at[index], device_id=device, device_id_type=pl.DeviceIdType.MESH
        )

    first_copy = side(0, first_ref, first_land_ref, partner)
    first_copy.start()

    regions = []
    for _, _, place, lanes, order, _ in chunks:
        row, rows, lane = 0, 128, place
        levels = [(row, rows, lane, lanes)]
        for i, d in enumerate(order):
            if i < 3:
                rows //= 2
                row = row + bits[d] * rows
            else:
                lanes //= 2
                lane = lane + bits[d] * lanes
            levels.append((row, rows, lane, lanes))
        regions.append(levels)

    def window(row, rows, lane, lanes):
        if not isinstance(row, int):
            row = pl.multiple_of(row, 16)
        if not isinstance(lane, int):
            lane = pl.multiple_of(lane, LANES)
        return (pl.ds(row, rows), pl.ds(lane, lanes))

    def sibling(c, i):
        row, rows, lane, lanes = regions[c][i]
        d = chunks[c][4][i]
        if i < 3:
            return (row + (1 - bits[d]) * (rows // 2), rows // 2, lane, lanes)
        return (row, rows, lane + (1 - bits[d]) * (lanes // 2), lanes // 2)

    def landing(c, i):
        _, rows, _, lanes = regions[c][i + 1]
        return land_refs[i].at[pl.ds(0, rows), pl.ds(chunks[c][2] >> max(0, i - 2), lanes)]

    def inside(c, window_):
        source, at, place = chunks[c][:3]
        row, rows, lane, lanes = window_
        return source, window(row, rows, lane - place + at, lanes)

    def total_at(c, window_):
        row, rows, lane, lanes = window_
        if chunks[c][0] is small_ref:
            return small_total_ref, window(row, rows, lane - width, lanes)
        return total_ref, window(row, rows, lane, lanes)

    def scatter(c, i):
        if i == 0:
            source, at = inside(c, sibling(c, i))
            source = source.at[at]
        else:
            source = work_ref.at[window(*sibling(c, i))]
        return pltpu.make_async_remote_copy(
            source, landing(c, i), send_sem.at[c, i], recv_sem.at[c, i],
            device_id=peers[chunks[c][4][i]], device_id_type=pl.DeviceIdType.MESH,
        )

    def gather(c, i):
        ref, at = total_at(c, regions[c][i + 1])
        return pltpu.make_async_remote_copy(
            ref.at[at], ref.at[at], send_sem.at[c, 2 * digits - 1 - i], recv_sem.at[c, 2 * digits - 1 - i],
            device_id=peers[chunks[c][4][i]], device_id_type=pl.DeviceIdType.MESH,
        )

    def start(c, phase):
        if phase < digits:
            scatter(c, phase).start()
        elif phase < 2 * digits:
            gather(c, 2 * digits - 1 - phase).start()

    def arrive(c, phase):
        if phase < digits:
            scatter(c, phase).wait_recv()
            kept = regions[c][phase + 1]
            if phase == 0:
                source, at = inside(c, kept)
            else:
                source, at = work_ref, window(*kept)
            landed = landing(c, phase)
            value = source[at].astype(F32) + landed[...].astype(F32)
            if phase == digits - 1:
                target, at = total_at(c, kept)
            else:
                target, at = work_ref, window(*kept)
            target[at] = value.astype(BF16)
        else:
            gather(c, 2 * digits - 1 - phase).wait_recv()

    members = [[c for c in range(len(chunks)) if chunks[c][5] == g] for g in range(groups)]
    for g in range(groups):
        for c in members[g]:
            if chunks[c][0] is not small_ref:
                start(c, 0)

    feat_copy = side(1, feat_ref, feat_land_ref, partner)
    feat_copy.start()
    border = source_ref.shape[0] - partial_ref.shape[0]
    rows = source_ref[...] + jnp.concatenate([jnp.zeros((border, LANES), F32), partial_ref[...]], axis=0)
    rows_send_ref[...] = rows.astype(BF16)
    rows_copy = side(2, rows_send_ref, rows_land_ref, partner)
    rows_copy.start()
    first_copy.wait()
    small_ref[...] = jnp.zeros_like(small_ref)
    half = second_bias_ref.shape[0]
    small_ref[:half, :LANES] = second_bias_ref[...].astype(BF16)
    small_ref[half : half + ROWS, :LANES] = (first_ref[...] + first_land_ref[...]).astype(BF16)
    small_ref[half + ROWS : half + ROWS + 16, : biases_ref.shape[1]] = jnp.concatenate(
        [biases_ref[...], jnp.zeros_like(biases_ref)], axis=0
    ).astype(BF16)
    small_ref[:, LANES : 4 * LANES] = weights_ref[...]
    start(len(chunks) - 1, 0)
    rows_copy.wait()
    rows = rows + rows_land_ref[...].astype(F32)
    rim_send_ref[...] = rows[:border].astype(BF16)
    rim_copy = side(3, rim_send_ref, rim_land_ref, before)
    rim_copy.start()
    feat_copy.wait()
    feat_out_ref[...] = feat_ref[...] + feat_land_ref[...]

    for step in range(groups + 2 * digits - 1):
        for g in range(groups):
            phase = step - g
            if 0 <= phase < 2 * digits:
                for c in members[g]:
                    arrive(c, phase)
                    start(c, phase + 1)

    rim_copy.wait()
    rows = rows[border:]
    rows = jnp.concatenate([rows[:-border], rows[-border:] + rim_land_ref[...].astype(F32)], axis=0)
    side_half = own_ref.shape[1]
    state_out_ref[...] = jnp.where(gate == 0, rows[:, :side_half], rows[:, side_half:]) + own_ref[...]
    for c in range(len(chunks)):
        for phase in range(2 * digits):
            if phase < digits:
                scatter(c, phase).wait_send()
            else:
                gather(c, 2 * digits - 1 - phase).wait_send()


def emit_kernel(
    total_ref, small_ref, new_in_ref, state_in_ref, feat_in_ref,
    new_ref, state_ref, feat_ref, first_ref, first_bias_ref, second_ref, second_bias_ref, input_ref, hidden_ref,
    input_bias_ref, hidden_bias_ref,
):
    second_ref[...] = total_ref[...].astype(F32)

    @pl.when(pl.program_id(0) == 0)
    def _():
        new_ref[...] = new_in_ref[...]
        state_ref[...] = state_in_ref[...]
        feat_ref[...] = feat_in_ref[...]
        small = small_ref[:, : 4 * LANES].astype(F32)
        half = second_bias_ref.shape[0]
        second_bias_ref[...] = small[:half, :LANES]
        first_ref[...] = small[half : half + 16, :LANES]
        first_bias_ref[...] = small[half + 18 : half + 19, :LANES]
        part = input_ref.shape[2]
        at = half + ROWS
        input_bias_ref[...] = small[at : at + 3, :part]
        hidden_bias_ref[...] = small[at + 3 : at + 6, :part]
        for k in range(3):
            input_ref[k] = small[:, LANES + k * part : LANES + (k + 1) * part]
            hidden_ref[k] = small[:, LANES + (3 + k) * part : LANES + (4 + k) * part]


def passed_along(block, axis, distance):
    devices = range(lax.axis_size(axis))
    route = [(i - distance, i) for i in devices if i - distance in devices]
    return lax.ppermute(block, axis, route)


def per_device(
    node_state, edge_feat, source, target, edge_mask, node_mask, net_first, net_first_bias, net_second,
    net_second_bias, gru_input, gru_hidden, gru_input_bias, gru_hidden_bias, cotangent,
):
    node_count, half_width = node_state.shape
    edge_count = source.shape[0]
    width = 2 * half_width
    chunks = edge_count // LANES
    slots = BORDER + node_count
    groups = slots // GROUP
    tiles = groups + edge_count // TILE - 1
    full_state = lax.all_gather(node_state, "gate", axis=1, tiled=True)
    earlier = passed_along(full_state[node_count - BORDER :], "edge", 1)
    extended = jnp.concatenate([earlier, full_state], axis=0)
    params = pltpu.CompilerParams(vmem_limit_bytes=VMEM_LIMIT)
    first_bias = net_first_bias.reshape(1, width)
    second_bias = net_second_bias.reshape(half_width, width)
    shape = jax.ShapeDtypeStruct
    vmem = pl.BlockSpec(memory_space=pltpu.VMEM)
    incoming, moved, table, tile_rows, lane_rows, meta = pl.pallas_call(
        forward_kernel,
        out_shape=(
            shape((node_count, half_width), BF16),
            shape((tiles, ROWS, TILE), BF16),
            shape((groups, half_width * HALF, 2 * width), BF16),
            shape((chunks, LANES), F32),
            shape((chunks, LANES), F32),
            shape((8, LANES), jnp.int32),
        ),
        scratch_shapes=[
            pltpu.VMEM((chunks * ROWS, LANES), BF16),
            pltpu.VMEM(((groups + 1) * ROWS, edge_count), BF16),
            pltpu.VMEM((TILE, edge_count), BF16),
            pltpu.VMEM((slots, half_width), F32),
            pltpu.VMEM((node_count, half_width), F32),
            pltpu.SMEM((8, LANES), jnp.int32),
            pltpu.SemaphoreType.DMA,
        ],
        compiler_params=params,
        name="forward_edges",
    )(
        source.reshape(chunks, LANES), target.reshape(chunks, LANES), edge_mask.reshape(chunks, LANES),
        edge_feat, extended, net_first, first_bias, net_second, second_bias,
    )

    message_grad, new_state, grad_own, state_partial, weight_grads, bias_grads = pl.pallas_call(
        node_kernel,
        out_shape=(
            shape((node_count, half_width), BF16),
            shape((node_count, half_width), BF16),
            shape((node_count, half_width), F32),
            shape((node_count, width), F32),
            shape((width, 6 * half_width), BF16),
            shape((8, half_width), F32),
        ),
        in_specs=[vmem] * 9,
        out_specs=(vmem,) * 6,
        scratch_shapes=[
            pltpu.VMEM((node_count, half_width), BF16),
            pltpu.VMEM((node_count, half_width), F32),
            pltpu.VMEM((node_count, half_width), F32),
            pltpu.SemaphoreType.DMA((2,)),
            pltpu.SemaphoreType.DMA((2,)),
        ],
        compiler_params=pltpu.CompilerParams(vmem_limit_bytes=VMEM_LIMIT, collective_id=1, has_side_effects=True),
        name="node_update",
    )(
        incoming, full_state, node_state, node_mask.reshape(node_count // LANES, LANES), gru_input, gru_hidden,
        gru_input_bias, gru_hidden_bias, cotangent,
    )

    second_grad, second_bias_grad, source_grads, feat_part, first_part = pl.pallas_call(
        backward_kernel,
        out_shape=(
            shape((width, half_width * width), BF16),
            shape((half_width, width), F32),
            shape((slots, width), F32),
            shape((16, edge_count), F32),
            shape((ROWS, width), F32),
        ),
        in_specs=[pl.BlockSpec(memory_space=pltpu.SMEM)] + [vmem] * 10,
        out_specs=(vmem,) * 5,
        scratch_shapes=[
            pltpu.VMEM((groups, half_width * HALF, 2 * width), F32),
            pltpu.VMEM((slots, half_width), F32),
            pltpu.VMEM((tiles * 16, TILE), BF16),
            pltpu.VMEM((TILE, edge_count), BF16),
            pltpu.VMEM((slots, width), F32),
        ],
        compiler_params=params,
        name="backward_edges",
    )(
        meta, message_grad, extended, net_first, first_bias, net_second, second_bias, moved, table, tile_rows, lane_rows,
    )

    digits = (lax.axis_size("edge") - 1).bit_length()
    unit = LANES << (digits - 3)
    columns = half_width * width
    small_width = max(4 * LANES, unit)
    parts = 4
    steps = min(columns // unit, 3 * parts) + 1
    whole = columns + small_width
    total, small_total, grad_feat, grad_state = pl.pallas_call(
        functools.partial(finish_kernel, digits, parts),
        out_shape=(
            shape((width, columns), BF16),
            shape((width, small_width), BF16),
            shape((16, edge_count), F32),
            shape((node_count, half_width), F32),
        ),
        in_specs=[vmem] * 9,
        out_specs=(vmem,) * 4,
        scratch_shapes=[
            pltpu.VMEM((width, whole), BF16),
            [pltpu.VMEM((max(16, width >> (i + 1)), whole >> max(0, i - 2)), BF16) for i in range(digits)],
            pltpu.VMEM((width, small_width), BF16),
            pltpu.VMEM((ROWS, width), F32),
            pltpu.VMEM((16, edge_count), F32),
            pltpu.VMEM((slots, width), BF16),
            pltpu.VMEM((slots, width), BF16),
            pltpu.VMEM((BORDER, width), BF16),
            pltpu.VMEM((BORDER, width), BF16),
            pltpu.SemaphoreType.DMA((steps, 2 * digits)),
            pltpu.SemaphoreType.DMA((steps, 2 * digits)),
            pltpu.SemaphoreType.DMA((4,)),
            pltpu.SemaphoreType.DMA((4,)),
        ],
        compiler_params=pltpu.CompilerParams(vmem_limit_bytes=VMEM_LIMIT, collective_id=2, has_side_effects=True),
        name="finish_sums",
    )(
        second_grad, second_bias_grad, first_part, weight_grads, bias_grads, feat_part, source_grads, state_partial,
        grad_own,
    )

    blocks = 8
    fixed = lambda *dims: pl.BlockSpec(dims, lambda i: (0,) * len(dims))
    outs = pl.pallas_call(
        emit_kernel,
        grid=(blocks,),
        out_shape=(
            shape((node_count, half_width), BF16),
            shape((node_count, half_width), F32),
            shape((16, edge_count), F32),
            shape((16, width), F32),
            shape((1, width), F32),
            shape((width, columns), F32),
            shape((half_width, width), F32),
            shape((3, width, half_width), F32),
            shape((3, width, half_width), F32),
            shape((3, half_width), F32),
            shape((3, half_width), F32),
        ),
        in_specs=[
            pl.BlockSpec((width, columns // blocks), lambda i: (0, i)),
            fixed(width, small_width), fixed(node_count, half_width), fixed(node_count, half_width), fixed(16, edge_count),
        ],
        out_specs=(
            fixed(node_count, half_width), fixed(node_count, half_width), fixed(16, edge_count), fixed(16, width),
            fixed(1, width), pl.BlockSpec((width, columns // blocks), lambda i: (0, i)), fixed(half_width, width),
            fixed(3, width, half_width), fixed(3, width, half_width), fixed(3, half_width), fixed(3, half_width),
        ),
        compiler_params=params,
        name="emit",
    )(total, small_total, new_state, grad_state, grad_feat)
    outs = list(outs)
    outs[4] = outs[4].reshape(width)
    outs[6] = outs[6].reshape(columns)
    return tuple(outs)


def solution(mesh):
    return jax.shard_map(
        per_device,
        mesh=mesh,
        in_specs=(
            P("edge", "gate"), P(None, "edge"), P("edge"), P("edge"), P("edge"), P("edge"), P(), P(), P(None, "gate"),
            P("gate"), P(None, None, "gate"), P(None, None, "gate"), P(None, "gate"), P(None, "gate"), P("edge", "gate"),
        ),
        out_specs=(
            P("edge", "gate"), P("edge", "gate"), P(None, "edge"), P(), P(), P(None, "gate"), P("gate"),
            P(None, None, "gate"), P(None, None, "gate"), P(None, "gate"), P(None, "gate"),
        ),
        check_vma=False,
    )
```

```python
import functools

import jax
import jax.numpy as jnp
from jax import lax
from jax.experimental import pallas as pl
from jax.experimental.pallas import tpu as pltpu
from jax.sharding import PartitionSpec as P

BORDER = 64
GROUP = 14
HALF = 8
TILE = 256
MAIN = 26
LANES = 128
ROWS = 32
MIB = 1024 * 1024

KINDS = ("span", "chunk", "go", "tiles", "first", "back", "sources", "rim", "state", "feat")
SCHEDULE = (
    16, 18, 17, 1, 21, 20, 32, 34, 19, 33, 52, 50, 32, 37, 22, 36, 56, 33, 48, 32, 35, 34, 38, 54, 33, 55, 37, 32,
    34, 36, 35, 53, 38, 33, 37, 96, 34, 36, 32, 51, 35, 33, 37, 49, 64, 38, 34, 36, 32, 65, 35, 33, 37, 34, 66, 36,
    82, 38, 35, 32, 67, 37, 36, 33, 38, 34, 68, 35, 80, 81, 112, 36, 37, 83, 38, 35, 34, 32, 144, 38, 36, 69, 33,
    128, 37, 38, 35,
)

NN = ((1,), (0,))
NT = ((1,), (1,))
TN = ((0,), (0,))
F32 = jnp.float32
BF16 = jnp.bfloat16


def dot(left, right, dims=NN):
    return lax.dot_general(left, right, (dims, ((), ())), preferred_element_type=F32)


def iota(shape, dim):
    return lax.broadcasted_iota(jnp.int32, shape, dim)


def extended_first(first_ref, bias_ref):
    extra = jnp.where(iota((ROWS - 16, LANES), 0) == 2, bias_ref[...].astype(F32), 0.0)
    return jnp.concatenate([first_ref[...].astype(F32), extra], axis=0).astype(BF16)


def tile_masks(slot_row):
    place = slot_row.astype(jnp.int32) - 1
    low = jnp.logical_and(place >= 0, place < HALF)
    high = place >= HALF
    within = jnp.where(high, place - HALF, place)
    return low, high, within


def halves(hidden, low, high):
    return jnp.concatenate(
        [jnp.where(low, hidden, 0.0), jnp.where(high, hidden, 0.0)], axis=0
    ).astype(BF16)


def keep_within(values, within):
    rows, width = values.shape
    match = iota((HALF, width), 0) == within
    kept = jnp.where(match[None], values.reshape(rows // HALF, HALF, width), 0.0)
    return kept.reshape(rows, width).astype(BF16)


def target_hot(target_row, node_count):
    width = target_row.shape[1]
    return (iota((node_count, width), 0) + 1 == target_row.astype(jnp.int32)).astype(F32).astype(BF16)


def lane_hot(lane_ref, out_ref):
    chunks = lane_ref.shape[0]
    for c in range(chunks):
        row = lane_ref[c : c + 1, :].astype(jnp.int32)
        out_ref[:, c * LANES : (c + 1) * LANES] = (
            (iota((TILE, LANES), 0) == row).astype(F32).astype(BF16)
        )


def tile_loop(count, body, step):
    def several(i, carry):
        for s in range(step):
            body(i * step + s)
        return carry

    whole = count // step
    lax.fori_loop(0, whole, several, 0)
    for t in range(whole * step, count):
        body(t)


def fetched(kernel, operands):
    count = len(operands)

    def body(*refs):
        sources, others, targets, sem = refs[:count], refs[count : -count - 1], refs[-count - 1 : -1], refs[-1]
        copies = [pltpu.make_async_copy(sources[i], targets[i], sem.at[i]) for i in range(count)]
        for copy in copies:
            copy.start()

        def ready():
            for copy in copies:
                copy.wait()

        kernel(ready, *targets, *others)

    scratch = [pltpu.VMEM(x.shape, x.dtype) for x in operands] + [pltpu.SemaphoreType.DMA((count,))]
    return body, [pl.BlockSpec(memory_space=pl.ANY)] * count, scratch


def in_hbm(*arrays):
    return tuple(pltpu.with_memory_space_constraint(x, pltpu.HBM) for x in arrays)


def place_kernel(
    ready, source_ref, target_ref, mask_ref, feat_ref, state_ref,
    full_ref, states_ref, tiles_ref, values_ref, tile_ref, lane_ref, meta_ref, slot_ref,
    counts_ref, spread_ref, hot_ref, other_ref, rim_ref, send_sem, recv_sem,
):
    chunks = source_ref.shape[0]
    half, node_count = state_ref.shape
    main = tiles_ref.shape[0]
    padded = states_ref.shape[1]
    groups = -(-(node_count + BORDER) // GROUP)
    edge, gate = lax.axis_index("edge"), lax.axis_index("gate")
    count = lax.axis_size("edge")
    first_node = edge * node_count
    partner = (edge, 1 - gate)
    after = lax.rem(edge + 1, count)
    before = lax.rem(edge + count - 1, count)
    mesh_signal(
        pltpu.get_barrier_semaphore(), [partner, (after, gate), (after, 1 - gate), (before, gate), (before, 1 - gate)]
    )

    def send(index, source, target, device):
        return pltpu.make_async_remote_copy(
            source, target, send_sem.at[index], recv_sem.at[index], device_id=device, device_id_type=pl.DeviceIdType.MESH
        )

    ready()
    rim = state_ref.at[:, pl.ds(node_count - LANES, LANES)]
    copies = [
        send(0, rim, rim_ref.at[0], (after, gate)),
        send(1, rim, rim_ref.at[1], (after, 1 - gate)),
        send(2, state_ref, other_ref, partner),
    ]
    for copy in copies:
        copy.start()

    group_rows = []
    slot_rows = []
    for c in range(chunks):
        slot = (source_ref[c : c + 1, :] - first_node + BORDER).astype(F32)
        group = jnp.floor((slot + 0.5) * (1.0 / GROUP))
        slot_rows.append(slot)
        group_rows.append(group)
        counts_ref[c * ROWS : (c + 1) * ROWS, :] = (
            (iota((ROWS, LANES), 0).astype(F32) == group).astype(F32).astype(BF16)
        )
    above = jnp.where(
        iota((LANES, 2 * LANES), 0) < iota((LANES, 2 * LANES), 1), 1.0, 0.0
    ).astype(BF16)
    sums = dot(counts_ref[...], above)
    running = jnp.zeros((ROWS, LANES), F32)
    ranks = []
    for c in range(chunks):
        hot = counts_ref[c * ROWS : (c + 1) * ROWS, :].astype(F32)
        part = sums[c * ROWS : (c + 1) * ROWS]
        ranks.append(jnp.sum(hot * (part[:, :LANES] + running), axis=0, keepdims=True))
        running = running + part[:, LANES:]
    owned = jnp.floor((running + (TILE - 1.0)) * (1.0 / TILE))
    earlier = (iota((ROWS, ROWS), 1) < iota((ROWS, ROWS), 0)).astype(F32).astype(BF16)
    start = dot(earlier, owned.astype(BF16))
    end = start + owned
    total = jnp.sum(owned, axis=0, keepdims=True)

    def group_of(tile):
        return jnp.minimum(jnp.sum((end <= tile).astype(F32), axis=0, keepdims=True), groups - 1.0)

    row8 = iota((8, LANES), 0)
    lane = iota((1, LANES), 1).astype(F32)
    meta_ref[...] = jnp.where(row8 == 0, group_of(lane), jnp.where(row8 == 1, total, 0.0)).astype(jnp.int32)
    for c in range(slot_ref.shape[1] // LANES):
        row = lane + float(c * LANES)
        high = jnp.where(row >= main * HALF, 1.0, 0.0)
        row = row - high * (main * HALF)
        tile = jnp.floor((row + 0.5) * (1.0 / HALF))
        place = row - tile * HALF + high * HALF
        slot = group_of(tile) * GROUP + place
        slot = jnp.where(jnp.logical_and(place < GROUP, tile < jnp.minimum(total, float(main))), slot, -1.0)
        slot_ref[:, c * LANES : (c + 1) * LANES] = jnp.broadcast_to(slot, (8, LANES))

    row16 = iota((ROWS - 16, LANES), 0)
    for c in range(chunks):
        cols = slice(c * LANES, (c + 1) * LANES)
        hot = counts_ref[c * ROWS : (c + 1) * ROWS, :].astype(F32)
        over = jnp.floor(ranks[c] * (1.0 / TILE))
        tile = jnp.sum(hot * start, axis=0, keepdims=True) + over
        lane = ranks[c] - TILE * over
        tile_ref[c : c + 1, :] = tile
        lane_ref[c : c + 1, :] = lane
        hot_ref[:, cols] = (iota((TILE, LANES), 0).astype(F32) == lane).astype(F32).astype(BF16)
        place = slot_rows[c] - GROUP * group_rows[c] + 1.0
        target = jnp.where(
            mask_ref[c : c + 1, :] > 0, target_ref[c : c + 1, :] - first_node + 1, 0
        ).astype(F32)
        more = jnp.where(row16 == 0, target, jnp.where(row16 == 1, place, jnp.where(row16 == 2, 1.0, 0.0)))
        values = jnp.concatenate([feat_ref[:, cols].astype(F32), more], axis=0)
        values_ref[:, cols] = values.astype(BF16)
        for t in range(main):
            spread_ref[t * ROWS : (t + 1) * ROWS, cols] = jnp.where(tile == float(t), values, 0.0).astype(BF16)
    moved = dot(spread_ref[...], hot_ref[...], NT)
    tiles_ref[...] = moved.reshape(main, ROWS, TILE).astype(BF16)

    for copy in copies:
        copy.wait()
    is_first = gate == 0
    mine, other = state_ref[...], other_ref[...]
    full = jnp.concatenate([jnp.where(is_first, mine, other), jnp.where(is_first, other, mine)], axis=0)
    full_ref[...] = full
    own, swapped = rim_ref[0], rim_ref[1]
    rims = jnp.concatenate([jnp.where(is_first, own, swapped), jnp.where(is_first, swapped, own)], axis=0)
    rows = jnp.concatenate(
        [rims.astype(F32).T[LANES - BORDER :], full.astype(F32).T], axis=0
    )
    spare = padded * GROUP + 16 - rows.shape[0]
    rows = jnp.concatenate([rows, jnp.zeros((spare, 2 * half), F32)], axis=0)
    for g in range(padded):
        for a in range(2):
            states_ref[a, g] = rows[g * GROUP + a * HALF : g * GROUP + (a + 1) * HALF]


def group_states(states_ref):
    _, padded, half, width = states_ref.shape
    return jnp.concatenate([states_ref[a].reshape(padded * half, width) for a in range(2)], axis=0).astype(BF16)


def group_counts(counts_ref):
    padded, _, node_count = counts_ref.shape
    return jnp.concatenate(
        [counts_ref[:, a * HALF : (a + 1) * HALF, :].reshape(padded * HALF, node_count) for a in range(2)], axis=0
    ).astype(BF16)


def forward_kernel(
    ready, first_ref, first_bias_ref, second_bias_ref, meta_ref, tiles_ref, values_hbm, tile_hbm, lane_hbm, states_ref,
    second_ref,
    incoming_ref, over_hbm, counts_out_ref, table_out_ref, *rest,
):
    blank_refs, rest = rest[:4], rest[4:]
    counts_ref, table_ref, hidden_ref, targets_ref, hot_ref, total_ref, second_vmem, narrow_ref, zeros_ref = rest[:9]
    values_ref, tile_ref, lane_ref, held_ref, sems, blank_sems = rest[9:]
    chunks = tile_ref.shape[0]
    half_width, node_count = incoming_ref.shape
    main = tiles_ref.shape[0]
    padded = table_ref.shape[0]
    over_total = jnp.maximum(meta_ref[1, 0] - main, 0)
    fetch = pltpu.make_async_copy(second_ref, second_vmem, sems.at[0])
    fetch.start()
    narrow_ref[...] = jnp.zeros_like(narrow_ref)
    zeros_ref[...] = jnp.zeros_like(zeros_ref)
    blanks = []
    for i, blank_ref in enumerate(blank_refs):
        rows, cols = blank_ref.shape
        zeros = narrow_ref if blank_ref.dtype == BF16 else zeros_ref
        blanks.append(pltpu.make_async_copy(zeros.at[pl.ds(0, rows), pl.ds(0, cols)], blank_ref, blank_sems.at[i]))
        blanks[i].start()
    ready()
    first_t = extended_first(first_ref, first_bias_ref)

    def expand(t, held):
        low, high, _ = tile_masks(held[17:18, :].astype(F32))
        pre = dot(first_t, held, TN)
        hidden_ref[t] = halves(pre * jax.nn.sigmoid(pre), low, high)
        targets_ref[t] = target_hot(held[16:17, :].astype(F32), node_count)

    tile_loop(main, lambda t: expand(t, tiles_ref[t]), 13)

    states = group_states(states_ref)
    fetch.wait()

    def table_pair(p):
        pair = second_vmem[:, pl.ds(pl.multiple_of(p * 2 * LANES, 2 * LANES), 2 * LANES)]
        both = jnp.concatenate([pair[:, :LANES], pair[:, LANES:]], axis=0)
        product = dot(states, both, NT).reshape(2, padded, HALF, 2 * LANES)
        for a in range(2):
            rows = jnp.concatenate([product[a, :, :, :LANES], product[a, :, :, LANES:]], axis=1)
            table_ref[:, pl.ds(pl.multiple_of(p * 16, 16), 16), a * LANES : (a + 1) * LANES] = rows.astype(BF16)

    tile_loop(half_width // 2, table_pair, 8)
    keep = pltpu.make_async_copy(table_ref, table_out_ref, sems.at[1])
    keep.start()

    def messages(t, group, held):
        _, _, within = tile_masks(held[17:18, :].astype(F32))
        message = keep_within(dot(table_ref[group], hidden_ref[t]), within)
        place = held[17:18, :].astype(jnp.int32) - 1
        places = (iota((16, TILE), 0) == place).astype(F32).astype(BF16)
        sums = dot(jnp.concatenate([message, places], axis=0), targets_ref[t], NT)
        total_ref[...] += sums[: half_width * HALF]
        counts_ref[group] += sums[half_width * HALF :]

    total_ref[...] = jnp.zeros_like(total_ref)
    counts_ref[...] = jnp.zeros_like(counts_ref)
    tile_loop(main, lambda t: messages(t, meta_ref[0, t], tiles_ref[t]), 13)

    @pl.when(over_total > 0)
    def _():
        for source, target in [(values_hbm, values_ref), (tile_hbm, tile_ref), (lane_hbm, lane_ref)]:
            load = pltpu.make_async_copy(source, target, sems.at[2])
            load.start()
            load.wait()
        lane_hot(lane_ref, hot_ref)

    def over_messages(u, carry):
        wanted = (main + u).astype(F32)
        pieces = []
        for c in range(chunks):
            values = values_ref[:, c * LANES : (c + 1) * LANES].astype(F32)
            pieces.append(jnp.where(tile_ref[c : c + 1, :] == wanted, values, 0.0).astype(BF16))
        held = dot(jnp.concatenate(pieces, axis=1), hot_ref[...], NT).astype(BF16)
        held_ref[...] = held
        save = pltpu.make_async_copy(held_ref, over_hbm.at[u], sems.at[2])
        save.start()
        save.wait()
        expand(0, held)
        messages(0, meta_ref[0, main + u], held)
        return carry

    lax.fori_loop(0, over_total, over_messages, 0)
    bias = dot(second_bias_ref[...], states, NT)
    summed = jnp.sum(total_ref[...].reshape(half_width, HALF, node_count), axis=1)
    counts = group_counts(counts_ref)
    counts_out_ref[...] = counts
    incoming_ref[...] = (summed + dot(bias.astype(BF16), counts)).astype(BF16)
    keep.wait()
    for blank in blanks:
        blank.wait()


def expand_tile(held, first_t, wide, node_count):
    low, high, within = tile_masks(held[17:18, :].astype(F32))
    pre = dot(first_t, held, TN)
    logistic = jax.nn.sigmoid(pre)
    hidden = halves(pre * logistic, low, high)
    slope = logistic * (1.0 + pre * (1.0 - logistic))
    spread = keep_within(dot(wide, target_hot(held[16:17, :].astype(F32), node_count)), within)
    return hidden, slope, spread


def widened(grad_ref):
    half_width, node_count = grad_ref.shape
    wide = jnp.broadcast_to(grad_ref[...].astype(F32)[:, None, :], (half_width, HALF, node_count))
    return wide.reshape(half_width * HALF, node_count).astype(BF16)


def hidden_slopes(held, table, spread, slope, first):
    low, _, _ = tile_masks(held[17:18, :].astype(F32))
    grad_hidden = dot(table, spread, TN)
    grad_hidden = jnp.where(low, grad_hidden[:LANES], grad_hidden[LANES:])
    grad_pre = (grad_hidden * slope).astype(BF16)
    return dot(first, grad_pre).astype(BF16), dot(held, grad_pre, NT)


def split_pair(held):
    tiles = held.shape[0]
    held = held.astype(F32)
    parts = []
    for q in range(2):
        rows = held[:, q * HALF : (q + 1) * HALF, :].reshape(tiles * HALF, 2 * LANES).astype(BF16)
        parts.append(jnp.concatenate([rows[:, :LANES], rows[:, LANES:]], axis=0))
    return jnp.concatenate(parts, axis=1)


def overflow_kernel(
    meta_ref, grad_hbm, first_hbm, first_bias_hbm, over_hbm, table_hbm, states_hbm, second_hbm, _grads, _rows, _part, _first,
    grads_hbm, rows_hbm, part_hbm, first_grad_hbm,
    grad_ref, first_ref, first_bias_ref, over_ref, states_ref, rows_ref, part_ref, first_grad_ref,
    grads_ref, weight_ref, outer_ref, table_ref, sem,
):
    total = jnp.maximum(meta_ref[1, 0] - MAIN, 0)

    def move(source, target):
        copy = pltpu.make_async_copy(source, target, sem)
        copy.start()
        copy.wait()

    @pl.when(total > 0)
    def _():
        half_width, node_count = grad_ref.shape
        move(grad_hbm, grad_ref)
        move(first_hbm, first_ref)
        move(first_bias_hbm, first_bias_ref)
        move(states_hbm, states_ref)
        move(second_hbm, weight_ref)
        first_grad_ref[...] = jnp.zeros_like(first_grad_ref)
        part_ref[...] = jnp.zeros_like(part_ref)
        rows_ref[...] = jnp.zeros_like(rows_ref)
        grads_ref[...] = jnp.zeros_like(grads_ref)
        first_t = extended_first(first_ref, first_bias_ref)
        wide = widened(grad_ref)

        def tile_work(u, carry):
            group = meta_ref[0, MAIN + u]
            move(table_hbm.at[group], table_ref)
            move(over_hbm.at[u], over_ref)
            held = over_ref[...]
            hidden, slope, spread = expand_tile(held, first_t, wide, node_count)
            outer_ref[0] = dot(spread, hidden, NT).astype(BF16)
            part, first_grad = hidden_slopes(held, table_ref[...], spread, slope, first_ref[...])
            part_ref[pl.ds(pl.multiple_of(u * 16, 16), 16), :] = part
            first_grad_ref[...] += first_grad
            states = jnp.concatenate([states_ref[0, group], states_ref[1, group]], axis=0).astype(BF16)

            def pair_work(p, carry):
                cols = pl.ds(pl.multiple_of(p * 2 * LANES, 2 * LANES), 2 * LANES)
                quarters = split_pair(outer_ref[:, pl.ds(pl.multiple_of(p * 16, 16), 16), :])
                product = dot(quarters, states, TN)
                grads_ref[:, cols] += jnp.concatenate([product[:LANES], product[LANES:]], axis=1)
                pair = weight_ref[:, cols]
                return carry + dot(quarters, jnp.concatenate([pair[:, :LANES], pair[:, LANES:]], axis=0))

            rows = lax.fori_loop(0, half_width // 2, pair_work, jnp.zeros((2 * HALF, LANES), F32))
            at = group * GROUP
            rows_ref[pl.ds(at, HALF), :] += rows[:HALF]
            rows_ref[pl.ds(at + HALF, HALF), :] += rows[HALF:]
            return carry

        lax.fori_loop(0, total, tile_work, 0)
        weight_ref[...] = grads_ref[...].astype(BF16)
        move(weight_ref, grads_hbm)
        move(rows_ref, rows_hbm)
        move(part_ref, part_hbm)
        move(first_grad_ref, first_grad_hbm)


def mesh_signal(sem, peers):
    for peer in peers:
        pl.semaphore_signal(sem, inc=1, device_id=peer, device_id_type=pl.DeviceIdType.MESH)
    pl.semaphore_wait(sem, len(peers))


def node_kernel(
    ready, state_ref, mask_ref, input_ref, hidden_ref, input_bias_ref, hidden_bias_ref, cotangent_ref, incoming_ref, full_ref,
    message_grad_ref, new_ref, own_ref, partial_ref, weights_ref, biases_ref,
    other_ref, onto_ref, back_ref, send_sem, recv_sem,
):
    edge, gate = lax.axis_index("edge"), lax.axis_index("gate")
    partner = (edge, 1 - gate)
    half = state_ref.shape[0]
    mesh_signal(pltpu.get_barrier_semaphore(), [partner])
    swap = pltpu.make_async_remote_copy(
        incoming_ref, other_ref, send_sem.at[0], recv_sem.at[0], device_id=partner, device_id_type=pl.DeviceIdType.MESH
    )
    swap.start()
    ready()
    full = full_ref[...]
    biases = jnp.concatenate(
        [input_bias_ref[...].astype(F32), hidden_bias_ref[...].astype(F32), jnp.zeros((2, half), F32)], axis=0
    ).T
    hidden_pre = [dot(hidden_ref[k], full) + biases[:, 3 + k : 4 + k] for k in range(3)]
    keep = jnp.concatenate([mask_ref[c : c + 1, :] for c in range(mask_ref.shape[0])], axis=1).astype(F32)
    own = state_ref[...].astype(F32)
    grad_output = cotangent_ref[...].astype(F32) * keep
    mine = incoming_ref[...]
    swap.wait()
    other = other_ref[...]
    is_first = gate == 0
    message = jnp.concatenate(
        [jnp.where(is_first, mine, other), jnp.where(is_first, other, mine)], axis=0
    )
    input_pre = [dot(input_ref[k], message) + biases[:, k : k + 1] for k in range(3)]
    reset = jax.nn.sigmoid(input_pre[0] + hidden_pre[0])
    update = jax.nn.sigmoid(input_pre[1] + hidden_pre[1])
    candidate = jnp.tanh(input_pre[2] + reset * hidden_pre[2])
    grad_cand = grad_output * (1.0 - update) * (1.0 - candidate * candidate)
    grad_update = grad_output * (own - candidate) * update * (1.0 - update)
    grad_reset = grad_cand * hidden_pre[2] * reset * (1.0 - reset)
    grad_input = [grad_reset.astype(BF16), grad_update.astype(BF16), grad_cand.astype(BF16)]
    grad_hidden = [grad_input[0], grad_input[1], (grad_cand * reset).astype(BF16)]
    onto_ref[...] = sum(dot(input_ref[k], grad_input[k], TN) for k in range(3))
    back = pltpu.make_async_remote_copy(
        onto_ref.at[pl.ds(pl.multiple_of((1 - gate) * half, half), half)], back_ref, send_sem.at[1], recv_sem.at[1],
        device_id=partner, device_id_type=pl.DeviceIdType.MESH,
    )
    back.start()
    new_ref[...] = (keep * ((1.0 - update) * candidate + update * own)).astype(BF16)
    own_ref[...] = grad_output * update
    partial_ref[...] = sum(dot(hidden_ref[k], grad_hidden[k], TN) for k in range(3))
    for k in range(3):
        weights_ref[:, k * LANES : (k + 1) * LANES] = jnp.concatenate(
            [dot(grad_input[k], message, NT), dot(grad_hidden[k], full, NT)], axis=0
        ).astype(BF16)
    lane = iota((half, LANES), 1)
    sums = jnp.zeros((half, LANES), F32)
    for k, grad in enumerate(grad_input + grad_hidden):
        sums = jnp.where(lane == k, jnp.sum(grad.astype(F32), axis=1, keepdims=True), sums)
    biases_ref[...] = sums.T[:8]
    back.wait()
    kept = onto_ref[pl.ds(pl.multiple_of(gate * half, half), half), :]
    message_grad_ref[...] = (kept + back_ref[...]).astype(BF16)


def spread_units(units, parts):
    parts = min(units, parts)
    sizes = [units // parts + (1 if i < units % parts else 0) for i in range(parts)]
    return [(sum(sizes[:i]), sizes[i]) for i in range(parts)]


def event_order(members, digits, tiles, backs):
    if digits == 4:
        return [(KINDS[code // 16], code % 16) for code in SCHEDULE]
    parts = len(members)
    steps = [[] for _ in range(parts + 2 * digits + 4)]
    for g in range(parts):
        if g > 0:
            steps[g].append(("span", g))
        steps[g] += [("chunk", c) for c in members[g]]
        for phase in range(2 * digits):
            steps[g + phase + 1] += [("go", c) for c in members[g]]
    at = parts
    steps[at].append(("sources", 0))
    for i in range(tiles):
        steps[at + i // 2].append(("tiles", i))
    steps[at + 1].append(("rim", 0))
    steps[at + 3].append(("state", 0))
    at += (tiles + 1) // 2
    for i in range(digits + 2):
        steps[min(at + i, len(steps) - 1)].append(("first", i))
    for i in range(backs):
        steps[min(at + i, len(steps) - 1)].append(("back", i))
    steps[min(at + backs, len(steps) - 1)].append(("feat", 0))
    return [event for step in steps for event in step]


def finish_kernel(
    digits, per, ready, first_ref, first_bias_ref, meta_ref, grad_ref, states_ref, tiles_ref, table_hbm, second_hbm,
    grads_over_hbm, *rest,
):
    late_hbms, rest = rest[:12], rest[12:]
    total_ref, small_total_ref, feat_hbm, state_hbm, first_hbm, late_refs, *rest = rest
    finish_body(
        digits, per, ready, meta_ref, grad_ref, states_ref, first_ref, first_bias_ref, tiles_ref, table_hbm, second_hbm,
        grads_over_hbm, late_hbms, total_ref, small_total_ref, feat_hbm, state_hbm, first_hbm, late_refs, *rest,
    )


def finish_body(
    digits, per, ready, meta_ref, grad_ref, states_ref, first_ref, first_bias_ref, tiles_ref, table_hbm, second_hbm,
    grads_over_hbm, late_hbms, total_ref, small_total_ref, feat_hbm, state_hbm, first_hbm, late_refs, late_sem,
    feat_out_ref, state_out_ref,
    table_ref, weight_ref, grads_over_ref, hidden_ref, target_ref, slope_ref, wide_ref, spread_ref, outer_ref, grads_ref,
    work_ref, land_refs, small_ref, part_ref, rows_ref, source_ref, first_sum_ref,
    first_land_ref, feat_ref, feat_land_ref, rows_send_ref, rows_land_ref, rim_send_ref, rim_land_ref,
    send_sem, recv_sem, side_send, side_recv, first_send, first_recv, fetch_sem,
):
    (
        slot_ref, counts_ref, second_bias_ref, rows_over_ref, part_over_ref, first_over_ref, tile_ref, lane_ref, weights_ref,
        biases_ref, partial_ref, own_ref,
    ) = late_refs
    edge, gate = lax.axis_index("edge"), lax.axis_index("gate")
    count = 1 << digits
    half_width, node_count = grad_ref.shape
    main = tiles_ref.shape[0]
    padded = states_ref.shape[1]
    chunk_count = tile_ref.shape[0]
    over = part_over_ref.shape[0] // 16
    slots = source_ref.shape[0]
    border = slots - node_count
    width = grads_ref.shape[1]
    partner = (edge, 1 - gate)
    before = (lax.rem(edge + count - 1, count), gate)
    after = (lax.rem(edge + 1, count), gate)
    peers = [(edge ^ (1 << d), gate) for d in range(digits)]
    bits = [lax.rem(lax.shift_right_logical(edge, d), 2) for d in range(digits)]
    greeted = peers + [partner, before, after]
    barrier = pltpu.get_barrier_semaphore()
    for peer in greeted:
        pl.semaphore_signal(barrier, inc=1, device_id=peer, device_id_type=pl.DeviceIdType.MESH)

    unit = LANES << (digits - 3)
    orders = [[0, 1, 2], [1, 2, 0], [2, 0, 1], [1, 0, 2], [0, 2, 1], [2, 1, 0]]
    rest = list(range(3, digits))
    chunks = [
        (grads_ref, start * unit, start * unit, size * unit, orders[i % len(orders)] + rest, i // per)
        for i, (start, size) in enumerate(spread_units(width // unit, len(orders)))
    ]
    parts = chunks[-1][5] + 1
    chunks.append((small_ref, 0, width, small_ref.shape[1], orders[0] + rest, parts - 1))
    members = [[c for c in range(len(chunks)) if chunks[c][5] == g] for g in range(parts)]
    spans = []
    for g in range(parts):
        ours = [chunks[c] for c in members[g] if chunks[c][0] is grads_ref]
        spans.append((ours[0][2] // (2 * LANES), (ours[-1][2] + ours[-1][3]) // (2 * LANES)))

    fetch_weight = pltpu.make_async_copy(second_hbm, weight_ref, fetch_sem.at[0])
    fetch_over = pltpu.make_async_copy(grads_over_hbm, grads_over_ref, fetch_sem.at[1])
    fetch_table = pltpu.make_async_copy(table_hbm, table_ref, fetch_sem.at[2])
    fetch_weight.start()
    fetch_over.start()
    fetch_late = [
        pltpu.make_async_copy(source, target, late_sem.at[i])
        for i, (source, target) in enumerate(zip(late_hbms, late_refs))
    ]
    for fetch in fetch_late:
        fetch.start()

    def side(index, source, target, device):
        return pltpu.make_async_remote_copy(
            source, target, side_send.at[index], side_recv.at[index], device_id=device, device_id_type=pl.DeviceIdType.MESH
        )

    regions = []
    for _, _, place, lanes, order, _ in chunks:
        row, rows, lane = 0, 128, place
        levels = [(row, rows, lane, lanes)]
        for i, d in enumerate(order):
            if i < 3:
                rows //= 2
                row = row + bits[d] * rows
            else:
                lanes //= 2
                lane = lane + bits[d] * lanes
            levels.append((row, rows, lane, lanes))
        regions.append(levels)

    def window(row, rows, lane, lanes):
        if not isinstance(row, int):
            row = pl.multiple_of(row, 16)
        if not isinstance(lane, int):
            lane = pl.multiple_of(lane, LANES)
        return (pl.ds(row, rows), pl.ds(lane, lanes))

    def sibling(c, i):
        row, rows, lane, lanes = regions[c][i]
        d = chunks[c][4][i]
        if i < 3:
            return (row + (1 - bits[d]) * (rows // 2), rows // 2, lane, lanes)
        return (row, rows, lane + (1 - bits[d]) * (lanes // 2), lanes // 2)

    def landing(c, i):
        _, rows, _, lanes = regions[c][i + 1]
        return land_refs[i].at[pl.ds(0, rows), pl.ds(chunks[c][2] >> max(0, i - 2), lanes)]

    def inside(c, window_):
        source, at, place = chunks[c][:3]
        row, rows, lane, lanes = window_
        return source, window(row, rows, lane - place + at, lanes)

    def total_at(c, window_):
        row, rows, lane, lanes = window_
        if chunks[c][0] is small_ref:
            return small_total_ref, window(row, rows, lane - width, lanes)
        return total_ref, window(row, rows, lane, lanes)

    def scatter(c, i):
        if i == 0:
            source, at = inside(c, sibling(c, i))
            source = source.at[at]
        else:
            source = work_ref.at[window(*sibling(c, i))]
        return pltpu.make_async_remote_copy(
            source, landing(c, i), send_sem.at[c, i], recv_sem.at[c, i],
            device_id=peers[chunks[c][4][i]], device_id_type=pl.DeviceIdType.MESH,
        )

    def gather(c, i):
        ref, at = total_at(c, regions[c][i + 1])
        return pltpu.make_async_remote_copy(
            ref.at[at], ref.at[at], send_sem.at[c, 2 * digits - 1 - i], recv_sem.at[c, 2 * digits - 1 - i],
            device_id=peers[chunks[c][4][i]], device_id_type=pl.DeviceIdType.MESH,
        )

    def start(c, phase):
        if phase < digits:
            scatter(c, phase).start()
        elif phase < 2 * digits:
            gather(c, 2 * digits - 1 - phase).start()

    def arrive(c, phase):
        if phase < digits:
            scatter(c, phase).wait_recv()
            kept = regions[c][phase + 1]
            if phase == 0:
                source, at = inside(c, kept)
            else:
                source, at = work_ref, window(*kept)
            landed = landing(c, phase)
            value = source[at].astype(F32) + landed[...].astype(F32)
            if phase == digits - 1:
                target, at = total_at(c, kept)
            else:
                target, at = work_ref, window(*kept)
            target[at] = value.astype(BF16)
        else:
            gather(c, 2 * digits - 1 - phase).wait_recv()

    ready()
    first_t = extended_first(first_ref, first_bias_ref)
    wide_ref[...] = widened(grad_ref)

    def expand(t):
        held = tiles_ref[t]
        low, high, _ = tile_masks(held[17:18, :].astype(F32))
        pre = dot(first_t, held, TN)
        logistic = jax.nn.sigmoid(pre)
        hidden_ref[t] = halves(pre * logistic, low, high)
        slope_ref[t] = logistic * (1.0 + pre * (1.0 - logistic))
        target_ref[t] = target_hot(held[16:17, :].astype(F32), node_count)

    tile_loop(main, expand, 13)
    states = jnp.concatenate([states_ref[a, meta_ref[0, t]] for a in range(2) for t in range(main)], axis=0).astype(BF16)
    rows_ref[...] = jnp.zeros_like(rows_ref)

    def pair_grads(p):
        quarters = split_pair(outer_ref[:, p * 16 : (p + 1) * 16, :])
        cols = slice(p * 2 * LANES, (p + 1) * 2 * LANES)
        pair = weight_ref[:, cols]
        product = dot(quarters, states, TN)
        product = jnp.concatenate([product[:LANES], product[LANES:]], axis=1)
        grads_ref[:, cols] = (product + grads_over_ref[:, cols].astype(F32)).astype(BF16)
        rows_ref[...] += dot(quarters, jnp.concatenate([pair[:, :LANES], pair[:, LANES:]], axis=0))

    def span_outer(g):
        first, last = spans[g]
        rows = pl.ds(first * 16, (last - first) * 16)

        def spread(t):
            _, _, within = tile_masks(tiles_ref[t, 17:18, :].astype(F32))
            spread_ref[t, rows, :] = keep_within(dot(wide_ref[rows, :], target_ref[t]), within)

        def outer(t):
            outer_ref[t, rows, :] = dot(spread_ref[t, rows, :], hidden_ref[t], NT).astype(BF16)

        tile_loop(main, spread, main)
        tile_loop(main, outer, main)

    def chunk_grads(c):
        if chunks[c][0] is grads_ref:
            first = chunks[c][2] // (2 * LANES)
            for p in range(first, first + chunks[c][3] // (2 * LANES)):
                pair_grads(p)
        start(c, 0)

    span_outer(0)
    fetch_weight.wait()
    fetch_over.wait()
    pl.semaphore_wait(barrier, len(greeted))
    fetch_table.start()
    for fetch in fetch_late:
        fetch.wait()

    sums = dot(counts_ref[...], grad_ref[...], NT).astype(BF16)
    small_ref[...] = jnp.zeros_like(small_ref)
    small_ref[:half_width, :LANES] = dot(sums, group_states(states_ref), TN).astype(BF16)
    small_ref[half_width + ROWS : half_width + ROWS + 16, : biases_ref.shape[1]] = jnp.concatenate(
        [biases_ref[...], jnp.zeros_like(biases_ref)], axis=0
    ).astype(BF16)
    small_ref[:, LANES : 4 * LANES] = weights_ref[...]
    first_sum_ref[...] = first_over_ref[...]
    part_ref[main * 16 :, :] = part_over_ref[...]

    rows_copy = side(1, rows_send_ref, rows_land_ref, partner)
    rim_copy = side(2, rim_send_ref, rim_land_ref, before)
    feat_copy = side(3, feat_ref, feat_land_ref, partner)
    state_store = pltpu.make_async_copy(state_out_ref, state_hbm, late_sem.at[0])
    first_store = pltpu.make_async_copy(first_sum_ref, first_hbm, late_sem.at[1])
    feat_store = pltpu.make_async_copy(feat_out_ref, feat_hbm, late_sem.at[2])

    def source_rows():
        rows = slot_ref[0:1, : 2 * main * HALF].astype(jnp.int32)
        hot = (iota((slots, 2 * main * HALF), 0) == rows).astype(F32).astype(BF16)
        source_ref[...] = dot(hot, rows_ref[...].astype(BF16)) + rows_over_ref[:slots, :]
        bias = dot(sums, second_bias_ref[...])
        for g in range(padded):
            for a in range(2):
                at = g * GROUP + a * HALF
                size = min(HALF, GROUP - a * HALF, slots - at)
                if size > 0:
                    source_ref[at : at + size, :] += bias[(a * padded + g) * HALF : (a * padded + g) * HALF + size]
        source_ref[border:, :] += partial_ref[...].T
        rows_send_ref[...] = source_ref[...].astype(BF16)
        rows_copy.start()

    def rim_rows():
        rows_copy.wait()
        source_ref[...] += rows_land_ref[...].astype(F32)
        rim_send_ref[...] = source_ref[:border, :].astype(BF16)
        rim_copy.start()

    def state_rows():
        rim_copy.wait()
        source_ref[slots - border :, :] += rim_land_ref[...].astype(F32)
        rows = source_ref[border:, :].T
        state_out_ref[...] = jnp.where(gate == 0, rows[:half_width], rows[half_width:]) + own_ref[...]
        state_store.start()

    table_ready = []

    def tile_grads(first, last):
        if not table_ready:
            fetch_table.wait()
            table_ready.append(True)
        total = first_sum_ref[...]
        for t in range(first, last):
            table = table_ref[meta_ref[0, t]]
            part, first_grad = hidden_slopes(tiles_ref[t], table, spread_ref[t], slope_ref[t], first_ref[...])
            part_ref[t * 16 : (t + 1) * 16, :] = part
            total = total + first_grad
        first_sum_ref[...] = total

    def first_copy(i):
        device = partner if i == 0 else peers[i - 1]
        return pltpu.make_async_remote_copy(
            first_land_ref.at[2 * i], first_land_ref.at[2 * i + 1], first_send.at[i], first_recv.at[i],
            device_id=device, device_id_type=pl.DeviceIdType.MESH,
        )

    def first_step(i):
        if i > 0:
            first_copy(i - 1).wait()
            first_sum_ref[...] = first_land_ref[2 * i - 2] + first_land_ref[2 * i - 1]
        if i <= digits:
            first_land_ref[2 * i] = first_sum_ref[...]
            first_copy(i).start()
        else:
            first_store.start()

    def back(first, last):
        for c in range(first, last):
            cols = slice(c * LANES, (c + 1) * LANES)
            lane = lane_ref[c : c + 1, :].astype(jnp.int32)
            hot = (iota((TILE, LANES), 0) == lane).astype(F32).astype(BF16)
            moved = dot(part_ref[...], hot)
            tile = tile_ref[c : c + 1, :]
            total = jnp.zeros((16, LANES), F32)
            for t in range(main + over):
                total = total + jnp.where(tile == float(t), moved[t * 16 : (t + 1) * 16], 0.0)
            feat_ref[:, cols] = total
        if last == chunk_count:
            feat_copy.start()

    def feat_total():
        feat_copy.wait()
        feat_out_ref[...] = feat_ref[...] + feat_land_ref[...]
        feat_store.start()

    batch = 3
    tile_batches = range(0, main, batch)
    back_batches = range(0, chunk_count, 8)
    done = [0] * len(chunks)

    def go(c):
        arrive(c, done[c])
        start(c, done[c] + 1)
        done[c] += 1

    actions = {
        "span": span_outer,
        "chunk": chunk_grads,
        "go": go,
        "tiles": lambda i: tile_grads(tile_batches[i], min(tile_batches[i] + batch, main)),
        "first": first_step,
        "back": lambda i: back(back_batches[i], min(back_batches[i] + 8, chunk_count)),
        "sources": lambda i: source_rows(),
        "rim": lambda i: rim_rows(),
        "state": lambda i: state_rows(),
        "feat": lambda i: feat_total(),
    }
    for name, i in event_order(members, digits, len(tile_batches), len(back_batches)):
        actions[name](i)

    for c in range(len(chunks)):
        for phase in range(2 * digits):
            if phase < digits:
                scatter(c, phase).wait_send()
            else:
                gather(c, 2 * digits - 1 - phase).wait_send()
    for copy in (state_store, first_store, feat_store):
        copy.wait()


def emit_kernel(
    total_ref, small_ref, first_in_ref, new_in_ref, state_in_ref, feat_in_ref,
    new_ref, state_ref, feat_ref, first_ref, first_bias_ref, second_out, second_bias_ref, input_ref, hidden_ref,
    input_bias_ref, hidden_bias_ref,
    wide_ref, sems,
):
    blocks = sems.shape[0]
    size = wide_ref.shape[1] // blocks
    writes = []
    for i in range(blocks):
        cols = pl.ds(i * size, size)
        wide_ref[:, cols] = total_ref[:, cols].astype(F32)
        writes.append(pltpu.make_async_copy(wide_ref.at[:, cols], second_out.at[:, cols], sems.at[i]))
        writes[i].start()
    new_ref[...] = new_in_ref[...]
    state_ref[...] = state_in_ref[...]
    feat_ref[...] = feat_in_ref[...]
    small = small_ref[:, : 4 * LANES].astype(F32)
    half = second_bias_ref.shape[0]
    second_bias_ref[...] = small[:half, :LANES]
    first_ref[...] = first_in_ref[:16]
    first_bias_ref[...] = first_in_ref[18:19]
    part = input_ref.shape[1]
    at = half + ROWS
    input_bias_ref[...] = small[at : at + 3, :part]
    hidden_bias_ref[...] = small[at + 3 : at + 6, :part]
    for k in range(3):
        input_ref[k] = small[:part, LANES + k * LANES : LANES + (k + 1) * LANES]
        hidden_ref[k] = small[part:, LANES + k * LANES : LANES + (k + 1) * LANES]
    for copy in writes:
        copy.wait()


def per_device(
    node_state, edge_feat, source, target, edge_mask, node_mask, net_first, net_first_bias, net_second,
    net_second_bias, gru_input, gru_hidden, gru_input_bias, gru_hidden_bias, cotangent,
):
    node_count, half_width = node_state.shape
    edge_count = source.shape[0]
    width = 2 * half_width
    chunks = edge_count // LANES
    slots = BORDER + node_count
    groups = -(-slots // GROUP)
    padded = (groups + 1) // 2 * 2
    over = groups + edge_count // TILE - 1 - MAIN
    first_bias = net_first_bias.reshape(1, width)
    second_bias = net_second_bias.reshape(half_width, width)
    shape = jax.ShapeDtypeStruct
    vmem = pl.BlockSpec(memory_space=pltpu.VMEM)
    smem = pl.BlockSpec(memory_space=pltpu.SMEM)
    hbm = pl.BlockSpec(memory_space=pl.ANY)

    def local(mib):
        return pltpu.CompilerParams(vmem_limit_bytes=mib * MIB)

    def remote(collective_id, mib):
        return pltpu.CompilerParams(vmem_limit_bytes=mib * MIB, collective_id=collective_id, has_side_effects=True)

    state_t = node_state.T
    operands = in_hbm(
        source.reshape(chunks, LANES), target.reshape(chunks, LANES), edge_mask.reshape(chunks, LANES), edge_feat, state_t
    )
    body, specs, scratch = fetched(place_kernel, operands)
    full_t, states, placed, values, tile_rows, lane_rows, meta, slot_rows = pl.pallas_call(
        body,
        out_shape=(
            shape((width, node_count), BF16),
            shape((2, padded, HALF, width), F32),
            shape((MAIN, ROWS, TILE), BF16),
            shape((ROWS, edge_count), BF16),
            shape((chunks, LANES), F32),
            shape((chunks, LANES), F32),
            shape((8, LANES), jnp.int32),
            shape((8, -(-2 * MAIN * HALF // LANES) * LANES), F32),
        ),
        in_specs=specs,
        out_specs=(vmem,) * 8,
        scratch_shapes=[
            pltpu.VMEM((chunks * ROWS, LANES), BF16),
            pltpu.VMEM((MAIN * ROWS, edge_count), BF16),
            pltpu.VMEM((TILE, edge_count), BF16),
            pltpu.VMEM((half_width, node_count), BF16),
            pltpu.VMEM((2, half_width, LANES), BF16),
            pltpu.SemaphoreType.DMA((3,)),
            pltpu.SemaphoreType.DMA((3,)),
        ]
        + scratch,
        compiler_params=remote(0, 20),
        name="place_edges",
    )(*operands)

    blank_shapes = (
        pltpu.HBM((width, half_width * width), BF16),
        pltpu.HBM((padded * GROUP + 16, width), F32),
        pltpu.HBM((over * 16, TILE), BF16),
        pltpu.HBM((ROWS, width), F32),
    )
    (second,) = in_hbm(net_second)
    operands = in_hbm(net_first, first_bias, second_bias)
    body, specs, scratch = fetched(forward_kernel, operands)
    incoming, over_tiles, counts, table, *blanks = pl.pallas_call(
        body,
        out_shape=(
            shape((half_width, node_count), BF16),
            pltpu.HBM((over, ROWS, TILE), BF16),
            shape((2 * padded * HALF, node_count), BF16),
            pltpu.HBM((padded, half_width * HALF, 2 * width), BF16),
        )
        + blank_shapes,
        in_specs=specs + [smem, vmem] + [hbm] * 3 + [vmem, hbm],
        out_specs=(vmem, hbm, vmem) + (hbm,) * 5,
        scratch_shapes=[
            pltpu.VMEM((padded, 16, node_count), F32),
            pltpu.VMEM((padded, half_width * HALF, 2 * width), BF16),
            pltpu.VMEM((MAIN, 2 * width, TILE), BF16),
            pltpu.VMEM((MAIN, node_count, TILE), BF16),
            pltpu.VMEM((TILE, edge_count), BF16),
            pltpu.VMEM((half_width * HALF, node_count), F32),
            pltpu.VMEM((width, half_width * width), BF16),
            pltpu.VMEM((max(width, over * 16), half_width * width), BF16),
            pltpu.VMEM((padded * GROUP + 16, width), F32),
            pltpu.VMEM((ROWS, edge_count), BF16),
            pltpu.VMEM((chunks, LANES), F32),
            pltpu.VMEM((chunks, LANES), F32),
            pltpu.VMEM((ROWS, TILE), BF16),
            pltpu.SemaphoreType.DMA((3,)),
            pltpu.SemaphoreType.DMA((4,)),
        ]
        + scratch,
        compiler_params=local(36),
        name="forward_edges",
    )(*operands, meta, placed, values, tile_rows, lane_rows, states, second)

    operands = in_hbm(
        state_t, node_mask.reshape(node_count // LANES, LANES), gru_input.swapaxes(1, 2), gru_hidden.swapaxes(1, 2),
        gru_input_bias, gru_hidden_bias, cotangent.T
    )
    body, specs, scratch = fetched(node_kernel, operands)
    message_grad, new_state, grad_own, state_partial, weight_grads, bias_grads = pl.pallas_call(
        body,
        out_shape=(
            shape((half_width, node_count), BF16),
            shape((half_width, node_count), BF16),
            shape((half_width, node_count), F32),
            shape((width, node_count), F32),
            shape((width, 3 * width), BF16),
            shape((8, half_width), F32),
        ),
        in_specs=specs + [vmem] * 2,
        out_specs=(vmem,) * 6,
        scratch_shapes=[
            pltpu.VMEM((half_width, node_count), BF16),
            pltpu.VMEM((width, node_count), F32),
            pltpu.VMEM((half_width, node_count), F32),
            pltpu.SemaphoreType.DMA((2,)),
            pltpu.SemaphoreType.DMA((2,)),
        ]
        + scratch,
        compiler_params=remote(1, 6),
        name="node_update",
    )(*operands, incoming, full_t)

    grads_over, rows_over, part_over, first_over = pl.pallas_call(
        overflow_kernel,
        out_shape=blank_shapes,
        in_specs=[smem, hbm, hbm, hbm, hbm, hbm, hbm] + [hbm] * 5,
        out_specs=(hbm,) * 4,
        scratch_shapes=[
            pltpu.VMEM((half_width, node_count), BF16),
            pltpu.VMEM((16, width), BF16),
            pltpu.VMEM((1, width), BF16),
            pltpu.VMEM((ROWS, TILE), BF16),
            pltpu.VMEM((2, padded, HALF, width), F32),
            pltpu.VMEM((padded * GROUP + 16, width), F32),
            pltpu.VMEM((over * 16, TILE), BF16),
            pltpu.VMEM((ROWS, width), F32),
            pltpu.VMEM((width, half_width * width), F32),
            pltpu.VMEM((width, half_width * width), BF16),
            pltpu.VMEM((1, half_width * HALF, 2 * width), BF16),
            pltpu.VMEM((half_width * HALF, 2 * width), BF16),
            pltpu.SemaphoreType.DMA,
        ],
        input_output_aliases={8 + i: i for i in range(4)},
        compiler_params=local(16),
        name="overflow_edges",
    )(meta, message_grad, *in_hbm(net_first, first_bias), *in_hbm(over_tiles, table), states, second, *in_hbm(*blanks))

    digits = (lax.axis_size("edge") - 1).bit_length()
    unit = LANES << (digits - 3)
    columns = half_width * width
    small_width = max(4 * LANES, unit)
    per = 3
    steps = min(columns // unit, 6) + 1
    whole = columns + small_width
    late = (
        slot_rows, counts, *in_hbm(second_bias, rows_over, part_over, first_over), tile_rows, lane_rows, weight_grads, bias_grads,
        state_partial, grad_own,
    )
    operands = in_hbm(net_first, first_bias)
    body, specs, scratch = fetched(functools.partial(finish_kernel, digits, per), operands)
    total, small_total, grad_feat, grad_state, first_sum = pl.pallas_call(
        body,
        out_shape=(
            pltpu.VMEM((width, columns), BF16),
            pltpu.VMEM((width, small_width), BF16),
            shape((16, edge_count), F32),
            shape((half_width, node_count), F32),
            shape((ROWS, width), F32),
        ),
        in_specs=specs + [smem] + [vmem] * 3 + [hbm] * 3 + [hbm, hbm, hbm] + [hbm] * 3 + [hbm] * 6,
        out_specs=(vmem, vmem, hbm, hbm, hbm),
        scratch_shapes=[
            [pltpu.VMEM(x.shape, x.dtype) for x in late],
            pltpu.SemaphoreType.DMA((len(late),)),
            pltpu.VMEM((16, edge_count), F32),
            pltpu.VMEM((half_width, node_count), F32),
            pltpu.VMEM((padded, half_width * HALF, 2 * width), BF16),
            pltpu.VMEM((width, columns), BF16),
            pltpu.VMEM((width, columns), BF16),
            pltpu.VMEM((MAIN, 2 * width, TILE), BF16),
            pltpu.VMEM((MAIN, node_count, TILE), BF16),
            pltpu.VMEM((MAIN, width, TILE), F32),
            pltpu.VMEM((half_width * HALF, node_count), BF16),
            pltpu.VMEM((MAIN, half_width * HALF, TILE), BF16),
            pltpu.VMEM((MAIN, half_width * HALF, 2 * width), BF16),
            pltpu.VMEM((width, columns), BF16),
            pltpu.VMEM((width, whole), BF16),
            [pltpu.VMEM((max(16, width >> (i + 1)), whole >> max(0, i - 2)), BF16) for i in range(digits)],
            pltpu.VMEM((width, small_width), BF16),
            pltpu.VMEM(((MAIN + over) * 16, TILE), BF16),
            pltpu.VMEM((2 * MAIN * HALF, width), F32),
            pltpu.VMEM((slots, width), F32),
            pltpu.VMEM((ROWS, width), F32),
            pltpu.VMEM((2 * digits + 2, ROWS, width), F32),
            pltpu.VMEM((16, edge_count), F32),
            pltpu.VMEM((16, edge_count), F32),
            pltpu.VMEM((slots, width), BF16),
            pltpu.VMEM((slots, width), BF16),
            pltpu.VMEM((BORDER, width), BF16),
            pltpu.VMEM((BORDER, width), BF16),
            pltpu.SemaphoreType.DMA((steps, 2 * digits)),
            pltpu.SemaphoreType.DMA((steps, 2 * digits)),
            pltpu.SemaphoreType.DMA((4,)),
            pltpu.SemaphoreType.DMA((4,)),
            pltpu.SemaphoreType.DMA((digits + 1,)),
            pltpu.SemaphoreType.DMA((digits + 1,)),
            pltpu.SemaphoreType.DMA((3,)),
        ]
        + scratch,
        compiler_params=remote(2, 48),
        name="finish_sums",
    )(
        *operands, meta, message_grad, states, placed, *in_hbm(table), second, *in_hbm(grads_over), *late,
    )

    blocks = 8
    outs = pl.pallas_call(
        emit_kernel,
        out_shape=(
            shape((half_width, node_count), BF16),
            shape((half_width, node_count), F32),
            shape((16, edge_count), F32),
            shape((16, width), F32),
            shape((1, width), F32),
            shape((width, columns), F32),
            shape((half_width, width), F32),
            shape((3, half_width, width), F32),
            shape((3, half_width, width), F32),
            shape((3, half_width), F32),
            shape((3, half_width), F32),
        ),
        in_specs=[vmem] * 6,
        out_specs=(vmem,) * 5 + (hbm,) + (vmem,) * 5,
        scratch_shapes=[
            pltpu.VMEM((width, columns), F32),
            pltpu.SemaphoreType.DMA((blocks,)),
        ],
        compiler_params=local(12),
        name="emit",
    )(total, small_total, first_sum, new_state, grad_state, grad_feat)
    outs = list(outs)
    outs[0], outs[1] = outs[0].T, outs[1].T
    outs[7], outs[8] = outs[7].swapaxes(1, 2), outs[8].swapaxes(1, 2)
    outs[4] = outs[4].reshape(width)
    outs[6] = outs[6].reshape(columns)
    return tuple(outs)


def solution(mesh):
    return jax.shard_map(
        per_device,
        mesh=mesh,
        in_specs=(
            P("edge", "gate"), P(None, "edge"), P("edge"), P("edge"), P("edge"), P("edge"), P(), P(), P(None, "gate"),
            P("gate"), P(None, None, "gate"), P(None, None, "gate"), P(None, "gate"), P(None, "gate"), P("edge", "gate"),
        ),
        out_specs=(
            P("edge", "gate"), P("edge", "gate"), P(None, "edge"), P(), P(), P(None, "gate"), P("gate"),
            P(None, None, "gate"), P(None, None, "gate"), P(None, "gate"), P(None, "gate"),
        ),
        check_vma=False,
    )
```

```python
import functools

import jax
import jax.numpy as jnp
from jax import lax
from jax.experimental import pallas as pl
from jax.experimental.pallas import tpu as pltpu
from jax.sharding import PartitionSpec as P

BORDER = 64
GROUP = 14
HALF = 8
TILE = 256
MAIN = 26
UNROLL_ROWS = 8
UNROLL_PAIRS = 99
UNROLL_SPAN = 26
UNROLL_BACK = 8
UNROLL_TILES = 3
TILE_BATCH = 3
LANES = 128
ROWS = 32
MIB = 1024 * 1024

KINDS = ("span", "chunk", "go", "tiles", "first", "back", "sources", "rim", "state", "feat", "rows")
SIZES = (5, 7, 4, 5, 6, 5)
ORDERS = ((0, 1, 2), (1, 2, 0), (2, 0, 1), (1, 0, 2), (0, 2, 1), (2, 1, 0), (0, 1, 2))
FIRST_SPAN = 3
SCHEDULE = (
    16, 17, 18, 1, 22, 21, 20, 49, 32, 55, 38, 33, 19, 52, 34, 32, 50, 37, 38, 36, 33, 54, 34, 38, 32, 35, 48, 33,
    53, 37, 38, 34, 36, 32, 35, 160, 33, 51, 38, 37, 36, 32, 56, 35, 33, 64, 38, 37, 65, 32, 36, 34, 38, 161, 35, 66,
    33, 37, 36, 32, 162, 34, 67, 37, 163, 35, 36, 34, 33, 96, 35, 37, 80, 82, 36, 68, 34, 81, 35, 83, 112, 38, 144,
    32, 37, 69, 128, 36, 33, 35, 34,
)

NN = ((1,), (0,))
NT = ((1,), (1,))
TN = ((0,), (0,))
F32 = jnp.float32
BF16 = jnp.bfloat16


def dot(left, right, dims=NN):
    return lax.dot_general(left, right, (dims, ((), ())), preferred_element_type=F32)


def iota(shape, dim):
    return lax.broadcasted_iota(jnp.int32, shape, dim)


def extended_first(first_ref, bias_ref):
    extra = jnp.where(iota((ROWS - 16, LANES), 0) == 2, bias_ref[...].astype(F32), 0.0)
    return jnp.concatenate([first_ref[...].astype(F32), extra], axis=0).astype(BF16)


def tile_masks(slot_row):
    place = slot_row.astype(jnp.int32) - 1
    low = jnp.logical_and(place >= 0, place < HALF)
    high = place >= HALF
    within = jnp.where(high, place - HALF, place)
    return low, high, within


def halves(hidden, low, high):
    return jnp.concatenate(
        [jnp.where(low, hidden, 0.0), jnp.where(high, hidden, 0.0)], axis=0
    ).astype(BF16)


def keep_within(values, within):
    rows, width = values.shape
    match = iota((HALF, width), 0) == within
    kept = jnp.where(match[None], values.reshape(rows // HALF, HALF, width), 0.0)
    return kept.reshape(rows, width).astype(BF16)


def target_hot(target_row, node_count):
    width = target_row.shape[1]
    return (iota((node_count, width), 0) + 1 == target_row.astype(jnp.int32)).astype(F32).astype(BF16)


def lane_hot(lane_ref, out_ref):
    chunks = lane_ref.shape[0]
    for c in range(chunks):
        row = lane_ref[c : c + 1, :].astype(jnp.int32)
        out_ref[:, c * LANES : (c + 1) * LANES] = (
            (iota((TILE, LANES), 0) == row).astype(F32).astype(BF16)
        )


def aligned(index, unit):
    return index * unit if isinstance(index, int) else pl.multiple_of(index * unit, unit)


def tile_loop(count, body, step):
    def several(i, carry):
        for s in range(step):
            body(i * step + s)
        return carry

    whole = count // step if step < count else 0
    if whole:
        lax.fori_loop(0, whole, several, 0)
    for t in range(whole * step, count):
        body(t)


def fetched(kernel, operands):
    count = len(operands)

    def body(*refs):
        sources, others, targets, sem = refs[:count], refs[count : -count - 1], refs[-count - 1 : -1], refs[-1]
        copies = [pltpu.make_async_copy(sources[i], targets[i], sem.at[i]) for i in range(count)]
        for copy in copies:
            copy.start()

        def ready():
            for copy in copies:
                copy.wait()

        kernel(ready, *targets, *others)

    scratch = [pltpu.VMEM(x.shape, x.dtype) for x in operands] + [pltpu.SemaphoreType.DMA((count,))]
    return body, [pl.BlockSpec(memory_space=pl.ANY)] * count, scratch


def in_hbm(*arrays):
    return tuple(pltpu.with_memory_space_constraint(x, pltpu.HBM) for x in arrays)


def place_kernel(
    ready, source_ref, target_ref, mask_ref, feat_ref, state_ref, second_hbm, second_bias_hbm, first_hbm, first_bias_hbm,
    second_ref, second_bias_ref, first_ref, first_bias_ref, full_ref, states_ref, tiles_ref, values_ref, tile_ref, lane_ref, meta_ref, slot_ref,
    counts_ref, spread_ref, hot_ref, other_ref, rim_ref, send_sem, recv_sem, load_sem,
):
    chunks = source_ref.shape[0]
    half, node_count = state_ref.shape
    main = tiles_ref.shape[0]
    padded = states_ref.shape[1]
    groups = -(-(node_count + BORDER) // GROUP)
    edge, gate = lax.axis_index("edge"), lax.axis_index("gate")
    count = lax.axis_size("edge")
    first_node = edge * node_count
    partner = (edge, 1 - gate)
    after = lax.rem(edge + 1, count)
    before = lax.rem(edge + count - 1, count)
    mesh_signal(
        pltpu.get_barrier_semaphore(), [partner, (after, gate), (after, 1 - gate), (before, gate), (before, 1 - gate)]
    )

    def send(index, source, target, device):
        return pltpu.make_async_remote_copy(
            source, target, send_sem.at[index], recv_sem.at[index], device_id=device, device_id_type=pl.DeviceIdType.MESH
        )

    loads = [
        pltpu.make_async_copy(far, near, load_sem.at[i])
        for i, (far, near) in enumerate(
            [(first_hbm, first_ref), (first_bias_hbm, first_bias_ref), (second_bias_hbm, second_bias_ref), (second_hbm, second_ref)]
        )
    ]
    ready()
    for load in loads:
        load.start()
    rim = state_ref.at[:, pl.ds(node_count - LANES, LANES)]
    copies = [
        send(0, rim, rim_ref.at[0], (after, gate)),
        send(1, rim, rim_ref.at[1], (after, 1 - gate)),
        send(2, state_ref, other_ref, partner),
    ]
    for copy in copies:
        copy.start()

    group_rows = []
    slot_rows = []
    for c in range(chunks):
        slot = (source_ref[c : c + 1, :] - first_node + BORDER).astype(F32)
        group = jnp.floor((slot + 0.5) * (1.0 / GROUP))
        slot_rows.append(slot)
        group_rows.append(group)
        counts_ref[c * ROWS : (c + 1) * ROWS, :] = (
            (iota((ROWS, LANES), 0).astype(F32) == group).astype(F32).astype(BF16)
        )
    above = jnp.where(
        iota((LANES, 2 * LANES), 0) < iota((LANES, 2 * LANES), 1), 1.0, 0.0
    ).astype(BF16)
    sums = dot(counts_ref[...], above)
    running = jnp.zeros((ROWS, LANES), F32)
    ranks = []
    for c in range(chunks):
        hot = counts_ref[c * ROWS : (c + 1) * ROWS, :].astype(F32)
        part = sums[c * ROWS : (c + 1) * ROWS]
        ranks.append(jnp.sum(hot * (part[:, :LANES] + running), axis=0, keepdims=True))
        running = running + part[:, LANES:]
    owned = jnp.floor((running + (TILE - 1.0)) * (1.0 / TILE))
    earlier = (iota((ROWS, ROWS), 1) < iota((ROWS, ROWS), 0)).astype(F32).astype(BF16)
    start = dot(earlier, owned.astype(BF16))
    end = start + owned
    total = jnp.sum(owned, axis=0, keepdims=True)

    def group_of(tile):
        return jnp.minimum(jnp.sum((end <= tile).astype(F32), axis=0, keepdims=True), groups - 1.0)

    row8 = iota((8, LANES), 0)
    lane = iota((1, LANES), 1).astype(F32)
    meta_ref[...] = jnp.where(row8 == 0, group_of(lane), jnp.where(row8 == 1, total, 0.0)).astype(jnp.int32)
    for c in range(slot_ref.shape[1] // LANES):
        row = lane + float(c * LANES)
        high = jnp.where(row >= main * HALF, 1.0, 0.0)
        row = row - high * (main * HALF)
        tile = jnp.floor((row + 0.5) * (1.0 / HALF))
        place = row - tile * HALF + high * HALF
        slot = group_of(tile) * GROUP + place
        slot = jnp.where(jnp.logical_and(place < GROUP, tile < jnp.minimum(total, float(main))), slot, -1.0)
        slot_ref[:, c * LANES : (c + 1) * LANES] = jnp.broadcast_to(slot, (8, LANES))

    row16 = iota((ROWS - 16, LANES), 0)
    for c in range(chunks):
        cols = slice(c * LANES, (c + 1) * LANES)
        hot = counts_ref[c * ROWS : (c + 1) * ROWS, :].astype(F32)
        over = jnp.floor(ranks[c] * (1.0 / TILE))
        tile = jnp.sum(hot * start, axis=0, keepdims=True) + over
        lane = ranks[c] - TILE * over
        tile_ref[c : c + 1, :] = tile
        lane_ref[c : c + 1, :] = lane
        hot_ref[:, cols] = (iota((TILE, LANES), 0).astype(F32) == lane).astype(F32).astype(BF16)
        place = slot_rows[c] - GROUP * group_rows[c] + 1.0
        target = jnp.where(
            mask_ref[c : c + 1, :] > 0, target_ref[c : c + 1, :] - first_node + 1, 0
        ).astype(F32)
        more = jnp.where(row16 == 0, target, jnp.where(row16 == 1, place, jnp.where(row16 == 2, 1.0, 0.0)))
        values = jnp.concatenate([feat_ref[:, cols].astype(F32), more], axis=0)
        values_ref[:, cols] = values.astype(BF16)
        for t in range(main):
            spread_ref[t * ROWS : (t + 1) * ROWS, cols] = jnp.where(tile == float(t), values, 0.0).astype(BF16)
    moved = dot(spread_ref[...], hot_ref[...], NT)
    tiles_ref[...] = moved.reshape(main, ROWS, TILE).astype(BF16)

    for copy in copies:
        copy.wait()
    is_first = gate == 0
    mine, other = state_ref[...], other_ref[...]
    full = jnp.concatenate([jnp.where(is_first, mine, other), jnp.where(is_first, other, mine)], axis=0)
    full_ref[...] = full
    own, swapped = rim_ref[0], rim_ref[1]
    rims = jnp.concatenate([jnp.where(is_first, own, swapped), jnp.where(is_first, swapped, own)], axis=0)
    rows = jnp.concatenate(
        [rims.astype(F32).T[LANES - BORDER :], full.astype(F32).T], axis=0
    )
    spare = padded * GROUP + 16 - rows.shape[0]
    rows = jnp.concatenate([rows, jnp.zeros((spare, 2 * half), F32)], axis=0)
    for load in loads:
        load.wait()
    for g in range(padded):
        for a in range(2):
            states_ref[a, g] = rows[g * GROUP + a * HALF : g * GROUP + (a + 1) * HALF]


def group_states(states_ref):
    _, padded, half, width = states_ref.shape
    return jnp.concatenate([states_ref[a].reshape(padded * half, width) for a in range(2)], axis=0).astype(BF16)


def group_counts(counts_ref):
    padded, _, node_count = counts_ref.shape
    return jnp.concatenate(
        [counts_ref[:, a * HALF : (a + 1) * HALF, :].reshape(padded * HALF, node_count) for a in range(2)], axis=0
    ).astype(BF16)


def forward_kernel(
    first_ref, first_bias_ref, second_bias_ref, second_ref, meta_ref, tiles_ref, values_hbm, tile_hbm, lane_hbm, states_ref,
    incoming_ref, over_hbm, counts_out_ref, table_out_ref, hidden_ref, targets_ref, *rest,
):
    blank_refs, rest = rest[:4], rest[4:]
    counts_ref, table_ref, hidden_over_ref, targets_over_ref, hot_ref, total_ref, narrow_ref, zeros_ref = rest[:8]
    values_ref, tile_ref, lane_ref, held_ref, sems, blank_sems = rest[8:]
    chunks = tile_ref.shape[0]
    half_width, node_count = incoming_ref.shape
    main = tiles_ref.shape[0]
    padded = table_ref.shape[0]
    over_total = jnp.maximum(meta_ref[1, 0] - main, 0)
    narrow_ref[...] = jnp.zeros_like(narrow_ref)
    zeros_ref[...] = jnp.zeros_like(zeros_ref)
    blanks = []
    for i, blank_ref in enumerate(blank_refs):
        rows, cols = blank_ref.shape
        zeros = narrow_ref if blank_ref.dtype == BF16 else zeros_ref
        blanks.append(pltpu.make_async_copy(zeros.at[pl.ds(0, rows), pl.ds(0, cols)], blank_ref, blank_sems.at[i]))
        blanks[i].start()
    first_t = extended_first(first_ref, first_bias_ref)

    def expand(held):
        low, high, _ = tile_masks(held[17:18, :].astype(F32))
        pre = dot(first_t, held, TN)
        return halves(pre * jax.nn.sigmoid(pre), low, high), target_hot(held[16:17, :].astype(F32), node_count)

    def expand_main(t):
        hidden_ref[t], targets_ref[t] = expand(tiles_ref[t])

    tile_loop(main, expand_main, 13)

    states = group_states(states_ref)

    def table_pair(p):
        pair = second_ref[:, pl.ds(pl.multiple_of(p * 2 * LANES, 2 * LANES), 2 * LANES)]
        both = jnp.concatenate([pair[:, :LANES], pair[:, LANES:]], axis=0)
        product = dot(states, both, NT).reshape(2, padded, HALF, 2 * LANES)
        for a in range(2):
            rows = jnp.concatenate([product[a, :, :, :LANES], product[a, :, :, LANES:]], axis=1)
            table_ref[:, pl.ds(pl.multiple_of(p * 16, 16), 16), a * LANES : (a + 1) * LANES] = rows.astype(BF16)

    tile_loop(half_width // 2, table_pair, 16)
    keep = pltpu.make_async_copy(table_ref, table_out_ref, sems.at[1])
    keep.start()

    def messages(hidden, targets, group, held):
        _, _, within = tile_masks(held[17:18, :].astype(F32))
        message = keep_within(dot(table_ref[group], hidden), within)
        place = held[17:18, :].astype(jnp.int32) - 1
        places = (iota((16, TILE), 0) == place).astype(F32).astype(BF16)
        sums = dot(jnp.concatenate([message, places], axis=0), targets, NT)
        total_ref[...] += sums[: half_width * HALF]
        counts_ref[group] += sums[half_width * HALF :]

    total_ref[...] = jnp.zeros_like(total_ref)
    counts_ref[...] = jnp.zeros_like(counts_ref)
    tile_loop(main, lambda t: messages(hidden_ref[t], targets_ref[t], meta_ref[0, t], tiles_ref[t]), 13)

    @pl.when(over_total > 0)
    def _():
        for source, target in [(values_hbm, values_ref), (tile_hbm, tile_ref), (lane_hbm, lane_ref)]:
            load = pltpu.make_async_copy(source, target, sems.at[2])
            load.start()
            load.wait()
        lane_hot(lane_ref, hot_ref)

    def over_messages(u, carry):
        wanted = (main + u).astype(F32)
        pieces = []
        for c in range(chunks):
            values = values_ref[:, c * LANES : (c + 1) * LANES].astype(F32)
            pieces.append(jnp.where(tile_ref[c : c + 1, :] == wanted, values, 0.0).astype(BF16))
        held = dot(jnp.concatenate(pieces, axis=1), hot_ref[...], NT).astype(BF16)
        held_ref[...] = held
        save = pltpu.make_async_copy(held_ref, over_hbm.at[u], sems.at[2])
        save.start()
        save.wait()
        hidden_over_ref[...], targets_over_ref[...] = expand(held)
        messages(hidden_over_ref[...], targets_over_ref[...], meta_ref[0, main + u], held)
        return carry

    lax.fori_loop(0, over_total, over_messages, 0)
    bias = dot(second_bias_ref[...], states, NT)
    summed = jnp.sum(total_ref[...].reshape(half_width, HALF, node_count), axis=1)
    counts = group_counts(counts_ref)
    counts_out_ref[...] = counts
    incoming_ref[...] = (summed + dot(bias.astype(BF16), counts)).astype(BF16)
    keep.wait()
    for blank in blanks:
        blank.wait()


def expand_tile(held, first_t, wide, node_count):
    low, high, within = tile_masks(held[17:18, :].astype(F32))
    pre = dot(first_t, held, TN)
    logistic = jax.nn.sigmoid(pre)
    hidden = halves(pre * logistic, low, high)
    slope = logistic * (1.0 + pre * (1.0 - logistic))
    spread = keep_within(dot(wide, target_hot(held[16:17, :].astype(F32), node_count)), within)
    return hidden, slope, spread


def widened(grad_ref):
    half_width, node_count = grad_ref.shape
    wide = jnp.broadcast_to(grad_ref[...].astype(F32)[:, None, :], (half_width, HALF, node_count))
    return wide.reshape(half_width * HALF, node_count).astype(BF16)


def hidden_slopes(held, table, spread, slope, first):
    low, _, _ = tile_masks(held[17:18, :].astype(F32))
    grad_hidden = dot(table, spread, TN)
    grad_hidden = jnp.where(low, grad_hidden[:LANES], grad_hidden[LANES:])
    grad_pre = (grad_hidden * slope).astype(BF16)
    return dot(first, grad_pre).astype(BF16), dot(held, grad_pre, NT)


def split_pair(held):
    tiles = held.shape[0]
    held = held.astype(F32)
    parts = []
    for q in range(2):
        rows = held[:, q * HALF : (q + 1) * HALF, :].reshape(tiles * HALF, 2 * LANES).astype(BF16)
        parts.append(jnp.concatenate([rows[:, :LANES], rows[:, LANES:]], axis=0))
    return jnp.concatenate(parts, axis=1)


def overflow_kernel(
    meta_ref, grad_hbm, first_hbm, first_bias_hbm, over_hbm, table_hbm, states_hbm, second_hbm, _grads, _rows, _part, _first,
    grads_hbm, rows_hbm, part_hbm, first_grad_hbm,
    grad_ref, first_ref, first_bias_ref, over_ref, states_ref, rows_ref, part_ref, first_grad_ref,
    grads_ref, weight_ref, outer_ref, table_ref, sem,
):
    total = jnp.maximum(meta_ref[1, 0] - MAIN, 0)

    def move(source, target):
        copy = pltpu.make_async_copy(source, target, sem)
        copy.start()
        copy.wait()

    @pl.when(total > 0)
    def _():
        half_width, node_count = grad_ref.shape
        move(grad_hbm, grad_ref)
        move(first_hbm, first_ref)
        move(first_bias_hbm, first_bias_ref)
        move(states_hbm, states_ref)
        move(second_hbm, weight_ref)
        first_grad_ref[...] = jnp.zeros_like(first_grad_ref)
        part_ref[...] = jnp.zeros_like(part_ref)
        rows_ref[...] = jnp.zeros_like(rows_ref)
        grads_ref[...] = jnp.zeros_like(grads_ref)
        first_t = extended_first(first_ref, first_bias_ref)
        wide = widened(grad_ref)

        def tile_work(u, carry):
            group = meta_ref[0, MAIN + u]
            move(table_hbm.at[group], table_ref)
            move(over_hbm.at[u], over_ref)
            held = over_ref[...]
            hidden, slope, spread = expand_tile(held, first_t, wide, node_count)
            outer_ref[0] = dot(spread, hidden, NT).astype(BF16)
            part, first_grad = hidden_slopes(held, table_ref[...], spread, slope, first_ref[...])
            part_ref[pl.ds(pl.multiple_of(u * 16, 16), 16), :] = part
            first_grad_ref[...] += first_grad
            states = jnp.concatenate([states_ref[0, group], states_ref[1, group]], axis=0).astype(BF16)

            def pair_work(p, carry):
                cols = pl.ds(pl.multiple_of(p * 2 * LANES, 2 * LANES), 2 * LANES)
                quarters = split_pair(outer_ref[:, pl.ds(pl.multiple_of(p * 16, 16), 16), :])
                product = dot(quarters, states, TN)
                grads_ref[:, cols] += jnp.concatenate([product[:LANES], product[LANES:]], axis=1)
                pair = weight_ref[:, cols]
                return carry + dot(quarters, jnp.concatenate([pair[:, :LANES], pair[:, LANES:]], axis=0))

            rows = lax.fori_loop(0, half_width // 2, pair_work, jnp.zeros((2 * HALF, LANES), F32))
            at = group * GROUP
            rows_ref[pl.ds(at, HALF), :] += rows[:HALF]
            rows_ref[pl.ds(at + HALF, HALF), :] += rows[HALF:]
            return carry

        lax.fori_loop(0, total, tile_work, 0)
        weight_ref[...] = grads_ref[...].astype(BF16)
        move(weight_ref, grads_hbm)
        move(rows_ref, rows_hbm)
        move(part_ref, part_hbm)
        move(first_grad_ref, first_grad_hbm)


def mesh_signal(sem, peers):
    for peer in peers:
        pl.semaphore_signal(sem, inc=1, device_id=peer, device_id_type=pl.DeviceIdType.MESH)
    pl.semaphore_wait(sem, len(peers))


def node_kernel(
    ready, state_ref, mask_ref, input_ref, hidden_ref, input_bias_ref, hidden_bias_ref, cotangent_ref, incoming_ref, full_ref,
    message_grad_ref, new_ref, own_ref, partial_ref, weights_ref, biases_ref,
    other_ref, onto_ref, back_ref, send_sem, recv_sem,
):
    edge, gate = lax.axis_index("edge"), lax.axis_index("gate")
    partner = (edge, 1 - gate)
    half = state_ref.shape[0]
    mesh_signal(pltpu.get_barrier_semaphore(), [partner])
    swap = pltpu.make_async_remote_copy(
        incoming_ref, other_ref, send_sem.at[0], recv_sem.at[0], device_id=partner, device_id_type=pl.DeviceIdType.MESH
    )
    swap.start()
    ready()
    full = full_ref[...]
    biases = jnp.concatenate(
        [input_bias_ref[...].astype(F32), hidden_bias_ref[...].astype(F32), jnp.zeros((2, half), F32)], axis=0
    ).T
    hidden_pre = [dot(hidden_ref[k], full) + biases[:, 3 + k : 4 + k] for k in range(3)]
    keep = jnp.concatenate([mask_ref[c : c + 1, :] for c in range(mask_ref.shape[0])], axis=1).astype(F32)
    own = state_ref[...].astype(F32)
    grad_output = cotangent_ref[...].astype(F32) * keep
    mine = incoming_ref[...]
    swap.wait()
    other = other_ref[...]
    is_first = gate == 0
    message = jnp.concatenate(
        [jnp.where(is_first, mine, other), jnp.where(is_first, other, mine)], axis=0
    )
    input_pre = [dot(input_ref[k], message) + biases[:, k : k + 1] for k in range(3)]
    reset = jax.nn.sigmoid(input_pre[0] + hidden_pre[0])
    update = jax.nn.sigmoid(input_pre[1] + hidden_pre[1])
    candidate = jnp.tanh(input_pre[2] + reset * hidden_pre[2])
    grad_cand = grad_output * (1.0 - update) * (1.0 - candidate * candidate)
    grad_update = grad_output * (own - candidate) * update * (1.0 - update)
    grad_reset = grad_cand * hidden_pre[2] * reset * (1.0 - reset)
    grad_input = [grad_reset.astype(BF16), grad_update.astype(BF16), grad_cand.astype(BF16)]
    grad_hidden = [grad_input[0], grad_input[1], (grad_cand * reset).astype(BF16)]
    onto_ref[...] = sum(dot(input_ref[k], grad_input[k], TN) for k in range(3))
    back = pltpu.make_async_remote_copy(
        onto_ref.at[pl.ds(pl.multiple_of((1 - gate) * half, half), half)], back_ref, send_sem.at[1], recv_sem.at[1],
        device_id=partner, device_id_type=pl.DeviceIdType.MESH,
    )
    back.start()
    new_ref[...] = (keep * ((1.0 - update) * candidate + update * own)).astype(BF16)
    own_ref[...] = grad_output * update
    partial_ref[...] = sum(dot(hidden_ref[k], grad_hidden[k], TN) for k in range(3))
    for k in range(3):
        weights_ref[:, k * LANES : (k + 1) * LANES] = jnp.concatenate(
            [dot(grad_input[k], message, NT), dot(grad_hidden[k], full, NT)], axis=0
        ).astype(BF16)
    lane = iota((half, LANES), 1)
    sums = jnp.zeros((half, LANES), F32)
    for k, grad in enumerate(grad_input + grad_hidden):
        sums = jnp.where(lane == k, jnp.sum(grad.astype(F32), axis=1, keepdims=True), sums)
    biases_ref[...] = sums.T[:8]
    back.wait()
    kept = onto_ref[pl.ds(pl.multiple_of(gate * half, half), half), :]
    message_grad_ref[...] = (kept + back_ref[...]).astype(BF16)


def chunk_plan(units, digits):
    orders = [list(order) + list(range(3, digits)) for order in ORDERS]
    count = len(SIZES)
    sizes = SIZES
    if units != sum(SIZES):
        count = min(units, count)
        sizes = [units // count + (1 if i < units % count else 0) for i in range(count)]
    plan = [(sum(sizes[:i]), sizes[i], orders[i], 0 if i < FIRST_SPAN else 1) for i in range(count)]
    return plan, orders[-1]


def event_order(members, digits, tiles, backs, rows):
    if digits == 4 and len(members) == 2:
        return [(KINDS[code // 16], code % 16) for code in SCHEDULE]
    parts = len(members)
    steps = [[] for _ in range(parts + 2 * digits + 4)]
    for g in range(parts):
        if g > 0:
            steps[g].append(("span", g))
        steps[g] += [("chunk", c) for c in members[g]]
        for phase in range(2 * digits):
            steps[g + phase + 1] += [("go", c) for c in members[g]]
    at = parts
    steps[at] += [("rows", i) for i in range(rows)]
    steps[at].append(("sources", 0))
    for i in range(tiles):
        steps[at + i // 2].append(("tiles", i))
    steps[at + 1].append(("rim", 0))
    steps[at + 3].append(("state", 0))
    at += (tiles + 1) // 2
    for i in range(digits + 2):
        steps[min(at + i, len(steps) - 1)].append(("first", i))
    for i in range(backs):
        steps[min(at + i, len(steps) - 1)].append(("back", i))
    steps[min(at + backs, len(steps) - 1)].append(("feat", 0))
    return [event for step in steps for event in step]


def finish_kernel(
    digits, first_ref, first_bias_ref, second_bias_ref, weight_ref, meta_ref, grad_ref, states_ref, tiles_ref, hidden_ref,
    target_ref, table_hbm, grads_over_hbm, *rest,
):
    late_hbms, rest = rest[:11], rest[11:]
    total_ref, small_total_ref, feat_hbm, state_hbm, first_hbm, late_refs, *rest = rest
    finish_body(
        digits, meta_ref, grad_ref, states_ref, first_ref, first_bias_ref, second_bias_ref, weight_ref, tiles_ref, hidden_ref,
        target_ref, table_hbm, grads_over_hbm, late_hbms, total_ref, small_total_ref, feat_hbm, state_hbm, first_hbm, late_refs, *rest,
    )


def finish_body(
    digits, meta_ref, grad_ref, states_ref, first_ref, first_bias_ref, second_bias_ref, weight_ref, tiles_ref, hidden_ref,
    target_ref, table_hbm, grads_over_hbm, late_hbms, total_ref, small_total_ref, feat_hbm, state_hbm, first_hbm, late_refs, late_sem,
    feat_out_ref, state_out_ref,
    table_ref, grads_over_ref, wide_ref, spread_ref, outer_ref, quarters_ref, grads_ref,
    work_ref, land_refs, small_ref, part_ref, rows_ref, source_ref, first_sum_ref,
    first_land_ref, feat_ref, feat_land_ref, rows_send_ref, rows_land_ref, rim_send_ref, rim_land_ref,
    send_sem, recv_sem, side_send, side_recv, first_send, first_recv, fetch_sem,
):
    (
        slot_ref, counts_ref, rows_over_ref, part_over_ref, first_over_ref, tile_ref, lane_ref, weights_ref,
        biases_ref, partial_ref, own_ref,
    ) = late_refs
    edge, gate = lax.axis_index("edge"), lax.axis_index("gate")
    count = 1 << digits
    half_width, node_count = grad_ref.shape
    main = tiles_ref.shape[0]
    padded = states_ref.shape[1]
    chunk_count = tile_ref.shape[0]
    over = part_over_ref.shape[0] // 16
    slots = source_ref.shape[0]
    border = slots - node_count
    width = grads_ref.shape[1]
    partner = (edge, 1 - gate)
    before = (lax.rem(edge + count - 1, count), gate)
    after = (lax.rem(edge + 1, count), gate)
    peers = [(edge ^ (1 << d), gate) for d in range(digits)]
    bits = [lax.rem(lax.shift_right_logical(edge, d), 2) for d in range(digits)]
    greeted = peers + [partner, before, after]
    barrier = pltpu.get_barrier_semaphore()
    for peer in greeted:
        pl.semaphore_signal(barrier, inc=1, device_id=peer, device_id_type=pl.DeviceIdType.MESH)

    unit = LANES << (digits - 3)
    plan, small_order = chunk_plan(width // unit, digits)
    chunks = [
        (grads_ref, start * unit, start * unit, size * unit, order, group) for start, size, order, group in plan
    ]
    parts = chunks[-1][5] + 1
    chunks.append((small_ref, 0, width, small_ref.shape[1], small_order, parts - 1))
    members = [[c for c in range(len(chunks)) if chunks[c][5] == g] for g in range(parts)]
    spans = []
    for g in range(parts):
        ours = [chunks[c] for c in members[g] if chunks[c][0] is grads_ref]
        spans.append((ours[0][2] // (2 * LANES), (ours[-1][2] + ours[-1][3]) // (2 * LANES)))

    fetch_over = pltpu.make_async_copy(grads_over_hbm, grads_over_ref, fetch_sem.at[1])
    fetch_table = pltpu.make_async_copy(table_hbm, table_ref, fetch_sem.at[2])
    fetch_over.start()
    fetch_late = [
        pltpu.make_async_copy(source, target, late_sem.at[i])
        for i, (source, target) in enumerate(zip(late_hbms, late_refs))
    ]
    for fetch in fetch_late:
        fetch.start()
    fetch_table.start()

    def side(index, source, target, device):
        return pltpu.make_async_remote_copy(
            source, target, side_send.at[index], side_recv.at[index], device_id=device, device_id_type=pl.DeviceIdType.MESH
        )

    regions = []
    for _, _, place, lanes, order, _ in chunks:
        row, rows, lane = 0, 128, place
        levels = [(row, rows, lane, lanes)]
        for i, d in enumerate(order):
            if i < 3:
                rows //= 2
                row = row + bits[d] * rows
            else:
                lanes //= 2
                lane = lane + bits[d] * lanes
            levels.append((row, rows, lane, lanes))
        regions.append(levels)

    def window(row, rows, lane, lanes):
        if not isinstance(row, int):
            row = pl.multiple_of(row, 16)
        if not isinstance(lane, int):
            lane = pl.multiple_of(lane, LANES)
        return (pl.ds(row, rows), pl.ds(lane, lanes))

    def sibling(c, i):
        row, rows, lane, lanes = regions[c][i]
        d = chunks[c][4][i]
        if i < 3:
            return (row + (1 - bits[d]) * (rows // 2), rows // 2, lane, lanes)
        return (row, rows, lane + (1 - bits[d]) * (lanes // 2), lanes // 2)

    def landing(c, i):
        _, rows, _, lanes = regions[c][i + 1]
        return land_refs[i].at[pl.ds(0, rows), pl.ds(chunks[c][2] >> max(0, i - 2), lanes)]

    def inside(c, window_):
        source, at, place = chunks[c][:3]
        row, rows, lane, lanes = window_
        return source, window(row, rows, lane - place + at, lanes)

    def total_at(c, window_):
        row, rows, lane, lanes = window_
        if chunks[c][0] is small_ref:
            return small_total_ref, window(row, rows, lane - width, lanes)
        return total_ref, window(row, rows, lane, lanes)

    def scatter(c, i):
        if i == 0:
            source, at = inside(c, sibling(c, i))
            source = source.at[at]
        else:
            source = work_ref.at[window(*sibling(c, i))]
        return pltpu.make_async_remote_copy(
            source, landing(c, i), send_sem.at[c, i], recv_sem.at[c, i],
            device_id=peers[chunks[c][4][i]], device_id_type=pl.DeviceIdType.MESH,
        )

    def gather(c, i):
        ref, at = total_at(c, regions[c][i + 1])
        return pltpu.make_async_remote_copy(
            ref.at[at], ref.at[at], send_sem.at[c, 2 * digits - 1 - i], recv_sem.at[c, 2 * digits - 1 - i],
            device_id=peers[chunks[c][4][i]], device_id_type=pl.DeviceIdType.MESH,
        )

    def start(c, phase):
        if phase < digits:
            scatter(c, phase).start()
        elif phase < 2 * digits:
            gather(c, 2 * digits - 1 - phase).start()

    def arrive(c, phase):
        if phase < digits:
            scatter(c, phase).wait_recv()
            kept = regions[c][phase + 1]
            if phase == 0:
                source, at = inside(c, kept)
            else:
                source, at = work_ref, window(*kept)
            landed = landing(c, phase)
            value = source[at].astype(F32) + landed[...].astype(F32)
            if phase == digits - 1:
                target, at = total_at(c, kept)
            else:
                target, at = work_ref, window(*kept)
            target[at] = value.astype(BF16)
        else:
            gather(c, 2 * digits - 1 - phase).wait_recv()

    wide_ref[...] = widened(grad_ref)
    states = jnp.concatenate([states_ref[a, meta_ref[0, t]] for a in range(2) for t in range(main)], axis=0).astype(BF16)

    def pair_grads(p, first_pair):
        quarters = split_pair(outer_ref[:, pl.ds(aligned(p - first_pair, 16), 16), :])
        cols = pl.ds(aligned(p, 2 * LANES), 2 * LANES)
        quarters_ref[p] = quarters
        product = dot(quarters, states, TN)
        product = jnp.concatenate([product[:LANES], product[LANES:]], axis=1)
        grads_ref[:, cols] = (product + grads_over_ref[:, cols].astype(F32)).astype(BF16)

    def pair_rows(first, last):
        if first == 0:
            rows_ref[...] = jnp.zeros_like(rows_ref)

        def pair(p):
            weight = weight_ref[:, pl.ds(aligned(first + p, 2 * LANES), 2 * LANES)]
            weight = jnp.concatenate([weight[:, :LANES], weight[:, LANES:]], axis=0)
            rows_ref[...] += dot(quarters_ref[first + p], weight)

        tile_loop(last - first, pair, UNROLL_ROWS)

    def span_outer(g):
        first, last = spans[g]
        rows = pl.ds(first * 16, (last - first) * 16)

        def spread(t):
            _, _, within = tile_masks(tiles_ref[t, 17:18, :].astype(F32))
            spread_ref[t, rows, :] = keep_within(dot(wide_ref[rows, :], target_ref[t]), within)

        def outer(t):
            outer_ref[t, : (last - first) * 16, :] = dot(spread_ref[t, rows, :], hidden_ref[t], NT).astype(BF16)

        tile_loop(main, spread, UNROLL_SPAN)
        tile_loop(main, outer, UNROLL_SPAN)

    settled = {}

    def settle():
        if not settled:
            for fetch in fetch_late:
                fetch.wait()
            settled["first"] = extended_first(first_ref, first_bias_ref)
            settled["sums"] = dot(counts_ref[...], grad_ref[...], NT).astype(BF16)

    def fill_small():
        settle()
        small_ref[...] = jnp.zeros_like(small_ref)
        small_ref[:half_width, :LANES] = dot(settled["sums"], group_states(states_ref), TN).astype(BF16)
        small_ref[half_width + ROWS : half_width + ROWS + 16, : biases_ref.shape[1]] = jnp.concatenate(
            [biases_ref[...], jnp.zeros_like(biases_ref)], axis=0
        ).astype(BF16)
        small_ref[:, LANES : 4 * LANES] = weights_ref[...]

    def chunk_grads(c):
        if chunks[c][0] is grads_ref:
            first = chunks[c][2] // (2 * LANES)
            tile_loop(
                chunks[c][3] // (2 * LANES), lambda p: pair_grads(first + p, spans[chunks[c][5]][0]), UNROLL_PAIRS
            )
        else:
            fill_small()
        start(c, 0)

    span_outer(0)
    fetch_over.wait()
    pl.semaphore_wait(barrier, len(greeted))

    rows_copy = side(1, rows_send_ref, rows_land_ref, partner)
    rim_copy = side(2, rim_send_ref, rim_land_ref, before)
    feat_copy = side(3, feat_ref, feat_land_ref, partner)
    state_store = pltpu.make_async_copy(state_out_ref, state_hbm, late_sem.at[0])
    first_store = pltpu.make_async_copy(first_sum_ref, first_hbm, late_sem.at[1])
    feat_store = pltpu.make_async_copy(feat_out_ref, feat_hbm, late_sem.at[2])

    def source_rows():
        settle()
        rows = slot_ref[0:1, : 2 * main * HALF].astype(jnp.int32)
        hot = (iota((slots, 2 * main * HALF), 0) == rows).astype(F32).astype(BF16)
        source_ref[...] = dot(hot, rows_ref[...].astype(BF16)) + rows_over_ref[:slots, :]
        bias = dot(settled["sums"], second_bias_ref[...])
        for g in range(padded):
            for a in range(2):
                at = g * GROUP + a * HALF
                size = min(HALF, GROUP - a * HALF, slots - at)
                if size > 0:
                    source_ref[at : at + size, :] += bias[(a * padded + g) * HALF : (a * padded + g) * HALF + size]
        source_ref[border:, :] += partial_ref[...].T
        rows_send_ref[...] = source_ref[...].astype(BF16)
        rows_copy.start()

    def rim_rows():
        rows_copy.wait()
        source_ref[...] += rows_land_ref[...].astype(F32)
        rim_send_ref[...] = source_ref[:border, :].astype(BF16)
        rim_copy.start()

    def state_rows():
        rim_copy.wait()
        source_ref[slots - border :, :] += rim_land_ref[...].astype(F32)
        rows = source_ref[border:, :].T
        state_out_ref[...] = jnp.where(gate == 0, rows[:half_width], rows[half_width:]) + own_ref[...]
        state_store.start()

    table_ready = []

    def tile_grads(first, last):
        settle()
        if not table_ready:
            fetch_table.wait()
            table_ready.append(True)
            first_sum_ref[...] = first_over_ref[...]
            part_ref[main * 16 :, :] = part_over_ref[...]

        def tile(t):
            t = first + t
            held = tiles_ref[t]
            pre = dot(settled["first"], held, TN)
            logistic = jax.nn.sigmoid(pre)
            slope = logistic * (1.0 + pre * (1.0 - logistic))
            table = table_ref[meta_ref[0, t]]
            part, first_grad = hidden_slopes(held, table, spread_ref[t], slope, first_ref[...])
            part_ref[pl.ds(aligned(t, 16), 16), :] = part
            first_sum_ref[...] += first_grad

        tile_loop(last - first, tile, UNROLL_TILES)

    def first_copy(i):
        device = partner if i == 0 else peers[i - 1]
        return pltpu.make_async_remote_copy(
            first_land_ref.at[2 * i], first_land_ref.at[2 * i + 1], first_send.at[i], first_recv.at[i],
            device_id=device, device_id_type=pl.DeviceIdType.MESH,
        )

    def first_step(i):
        if i > 0:
            first_copy(i - 1).wait()
            first_sum_ref[...] = first_land_ref[2 * i - 2] + first_land_ref[2 * i - 1]
        if i <= digits:
            first_land_ref[2 * i] = first_sum_ref[...]
            first_copy(i).start()
        else:
            first_store.start()

    def back(first, last):
        def chunk(c):
            c = first + c
            cols = pl.ds(aligned(c, LANES), LANES)
            lane = lane_ref[pl.ds(c, 1), :].astype(jnp.int32)
            hot = (iota((TILE, LANES), 0) == lane).astype(F32).astype(BF16)
            moved = dot(part_ref[...], hot)
            tile = tile_ref[pl.ds(c, 1), :]
            total = jnp.zeros((16, LANES), F32)
            for t in range(main + over):
                total = total + jnp.where(tile == float(t), moved[t * 16 : (t + 1) * 16], 0.0)
            feat_ref[:, cols] = total

        tile_loop(last - first, chunk, UNROLL_BACK)
        if last == chunk_count:
            feat_copy.start()

    def feat_total():
        feat_copy.wait()
        feat_out_ref[...] = feat_ref[...] + feat_land_ref[...]
        feat_store.start()

    batch = TILE_BATCH
    tile_batches = range(0, main, batch)
    back_batches = range(0, chunk_count, 8)
    row_batches = range(0, half_width // 2, 8)
    done = [0] * len(chunks)

    def go(c):
        arrive(c, done[c])
        start(c, done[c] + 1)
        done[c] += 1

    actions = {
        "span": span_outer,
        "chunk": chunk_grads,
        "go": go,
        "tiles": lambda i: tile_grads(tile_batches[i], min(tile_batches[i] + batch, main)),
        "first": first_step,
        "rows": lambda i: pair_rows(row_batches[i], row_batches[i] + 8),
        "back": lambda i: back(back_batches[i], min(back_batches[i] + 8, chunk_count)),
        "sources": lambda i: source_rows(),
        "rim": lambda i: rim_rows(),
        "state": lambda i: state_rows(),
        "feat": lambda i: feat_total(),
    }
    for name, i in event_order(members, digits, len(tile_batches), len(back_batches), len(row_batches)):
        actions[name](i)

    for c in range(len(chunks)):
        for phase in range(2 * digits):
            if phase < digits:
                scatter(c, phase).wait_send()
            else:
                gather(c, 2 * digits - 1 - phase).wait_send()
    for copy in (state_store, first_store, feat_store):
        copy.wait()


def emit_kernel(
    total_ref, small_ref, first_in_ref, new_in_ref, state_in_ref, feat_in_ref,
    new_ref, state_ref, feat_ref, first_ref, first_bias_ref, second_out, second_bias_ref, input_ref, hidden_ref,
    input_bias_ref, hidden_bias_ref,
    wide_ref, sems,
):
    blocks = sems.shape[0]
    size = wide_ref.shape[1] // blocks
    writes = []
    for i in range(blocks):
        cols = pl.ds(i * size, size)
        wide_ref[:, cols] = total_ref[:, cols].astype(F32)
        writes.append(pltpu.make_async_copy(wide_ref.at[:, cols], second_out.at[:, cols], sems.at[i]))
        writes[i].start()
    new_ref[...] = new_in_ref[...]
    state_ref[...] = state_in_ref[...]
    feat_ref[...] = feat_in_ref[...]
    small = small_ref[:, : 4 * LANES].astype(F32)
    half = second_bias_ref.shape[0]
    second_bias_ref[...] = small[:half, :LANES]
    first_ref[...] = first_in_ref[:16]
    first_bias_ref[...] = first_in_ref[18:19]
    part = input_ref.shape[1]
    at = half + ROWS
    input_bias_ref[...] = small[at : at + 3, :part]
    hidden_bias_ref[...] = small[at + 3 : at + 6, :part]
    for k in range(3):
        input_ref[k] = small[:part, LANES + k * LANES : LANES + (k + 1) * LANES]
        hidden_ref[k] = small[part:, LANES + k * LANES : LANES + (k + 1) * LANES]
    for copy in writes:
        copy.wait()


def per_device(
    node_state, edge_feat, source, target, edge_mask, node_mask, net_first, net_first_bias, net_second,
    net_second_bias, gru_input, gru_hidden, gru_input_bias, gru_hidden_bias, cotangent,
):
    node_count, half_width = node_state.shape
    edge_count = source.shape[0]
    width = 2 * half_width
    chunks = edge_count // LANES
    slots = BORDER + node_count
    groups = -(-slots // GROUP)
    padded = (groups + 1) // 2 * 2
    over = groups + edge_count // TILE - 1 - MAIN
    first_bias = net_first_bias.reshape(1, width)
    second_bias = net_second_bias.reshape(half_width, width)
    shape = jax.ShapeDtypeStruct
    vmem = pl.BlockSpec(memory_space=pltpu.VMEM)
    smem = pl.BlockSpec(memory_space=pltpu.SMEM)
    hbm = pl.BlockSpec(memory_space=pl.ANY)

    def local(mib):
        return pltpu.CompilerParams(vmem_limit_bytes=mib * MIB)

    def remote(collective_id, mib):
        return pltpu.CompilerParams(vmem_limit_bytes=mib * MIB, collective_id=collective_id, has_side_effects=True)

    state_t = node_state.T
    operands = in_hbm(
        source.reshape(chunks, LANES), target.reshape(chunks, LANES), edge_mask.reshape(chunks, LANES), edge_feat, state_t
    )
    body, specs, scratch = fetched(place_kernel, operands)
    weights = in_hbm(net_second, second_bias, net_first, first_bias)
    second_near, second_bias_near, first_near, first_bias_near, full_t, states, placed, values, tile_rows, lane_rows, meta, slot_rows = pl.pallas_call(
        body,
        out_shape=tuple(shape(x.shape, x.dtype) for x in weights)
        + (
            shape((width, node_count), BF16),
            shape((2, padded, HALF, width), F32),
            shape((MAIN, ROWS, TILE), BF16),
            shape((ROWS, edge_count), BF16),
            shape((chunks, LANES), F32),
            shape((chunks, LANES), F32),
            shape((8, LANES), jnp.int32),
            shape((8, -(-2 * MAIN * HALF // LANES) * LANES), F32),
        ),
        in_specs=specs + [hbm] * 4,
        out_specs=(vmem,) * 12,
        scratch_shapes=[
            pltpu.VMEM((chunks * ROWS, LANES), BF16),
            pltpu.VMEM((MAIN * ROWS, edge_count), BF16),
            pltpu.VMEM((TILE, edge_count), BF16),
            pltpu.VMEM((half_width, node_count), BF16),
            pltpu.VMEM((2, half_width, LANES), BF16),
            pltpu.SemaphoreType.DMA((3,)),
            pltpu.SemaphoreType.DMA((3,)),
            pltpu.SemaphoreType.DMA((4,)),
        ]
        + scratch,
        compiler_params=remote(0, 20),
        name="place_edges",
    )(*operands, *weights)

    blank_shapes = (
        pltpu.HBM((width, half_width * width), BF16),
        pltpu.HBM((padded * GROUP + 16, width), F32),
        pltpu.HBM((over * 16, TILE), BF16),
        pltpu.HBM((ROWS, width), F32),
    )
    incoming, over_tiles, counts, table, hidden, targets, *blanks = pl.pallas_call(
        forward_kernel,
        out_shape=(
            shape((half_width, node_count), BF16),
            pltpu.HBM((over, ROWS, TILE), BF16),
            shape((2 * padded * HALF, node_count), BF16),
            pltpu.HBM((padded, half_width * HALF, 2 * width), BF16),
            shape((MAIN, 2 * width, TILE), BF16),
            shape((MAIN, node_count, TILE), BF16),
        )
        + blank_shapes,
        in_specs=[vmem] * 4 + [smem, vmem] + [hbm] * 3 + [vmem],
        out_specs=(vmem, hbm, vmem, hbm, vmem, vmem) + (hbm,) * 4,
        scratch_shapes=[
            pltpu.VMEM((padded, 16, node_count), F32),
            pltpu.VMEM((padded, half_width * HALF, 2 * width), BF16),
            pltpu.VMEM((2 * width, TILE), BF16),
            pltpu.VMEM((node_count, TILE), BF16),
            pltpu.VMEM((TILE, edge_count), BF16),
            pltpu.VMEM((half_width * HALF, node_count), F32),
            pltpu.VMEM((max(width, over * 16), half_width * width), BF16),
            pltpu.VMEM((padded * GROUP + 16, width), F32),
            pltpu.VMEM((ROWS, edge_count), BF16),
            pltpu.VMEM((chunks, LANES), F32),
            pltpu.VMEM((chunks, LANES), F32),
            pltpu.VMEM((ROWS, TILE), BF16),
            pltpu.SemaphoreType.DMA((3,)),
            pltpu.SemaphoreType.DMA((4,)),
        ],
        compiler_params=local(28),
        name="forward_edges",
    )(first_near, first_bias_near, second_bias_near, second_near, meta, placed, values, tile_rows, lane_rows, states)

    operands = in_hbm(
        state_t, node_mask.reshape(node_count // LANES, LANES), gru_input.swapaxes(1, 2), gru_hidden.swapaxes(1, 2),
        gru_input_bias, gru_hidden_bias, cotangent.T
    )
    body, specs, scratch = fetched(node_kernel, operands)
    message_grad, new_state, grad_own, state_partial, weight_grads, bias_grads = pl.pallas_call(
        body,
        out_shape=(
            shape((half_width, node_count), BF16),
            shape((half_width, node_count), BF16),
            shape((half_width, node_count), F32),
            shape((width, node_count), F32),
            shape((width, 3 * width), BF16),
            shape((8, half_width), F32),
        ),
        in_specs=specs + [vmem] * 2,
        out_specs=(vmem,) * 6,
        scratch_shapes=[
            pltpu.VMEM((half_width, node_count), BF16),
            pltpu.VMEM((width, node_count), F32),
            pltpu.VMEM((half_width, node_count), F32),
            pltpu.SemaphoreType.DMA((2,)),
            pltpu.SemaphoreType.DMA((2,)),
        ]
        + scratch,
        compiler_params=remote(1, 6),
        name="node_update",
    )(*operands, incoming, full_t)

    grads_over, rows_over, part_over, first_over = pl.pallas_call(
        overflow_kernel,
        out_shape=blank_shapes,
        in_specs=[smem, hbm, hbm, hbm, hbm, hbm, hbm] + [hbm] * 5,
        out_specs=(hbm,) * 4,
        scratch_shapes=[
            pltpu.VMEM((half_width, node_count), BF16),
            pltpu.VMEM((16, width), BF16),
            pltpu.VMEM((1, width), BF16),
            pltpu.VMEM((ROWS, TILE), BF16),
            pltpu.VMEM((2, padded, HALF, width), F32),
            pltpu.VMEM((padded * GROUP + 16, width), F32),
            pltpu.VMEM((over * 16, TILE), BF16),
            pltpu.VMEM((ROWS, width), F32),
            pltpu.VMEM((width, half_width * width), F32),
            pltpu.VMEM((width, half_width * width), BF16),
            pltpu.VMEM((1, half_width * HALF, 2 * width), BF16),
            pltpu.VMEM((half_width * HALF, 2 * width), BF16),
            pltpu.SemaphoreType.DMA,
        ],
        input_output_aliases={8 + i: i for i in range(4)},
        compiler_params=local(16),
        name="overflow_edges",
    )(meta, message_grad, *in_hbm(net_first, first_bias), *in_hbm(over_tiles, table), states, *in_hbm(net_second, *blanks))

    digits = (lax.axis_size("edge") - 1).bit_length()
    unit = LANES << (digits - 3)
    columns = half_width * width
    small_width = max(4 * LANES, unit)
    steps = min(columns // unit, len(SIZES)) + 1
    whole = columns + small_width
    plan, _ = chunk_plan(columns // unit, digits)
    span = max(sum(p[1] for p in plan if p[3] == g) for g in range(2)) * unit // (2 * LANES)
    late = (
        slot_rows, counts, *in_hbm(rows_over, part_over, first_over), tile_rows, lane_rows, weight_grads, bias_grads,
        state_partial, grad_own,
    )
    total, small_total, grad_feat, grad_state, first_sum = pl.pallas_call(
        functools.partial(finish_kernel, digits),
        out_shape=(
            pltpu.VMEM((width, columns), BF16),
            pltpu.VMEM((width, small_width), BF16),
            shape((16, edge_count), F32),
            shape((half_width, node_count), F32),
            shape((ROWS, width), F32),
        ),
        in_specs=[vmem] * 4 + [smem] + [vmem] * 5 + [hbm] * 13,
        out_specs=(vmem, vmem, hbm, hbm, hbm),
        scratch_shapes=[
            [pltpu.VMEM(x.shape, x.dtype) for x in late],
            pltpu.SemaphoreType.DMA((len(late),)),
            pltpu.VMEM((16, edge_count), F32),
            pltpu.VMEM((half_width, node_count), F32),
            pltpu.VMEM((padded, half_width * HALF, 2 * width), BF16),
            pltpu.VMEM((width, columns), BF16),
            pltpu.VMEM((half_width * HALF, node_count), BF16),
            pltpu.VMEM((MAIN, half_width * HALF, TILE), BF16),
            pltpu.VMEM((MAIN, 16 * span, 2 * width), BF16),
            pltpu.VMEM((half_width // 2, 2 * MAIN * HALF, 2 * width), BF16),
            pltpu.VMEM((width, columns), BF16),
            pltpu.VMEM((width, whole), BF16),
            [pltpu.VMEM((max(16, width >> (i + 1)), whole >> max(0, i - 2)), BF16) for i in range(digits)],
            pltpu.VMEM((width, small_width), BF16),
            pltpu.VMEM(((MAIN + over) * 16, TILE), BF16),
            pltpu.VMEM((2 * MAIN * HALF, width), F32),
            pltpu.VMEM((slots, width), F32),
            pltpu.VMEM((ROWS, width), F32),
            pltpu.VMEM((2 * digits + 2, ROWS, width), F32),
            pltpu.VMEM((16, edge_count), F32),
            pltpu.VMEM((16, edge_count), F32),
            pltpu.VMEM((slots, width), BF16),
            pltpu.VMEM((slots, width), BF16),
            pltpu.VMEM((BORDER, width), BF16),
            pltpu.VMEM((BORDER, width), BF16),
            pltpu.SemaphoreType.DMA((steps, 2 * digits)),
            pltpu.SemaphoreType.DMA((steps, 2 * digits)),
            pltpu.SemaphoreType.DMA((4,)),
            pltpu.SemaphoreType.DMA((4,)),
            pltpu.SemaphoreType.DMA((digits + 1,)),
            pltpu.SemaphoreType.DMA((digits + 1,)),
            pltpu.SemaphoreType.DMA((3,)),
        ],
        compiler_params=remote(2, 38),
        name="finish_sums",
    )(
        first_near, first_bias_near, second_bias_near, second_near, meta, message_grad, states, placed, hidden, targets,
        *in_hbm(table, grads_over), *late,
    )

    blocks = 8
    outs = pl.pallas_call(
        emit_kernel,
        out_shape=(
            shape((half_width, node_count), BF16),
            shape((half_width, node_count), F32),
            shape((16, edge_count), F32),
            shape((16, width), F32),
            shape((1, width), F32),
            shape((width, columns), F32),
            shape((half_width, width), F32),
            shape((3, half_width, width), F32),
            shape((3, half_width, width), F32),
            shape((3, half_width), F32),
            shape((3, half_width), F32),
        ),
        in_specs=[vmem] * 6,
        out_specs=(vmem,) * 5 + (hbm,) + (vmem,) * 5,
        scratch_shapes=[
            pltpu.VMEM((width, columns), F32),
            pltpu.SemaphoreType.DMA((blocks,)),
        ],
        compiler_params=local(12),
        name="emit",
    )(total, small_total, first_sum, new_state, grad_state, grad_feat)
    outs = list(outs)
    outs[0], outs[1] = outs[0].T, outs[1].T
    outs[7], outs[8] = outs[7].swapaxes(1, 2), outs[8].swapaxes(1, 2)
    outs[4] = outs[4].reshape(width)
    outs[6] = outs[6].reshape(columns)
    return tuple(outs)


def solution(mesh):
    return jax.shard_map(
        per_device,
        mesh=mesh,
        in_specs=(
            P("edge", "gate"), P(None, "edge"), P("edge"), P("edge"), P("edge"), P("edge"), P(), P(), P(None, "gate"),
            P("gate"), P(None, None, "gate"), P(None, None, "gate"), P(None, "gate"), P(None, "gate"), P("edge", "gate"),
        ),
        out_specs=(
            P("edge", "gate"), P("edge", "gate"), P(None, "edge"), P(), P(), P(None, "gate"), P("gate"),
            P(None, None, "gate"), P(None, None, "gate"), P(None, "gate"), P(None, "gate"),
        ),
        check_vma=False,
    )
```

```python
import functools

import jax
import jax.numpy as jnp
from jax import lax
from jax.experimental import pallas as pl
from jax.experimental.pallas import tpu as pltpu
from jax.sharding import PartitionSpec as P

BORDER = 64
GROUP = 14
HALF = 8
TILE = 256
MAIN = 26
UNROLL_ROWS = 8
UNROLL_PAIRS = 99
UNROLL_SPAN = 26
UNROLL_TILES = 3
TILE_BATCH = 3
LANES = 128
ROWS = 32
MIB = 1024 * 1024

KINDS = ("span", "chunk", "go", "tiles", "first", "back", "sources", "rim", "state", "feat", "rows")
SIZES = (4, 7, 6, 5, 5, 5)
ORDERS = ((0, 2, 1), (1, 2, 0), (2, 1, 0), (2, 1, 0), (0, 1, 2), (0, 1, 2), (1, 0, 2))
FIRST_SPAN = 3
SCHEDULE = (
    17, 18, 16, 1, 20, 22, 19, 21, 32, 34, 56, 33, 55, 36, 54, 34, 50, 32, 35, 38, 36, 51, 34, 37, 33, 32, 160, 36,
    49, 38, 34, 33, 35, 37, 32, 36, 52, 38, 48, 35, 37, 161, 33, 32, 36, 38, 53, 64, 34, 35, 37, 32, 65, 33, 36, 162,
    163, 34, 35, 38, 37, 66, 33, 32, 81, 35, 38, 67, 36, 37, 34, 96, 33, 32, 80, 68, 35, 38, 37, 112, 82, 83, 69,
    128, 36, 33, 34, 144, 37, 35, 38,
)

NN = ((1,), (0,))
NT = ((1,), (1,))
TN = ((0,), (0,))
F32 = jnp.float32
BF16 = jnp.bfloat16


def dot(left, right, dims=NN):
    return lax.dot_general(left, right, (dims, ((), ())), preferred_element_type=F32)


def iota(shape, dim):
    return lax.broadcasted_iota(jnp.int32, shape, dim)


def extended_first(first_ref, bias_ref):
    extra = jnp.where(iota((ROWS - 16, LANES), 0) == 2, bias_ref[...].astype(F32), 0.0)
    return jnp.concatenate([first_ref[...].astype(F32), extra], axis=0).astype(BF16)


def tile_masks(slot_row):
    place = slot_row.astype(jnp.int32) - 1
    low = jnp.logical_and(place >= 0, place < HALF)
    high = place >= HALF
    within = jnp.where(high, place - HALF, place)
    return low, high, within


def halves(hidden, low, high):
    return jnp.concatenate(
        [jnp.where(low, hidden, 0.0), jnp.where(high, hidden, 0.0)], axis=0
    ).astype(BF16)


def keep_within(values, within):
    rows, width = values.shape
    match = iota((HALF, width), 0) == within
    kept = jnp.where(match[None], values.reshape(rows // HALF, HALF, width), 0.0)
    return kept.reshape(rows, width).astype(BF16)


def target_hot(target_row, node_count):
    width = target_row.shape[1]
    return (iota((node_count, width), 0) + 1 == target_row.astype(jnp.int32)).astype(F32).astype(BF16)


def lane_hot(lane_ref, out_ref):
    chunks = lane_ref.shape[0]
    for c in range(chunks):
        row = lane_ref[c : c + 1, :].astype(jnp.int32)
        out_ref[:, c * LANES : (c + 1) * LANES] = (
            (iota((TILE, LANES), 0) == row).astype(F32).astype(BF16)
        )


def aligned(index, unit):
    return index * unit if isinstance(index, int) else pl.multiple_of(index * unit, unit)


def tile_loop(count, body, step):
    def several(i, carry):
        for s in range(step):
            body(i * step + s)
        return carry

    whole = count // step if step < count else 0
    if whole:
        lax.fori_loop(0, whole, several, 0)
    for t in range(whole * step, count):
        body(t)


def fetched(kernel, operands):
    count = len(operands)

    def body(*refs):
        sources, others, targets, sem = refs[:count], refs[count : -count - 1], refs[-count - 1 : -1], refs[-1]
        copies = [pltpu.make_async_copy(sources[i], targets[i], sem.at[i]) for i in range(count)]
        for copy in copies:
            copy.start()

        def ready():
            for copy in copies:
                copy.wait()

        kernel(ready, *targets, *others)

    scratch = [pltpu.VMEM(x.shape, x.dtype) for x in operands] + [pltpu.SemaphoreType.DMA((count,))]
    return body, [pl.BlockSpec(memory_space=pl.ANY)] * count, scratch


def in_hbm(*arrays):
    return tuple(pltpu.with_memory_space_constraint(x, pltpu.HBM) for x in arrays)


def place_kernel(
    ready, source_ref, target_ref, mask_ref, feat_ref, state_ref, second_hbm, second_bias_hbm, first_hbm, first_bias_hbm,
    second_ref, second_bias_ref, first_ref, first_bias_ref, full_ref, states_ref, tiles_ref, values_ref, tile_ref, lane_ref, meta_ref, slot_ref,
    counts_ref, spread_ref, hot_ref, other_ref, rim_ref, send_sem, recv_sem, load_sem,
):
    chunks = source_ref.shape[0]
    half, node_count = state_ref.shape
    main = tiles_ref.shape[0]
    padded = states_ref.shape[1]
    groups = -(-(node_count + BORDER) // GROUP)
    edge, gate = lax.axis_index("edge"), lax.axis_index("gate")
    count = lax.axis_size("edge")
    first_node = edge * node_count
    partner = (edge, 1 - gate)
    after = lax.rem(edge + 1, count)
    before = lax.rem(edge + count - 1, count)
    mesh_signal(
        pltpu.get_barrier_semaphore(), [partner, (after, gate), (after, 1 - gate), (before, gate), (before, 1 - gate)]
    )

    def send(index, source, target, device):
        return pltpu.make_async_remote_copy(
            source, target, send_sem.at[index], recv_sem.at[index], device_id=device, device_id_type=pl.DeviceIdType.MESH
        )

    loads = [
        pltpu.make_async_copy(far, near, load_sem.at[i])
        for i, (far, near) in enumerate(
            [(first_hbm, first_ref), (first_bias_hbm, first_bias_ref), (second_bias_hbm, second_bias_ref), (second_hbm, second_ref)]
        )
    ]
    ready()
    for load in loads:
        load.start()
    rim = state_ref.at[:, pl.ds(node_count - LANES, LANES)]
    copies = [
        send(0, rim, rim_ref.at[0], (after, gate)),
        send(1, rim, rim_ref.at[1], (after, 1 - gate)),
        send(2, state_ref, other_ref, partner),
    ]
    for copy in copies:
        copy.start()

    group_rows = []
    slot_rows = []
    for c in range(chunks):
        slot = (source_ref[c : c + 1, :] - first_node + BORDER).astype(F32)
        group = jnp.floor((slot + 0.5) * (1.0 / GROUP))
        slot_rows.append(slot)
        group_rows.append(group)
        counts_ref[c * ROWS : (c + 1) * ROWS, :] = (
            (iota((ROWS, LANES), 0).astype(F32) == group).astype(F32).astype(BF16)
        )
    above = jnp.where(
        iota((LANES, 2 * LANES), 0) < iota((LANES, 2 * LANES), 1), 1.0, 0.0
    ).astype(BF16)
    sums = dot(counts_ref[...], above)
    running = jnp.zeros((ROWS, LANES), F32)
    ranks = []
    for c in range(chunks):
        hot = counts_ref[c * ROWS : (c + 1) * ROWS, :].astype(F32)
        part = sums[c * ROWS : (c + 1) * ROWS]
        ranks.append(jnp.sum(hot * (part[:, :LANES] + running), axis=0, keepdims=True))
        running = running + part[:, LANES:]
    owned = jnp.floor((running + (TILE - 1.0)) * (1.0 / TILE))
    earlier = (iota((ROWS, ROWS), 1) < iota((ROWS, ROWS), 0)).astype(F32).astype(BF16)
    start = dot(earlier, owned.astype(BF16))
    end = start + owned
    total = jnp.sum(owned, axis=0, keepdims=True)

    def group_of(tile):
        return jnp.minimum(jnp.sum((end <= tile).astype(F32), axis=0, keepdims=True), groups - 1.0)

    row8 = iota((8, LANES), 0)
    lane = iota((1, LANES), 1).astype(F32)
    meta_ref[...] = jnp.where(row8 == 0, group_of(lane), jnp.where(row8 == 1, total, 0.0)).astype(jnp.int32)
    for c in range(slot_ref.shape[1] // LANES):
        row = lane + float(c * LANES)
        high = jnp.where(row >= main * HALF, 1.0, 0.0)
        row = row - high * (main * HALF)
        tile = jnp.floor((row + 0.5) * (1.0 / HALF))
        place = row - tile * HALF + high * HALF
        slot = group_of(tile) * GROUP + place
        slot = jnp.where(jnp.logical_and(place < GROUP, tile < jnp.minimum(total, float(main))), slot, -1.0)
        slot_ref[:, c * LANES : (c + 1) * LANES] = jnp.broadcast_to(slot, (8, LANES))

    row16 = iota((ROWS - 16, LANES), 0)
    for c in range(chunks):
        cols = slice(c * LANES, (c + 1) * LANES)
        hot = counts_ref[c * ROWS : (c + 1) * ROWS, :].astype(F32)
        over = jnp.floor(ranks[c] * (1.0 / TILE))
        tile = jnp.sum(hot * start, axis=0, keepdims=True) + over
        lane = ranks[c] - TILE * over
        tile_ref[c : c + 1, :] = tile
        lane_ref[c : c + 1, :] = lane
        hot_ref[:, cols] = (iota((TILE, LANES), 0).astype(F32) == lane).astype(F32).astype(BF16)
        place = slot_rows[c] - GROUP * group_rows[c] + 1.0
        target = jnp.where(
            mask_ref[c : c + 1, :] > 0, target_ref[c : c + 1, :] - first_node + 1, 0
        ).astype(F32)
        more = jnp.where(row16 == 0, target, jnp.where(row16 == 1, place, jnp.where(row16 == 2, 1.0, 0.0)))
        feats = feat_ref[:, cols].astype(F32)
        values_ref[:, cols] = jnp.concatenate([feats, more], axis=0).astype(BF16)
        for t in range(main):
            spread_ref[t * 16 : (t + 1) * 16, cols] = jnp.where(tile == float(t), feats, 0.0).astype(BF16)
        in_tile = iota((ROWS, LANES), 0).astype(F32) == tile
        for i, value in enumerate((target, place, 1.0)):
            at = main * 16 + i * ROWS
            spread_ref[at : at + ROWS, cols] = jnp.where(in_tile, value, 0.0).astype(BF16)
    moved = dot(spread_ref[...], hot_ref[...], NT)
    blank = jnp.zeros((13, TILE), F32)
    for t in range(main):
        tiles_ref[t, :16, :] = moved[t * 16 : (t + 1) * 16].astype(BF16)
        more = [moved[main * 16 + i * ROWS + t : main * 16 + i * ROWS + t + 1] for i in range(3)]
        tiles_ref[t, 16:, :] = jnp.concatenate(more + [blank], axis=0).astype(BF16)

    for copy in copies:
        copy.wait()
    is_first = gate == 0
    mine, other = state_ref[...], other_ref[...]
    full = jnp.concatenate([jnp.where(is_first, mine, other), jnp.where(is_first, other, mine)], axis=0)
    full_ref[...] = full
    own, swapped = rim_ref[0], rim_ref[1]
    rims = jnp.concatenate([jnp.where(is_first, own, swapped), jnp.where(is_first, swapped, own)], axis=0)
    rows = jnp.concatenate(
        [rims.astype(F32).T[LANES - BORDER :], full.astype(F32).T], axis=0
    )
    spare = padded * GROUP + 16 - rows.shape[0]
    rows = jnp.concatenate([rows, jnp.zeros((spare, 2 * half), F32)], axis=0)
    for load in loads:
        load.wait()
    for g in range(padded):
        for a in range(2):
            states_ref[a, g] = rows[g * GROUP + a * HALF : g * GROUP + (a + 1) * HALF]


def group_states(states_ref):
    _, padded, half, width = states_ref.shape
    return jnp.concatenate([states_ref[a].reshape(padded * half, width) for a in range(2)], axis=0).astype(BF16)


def group_counts(counts_ref):
    padded, _, node_count = counts_ref.shape
    return jnp.concatenate(
        [counts_ref[:, a * HALF : (a + 1) * HALF, :].reshape(padded * HALF, node_count) for a in range(2)], axis=0
    ).astype(BF16)


def forward_kernel(
    first_ref, first_bias_ref, second_bias_ref, second_ref, meta_ref, tiles_ref, values_hbm, tile_hbm, lane_hbm, states_ref,
    incoming_ref, over_hbm, counts_out_ref, table_out_ref, hidden_ref, targets_ref, *rest,
):
    blank_refs, rest = rest[:4], rest[4:]
    counts_ref, table_ref, hidden_over_ref, targets_over_ref, hot_ref, total_ref, narrow_ref, zeros_ref = rest[:8]
    values_ref, tile_ref, lane_ref, held_ref, sems, blank_sems = rest[8:]
    chunks = tile_ref.shape[0]
    half_width, node_count = incoming_ref.shape
    main = tiles_ref.shape[0]
    padded = table_ref.shape[0]
    over_total = jnp.maximum(meta_ref[1, 0] - main, 0)
    narrow_ref[...] = jnp.zeros_like(narrow_ref)
    zeros_ref[...] = jnp.zeros_like(zeros_ref)
    blanks = []
    for i, blank_ref in enumerate(blank_refs):
        rows, cols = blank_ref.shape
        zeros = narrow_ref if blank_ref.dtype == BF16 else zeros_ref
        blanks.append(pltpu.make_async_copy(zeros.at[pl.ds(0, rows), pl.ds(0, cols)], blank_ref, blank_sems.at[i]))
        blanks[i].start()
    first_t = extended_first(first_ref, first_bias_ref)

    def expand(held):
        low, high, _ = tile_masks(held[17:18, :].astype(F32))
        pre = dot(first_t, held, TN)
        return halves(pre * jax.nn.sigmoid(pre), low, high), target_hot(held[16:17, :].astype(F32), node_count)

    def expand_main(t):
        hidden_ref[t], targets_ref[t] = expand(tiles_ref[t])


    states = group_states(states_ref)

    def table_pair(p):
        pair = second_ref[:, pl.ds(pl.multiple_of(p * 2 * LANES, 2 * LANES), 2 * LANES)]
        both = jnp.concatenate([pair[:, :LANES], pair[:, LANES:]], axis=0)
        product = dot(states, both, NT).reshape(2, padded, HALF, 2 * LANES)
        for a in range(2):
            rows = jnp.concatenate([product[a, :, :, :LANES], product[a, :, :, LANES:]], axis=1)
            table_ref[:, pl.ds(pl.multiple_of(p * 16, 16), 16), a * LANES : (a + 1) * LANES] = rows.astype(BF16)

    pairs = half_width // 2
    shared = min(main, pairs) // 4 * 4

    def both(i):
        expand_main(i)
        table_pair(i)

    tile_loop(shared, both, shared // 2)
    for t in range(shared, main):
        expand_main(t)
    for p in range(shared, pairs):
        table_pair(p)
    keep = pltpu.make_async_copy(table_ref, table_out_ref, sems.at[1])
    keep.start()

    def messages(hidden, targets, group, held):
        _, _, within = tile_masks(held[17:18, :].astype(F32))
        message = keep_within(dot(table_ref[group], hidden), within)
        place = held[17:18, :].astype(jnp.int32) - 1
        places = (iota((16, TILE), 0) == place).astype(F32).astype(BF16)
        sums = dot(jnp.concatenate([message, places], axis=0), targets, NT)
        total_ref[...] += sums[: half_width * HALF]
        counts_ref[group] += sums[half_width * HALF :]

    total_ref[...] = jnp.zeros_like(total_ref)
    counts_ref[...] = jnp.zeros_like(counts_ref)
    tile_loop(main, lambda t: messages(hidden_ref[t], targets_ref[t], meta_ref[0, t], tiles_ref[t]), 13)

    @pl.when(over_total > 0)
    def _():
        for source, target in [(values_hbm, values_ref), (tile_hbm, tile_ref), (lane_hbm, lane_ref)]:
            load = pltpu.make_async_copy(source, target, sems.at[2])
            load.start()
            load.wait()
        lane_hot(lane_ref, hot_ref)

    def over_messages(u, carry):
        wanted = (main + u).astype(F32)
        pieces = []
        for c in range(chunks):
            values = values_ref[:, c * LANES : (c + 1) * LANES].astype(F32)
            pieces.append(jnp.where(tile_ref[c : c + 1, :] == wanted, values, 0.0).astype(BF16))
        held = dot(jnp.concatenate(pieces, axis=1), hot_ref[...], NT).astype(BF16)
        held_ref[...] = held
        save = pltpu.make_async_copy(held_ref, over_hbm.at[u], sems.at[2])
        save.start()
        save.wait()
        hidden_over_ref[...], targets_over_ref[...] = expand(held)
        messages(hidden_over_ref[...], targets_over_ref[...], meta_ref[0, main + u], held)
        return carry

    lax.fori_loop(0, over_total, over_messages, 0)
    bias = dot(second_bias_ref[...], states, NT)
    summed = jnp.sum(total_ref[...].reshape(half_width, HALF, node_count), axis=1)
    counts = group_counts(counts_ref)
    counts_out_ref[...] = counts
    incoming_ref[...] = (summed + dot(bias.astype(BF16), counts)).astype(BF16)
    keep.wait()
    for blank in blanks:
        blank.wait()


def expand_tile(held, first_t, wide, node_count):
    low, high, within = tile_masks(held[17:18, :].astype(F32))
    pre = dot(first_t, held, TN)
    logistic = jax.nn.sigmoid(pre)
    hidden = halves(pre * logistic, low, high)
    slope = logistic * (1.0 + pre * (1.0 - logistic))
    spread = keep_within(dot(wide, target_hot(held[16:17, :].astype(F32), node_count)), within)
    return hidden, slope, spread


def widened(grad_ref):
    half_width, node_count = grad_ref.shape
    wide = jnp.broadcast_to(grad_ref[...].astype(F32)[:, None, :], (half_width, HALF, node_count))
    return wide.reshape(half_width * HALF, node_count).astype(BF16)


def hidden_slopes(held, table, spread, slope, first):
    low, _, _ = tile_masks(held[17:18, :].astype(F32))
    grad_hidden = dot(table, spread, TN)
    grad_hidden = jnp.where(low, grad_hidden[:LANES], grad_hidden[LANES:])
    grad_pre = (grad_hidden * slope).astype(BF16)
    return dot(first, grad_pre).astype(BF16), dot(held, grad_pre, NT)


def split_pair(held):
    tiles = held.shape[0]
    held = held.astype(F32)
    parts = []
    for q in range(2):
        rows = held[:, q * HALF : (q + 1) * HALF, :].reshape(tiles * HALF, 2 * LANES).astype(BF16)
        parts.append(jnp.concatenate([rows[:, :LANES], rows[:, LANES:]], axis=0))
    return jnp.concatenate(parts, axis=1)


def overflow_kernel(
    meta_ref, grad_hbm, first_hbm, first_bias_hbm, over_hbm, table_hbm, states_hbm, second_hbm, tile_hbm, lane_hbm,
    _grads, _rows, _feat, _first,
    grads_hbm, rows_hbm, feat_hbm, first_grad_hbm,
    grad_ref, first_ref, first_bias_ref, over_ref, states_ref, rows_ref, part_ref, feat_ref, first_grad_ref,
    grads_ref, weight_ref, outer_ref, table_ref, tile_ref, lane_ref, sem,
):
    total = jnp.maximum(meta_ref[1, 0] - MAIN, 0)

    def move(source, target):
        copy = pltpu.make_async_copy(source, target, sem)
        copy.start()
        copy.wait()

    @pl.when(total > 0)
    def _():
        half_width, node_count = grad_ref.shape
        move(grad_hbm, grad_ref)
        move(first_hbm, first_ref)
        move(first_bias_hbm, first_bias_ref)
        move(states_hbm, states_ref)
        move(second_hbm, weight_ref)
        move(tile_hbm, tile_ref)
        move(lane_hbm, lane_ref)
        first_grad_ref[...] = jnp.zeros_like(first_grad_ref)
        part_ref[...] = jnp.zeros_like(part_ref)
        rows_ref[...] = jnp.zeros_like(rows_ref)
        grads_ref[...] = jnp.zeros_like(grads_ref)
        first_t = extended_first(first_ref, first_bias_ref)
        wide = widened(grad_ref)

        def tile_work(u, carry):
            group = meta_ref[0, MAIN + u]
            move(table_hbm.at[group], table_ref)
            move(over_hbm.at[u], over_ref)
            held = over_ref[...]
            hidden, slope, spread = expand_tile(held, first_t, wide, node_count)
            outer_ref[0] = dot(spread, hidden, NT).astype(BF16)
            part, first_grad = hidden_slopes(held, table_ref[...], spread, slope, first_ref[...])
            part_ref[pl.ds(pl.multiple_of(u * 16, 16), 16), :] = part
            first_grad_ref[...] += first_grad
            states = jnp.concatenate([states_ref[0, group], states_ref[1, group]], axis=0).astype(BF16)

            def pair_work(p, carry):
                cols = pl.ds(pl.multiple_of(p * 2 * LANES, 2 * LANES), 2 * LANES)
                quarters = split_pair(outer_ref[:, pl.ds(pl.multiple_of(p * 16, 16), 16), :])
                product = dot(quarters, states, TN)
                grads_ref[:, cols] += jnp.concatenate([product[:LANES], product[LANES:]], axis=1)
                pair = weight_ref[:, cols]
                return carry + dot(quarters, jnp.concatenate([pair[:, :LANES], pair[:, LANES:]], axis=0))

            rows = lax.fori_loop(0, half_width // 2, pair_work, jnp.zeros((2 * HALF, LANES), F32))
            at = group * GROUP
            rows_ref[pl.ds(at, HALF), :] += rows[:HALF]
            rows_ref[pl.ds(at + HALF, HALF), :] += rows[HALF:]
            return carry

        lax.fori_loop(0, total, tile_work, 0)
        weight_ref[...] = grads_ref[...].astype(BF16)
        move(weight_ref, grads_hbm)
        move(rows_ref, rows_hbm)
        for c in range(tile_ref.shape[0]):
            hot = (iota((TILE, LANES), 0) == lane_ref[c : c + 1, :].astype(jnp.int32)).astype(F32).astype(BF16)
            moved = dot(part_ref[...], hot)
            tile = tile_ref[c : c + 1, :]
            part = jnp.zeros((16, LANES), F32)
            for u in range(part_ref.shape[0] // 16):
                part = part + jnp.where(tile == float(MAIN + u), moved[u * 16 : (u + 1) * 16], 0.0)
            feat_ref[c * 16 : (c + 1) * 16, :] = part
        move(feat_ref, feat_hbm)
        move(first_grad_ref, first_grad_hbm)


def mesh_signal(sem, peers):
    for peer in peers:
        pl.semaphore_signal(sem, inc=1, device_id=peer, device_id_type=pl.DeviceIdType.MESH)
    pl.semaphore_wait(sem, len(peers))


def node_kernel(
    ready, state_ref, mask_ref, input_ref, hidden_ref, input_bias_ref, hidden_bias_ref, cotangent_ref, incoming_ref, full_ref,
    message_grad_ref, new_ref, own_ref, partial_ref, weights_ref, biases_ref,
    other_ref, onto_ref, back_ref, send_sem, recv_sem,
):
    edge, gate = lax.axis_index("edge"), lax.axis_index("gate")
    partner = (edge, 1 - gate)
    half = state_ref.shape[0]
    mesh_signal(pltpu.get_barrier_semaphore(), [partner])
    swap = pltpu.make_async_remote_copy(
        incoming_ref, other_ref, send_sem.at[0], recv_sem.at[0], device_id=partner, device_id_type=pl.DeviceIdType.MESH
    )
    swap.start()
    ready()
    full = full_ref[...]
    biases = jnp.concatenate(
        [input_bias_ref[...].astype(F32), hidden_bias_ref[...].astype(F32), jnp.zeros((2, half), F32)], axis=0
    ).T
    hidden_pre = [dot(hidden_ref[k], full) + biases[:, 3 + k : 4 + k] for k in range(3)]
    keep = jnp.concatenate([mask_ref[c : c + 1, :] for c in range(mask_ref.shape[0])], axis=1).astype(F32)
    own = state_ref[...].astype(F32)
    grad_output = cotangent_ref[...].astype(F32) * keep
    mine = incoming_ref[...]
    swap.wait()
    other = other_ref[...]
    is_first = gate == 0
    message = jnp.concatenate(
        [jnp.where(is_first, mine, other), jnp.where(is_first, other, mine)], axis=0
    )
    input_pre = [dot(input_ref[k], message) + biases[:, k : k + 1] for k in range(3)]
    reset = jax.nn.sigmoid(input_pre[0] + hidden_pre[0])
    update = jax.nn.sigmoid(input_pre[1] + hidden_pre[1])
    candidate = jnp.tanh(input_pre[2] + reset * hidden_pre[2])
    grad_cand = grad_output * (1.0 - update) * (1.0 - candidate * candidate)
    grad_update = grad_output * (own - candidate) * update * (1.0 - update)
    grad_reset = grad_cand * hidden_pre[2] * reset * (1.0 - reset)
    grad_input = [grad_reset.astype(BF16), grad_update.astype(BF16), grad_cand.astype(BF16)]
    grad_hidden = [grad_input[0], grad_input[1], (grad_cand * reset).astype(BF16)]
    onto_ref[...] = sum(dot(input_ref[k], grad_input[k], TN) for k in range(3))
    back = pltpu.make_async_remote_copy(
        onto_ref.at[pl.ds(pl.multiple_of((1 - gate) * half, half), half)], back_ref, send_sem.at[1], recv_sem.at[1],
        device_id=partner, device_id_type=pl.DeviceIdType.MESH,
    )
    back.start()
    new_ref[...] = (keep * ((1.0 - update) * candidate + update * own)).astype(BF16)
    own_ref[...] = grad_output * update
    partial_ref[...] = sum(dot(hidden_ref[k], grad_hidden[k], TN) for k in range(3))
    for k in range(3):
        weights_ref[:, k * LANES : (k + 1) * LANES] = jnp.concatenate(
            [dot(grad_input[k], message, NT), dot(grad_hidden[k], full, NT)], axis=0
        ).astype(BF16)
    lane = iota((half, LANES), 1)
    sums = jnp.zeros((half, LANES), F32)
    for k, grad in enumerate(grad_input + grad_hidden):
        sums = jnp.where(lane == k, jnp.sum(grad.astype(F32), axis=1, keepdims=True), sums)
    biases_ref[...] = sums.T[:8]
    back.wait()
    kept = onto_ref[pl.ds(pl.multiple_of(gate * half, half), half), :]
    message_grad_ref[...] = (kept + back_ref[...]).astype(BF16)


def chunk_plan(units, digits):
    orders = [list(order) + list(range(3, digits)) for order in ORDERS]
    count = len(SIZES)
    sizes = SIZES
    if units != sum(SIZES):
        count = min(units, count)
        sizes = [units // count + (1 if i < units % count else 0) for i in range(count)]
    plan = [(sum(sizes[:i]), sizes[i], orders[i], 0 if i < FIRST_SPAN else 1) for i in range(count)]
    return plan, orders[-1]


def event_order(members, digits, tiles, backs, rows):
    if digits == 4 and len(members) == 2:
        return [(KINDS[code // 16], code % 16) for code in SCHEDULE]
    parts = len(members)
    steps = [[] for _ in range(parts + 2 * digits + 4)]
    for g in range(parts):
        if g > 0:
            steps[g].append(("span", g))
        steps[g] += [("chunk", c) for c in members[g]]
        for phase in range(2 * digits):
            steps[g + phase + 1] += [("go", c) for c in members[g]]
    at = parts
    steps[at] += [("rows", i) for i in range(rows)]
    steps[at].append(("sources", 0))
    for i in range(tiles):
        steps[at + i // 2].append(("tiles", i))
    steps[at + 1].append(("rim", 0))
    steps[at + 3].append(("state", 0))
    at += (tiles + 1) // 2
    for i in range(digits + 2):
        steps[min(at + i, len(steps) - 1)].append(("first", i))
    for i in range(backs):
        steps[min(at + i, len(steps) - 1)].append(("back", i))
    steps[min(at + backs, len(steps) - 1)].append(("feat", 0))
    return [event for step in steps for event in step]


def finish_kernel(
    digits, first_ref, first_bias_ref, second_bias_ref, weight_ref, meta_ref, grad_ref, states_ref, tiles_ref, hidden_ref,
    target_ref, table_hbm, grads_over_hbm, *rest,
):
    late_hbms, rest = rest[:11], rest[11:]
    total_ref, small_total_ref, feat_hbm, state_hbm, first_hbm, late_refs, *rest = rest
    finish_body(
        digits, meta_ref, grad_ref, states_ref, first_ref, first_bias_ref, second_bias_ref, weight_ref, tiles_ref, hidden_ref,
        target_ref, table_hbm, grads_over_hbm, late_hbms, total_ref, small_total_ref, feat_hbm, state_hbm, first_hbm, late_refs, *rest,
    )


def finish_body(
    digits, meta_ref, grad_ref, states_ref, first_ref, first_bias_ref, second_bias_ref, weight_ref, tiles_ref, hidden_ref,
    target_ref, table_hbm, grads_over_hbm, late_hbms, total_ref, small_total_ref, feat_hbm, state_hbm, first_hbm, late_refs, late_sem,
    feat_out_ref, state_out_ref,
    table_ref, grads_over_ref, wide_ref, spread_ref, outer_ref, quarters_ref, grads_ref,
    work_ref, land_refs, small_ref, part_ref, rows_ref, source_ref, first_sum_ref,
    first_land_ref, feat_ref, feat_land_ref, rows_send_ref, rows_land_ref, rim_send_ref, rim_land_ref,
    send_sem, recv_sem, side_send, side_recv, first_send, first_recv, fetch_sem,
):
    (
        slot_ref, counts_ref, rows_over_ref, feat_over_ref, first_over_ref, tile_ref, lane_ref, weights_ref,
        biases_ref, partial_ref, own_ref,
    ) = late_refs
    edge, gate = lax.axis_index("edge"), lax.axis_index("gate")
    count = 1 << digits
    half_width, node_count = grad_ref.shape
    main = tiles_ref.shape[0]
    padded = states_ref.shape[1]
    chunk_count = tile_ref.shape[0]
    slots = source_ref.shape[0]
    border = slots - node_count
    width = grads_ref.shape[1]
    partner = (edge, 1 - gate)
    before = (lax.rem(edge + count - 1, count), gate)
    after = (lax.rem(edge + 1, count), gate)
    peers = [(edge ^ (1 << d), gate) for d in range(digits)]
    bits = [lax.rem(lax.shift_right_logical(edge, d), 2) for d in range(digits)]
    greeted = peers + [partner, before, after]
    barrier = pltpu.get_barrier_semaphore()
    for peer in greeted:
        pl.semaphore_signal(barrier, inc=1, device_id=peer, device_id_type=pl.DeviceIdType.MESH)

    unit = LANES << (digits - 3)
    plan, small_order = chunk_plan(width // unit, digits)
    chunks = [
        (grads_ref, start * unit, start * unit, size * unit, order, group) for start, size, order, group in plan
    ]
    parts = chunks[-1][5] + 1
    chunks.append((small_ref, 0, width, small_ref.shape[1], small_order, parts - 1))
    members = [[c for c in range(len(chunks)) if chunks[c][5] == g] for g in range(parts)]
    spans = []
    for g in range(parts):
        ours = [chunks[c] for c in members[g] if chunks[c][0] is grads_ref]
        spans.append((ours[0][2] // (2 * LANES), (ours[-1][2] + ours[-1][3]) // (2 * LANES)))

    fetch_over = pltpu.make_async_copy(grads_over_hbm, grads_over_ref, fetch_sem.at[1])
    fetch_table = pltpu.make_async_copy(table_hbm, table_ref, fetch_sem.at[2])
    fetch_over.start()
    fetch_late = [
        pltpu.make_async_copy(source, target, late_sem.at[i])
        for i, (source, target) in enumerate(zip(late_hbms, late_refs))
    ]
    for fetch in fetch_late:
        fetch.start()
    fetch_table.start()

    def side(index, source, target, device):
        return pltpu.make_async_remote_copy(
            source, target, side_send.at[index], side_recv.at[index], device_id=device, device_id_type=pl.DeviceIdType.MESH
        )

    regions = []
    for _, _, place, lanes, order, _ in chunks:
        row, rows, lane = 0, 128, place
        levels = [(row, rows, lane, lanes)]
        for i, d in enumerate(order):
            if i < 3:
                rows //= 2
                row = row + bits[d] * rows
            else:
                lanes //= 2
                lane = lane + bits[d] * lanes
            levels.append((row, rows, lane, lanes))
        regions.append(levels)

    def window(row, rows, lane, lanes):
        if not isinstance(row, int):
            row = pl.multiple_of(row, 16)
        if not isinstance(lane, int):
            lane = pl.multiple_of(lane, LANES)
        return (pl.ds(row, rows), pl.ds(lane, lanes))

    def sibling(c, i):
        row, rows, lane, lanes = regions[c][i]
        d = chunks[c][4][i]
        if i < 3:
            return (row + (1 - bits[d]) * (rows // 2), rows // 2, lane, lanes)
        return (row, rows, lane + (1 - bits[d]) * (lanes // 2), lanes // 2)

    def landing(c, i):
        _, rows, _, lanes = regions[c][i + 1]
        return land_refs[i].at[pl.ds(0, rows), pl.ds(chunks[c][2] >> max(0, i - 2), lanes)]

    def inside(c, window_):
        source, at, place = chunks[c][:3]
        row, rows, lane, lanes = window_
        return source, window(row, rows, lane - place + at, lanes)

    def total_at(c, window_):
        row, rows, lane, lanes = window_
        if chunks[c][0] is small_ref:
            return small_total_ref, window(row, rows, lane - width, lanes)
        return total_ref, window(row, rows, lane, lanes)

    def scatter(c, i):
        if i == 0:
            source, at = inside(c, sibling(c, i))
            source = source.at[at]
        else:
            source = work_ref.at[window(*sibling(c, i))]
        return pltpu.make_async_remote_copy(
            source, landing(c, i), send_sem.at[c, i], recv_sem.at[c, i],
            device_id=peers[chunks[c][4][i]], device_id_type=pl.DeviceIdType.MESH,
        )

    def gather(c, i):
        ref, at = total_at(c, regions[c][i + 1])
        return pltpu.make_async_remote_copy(
            ref.at[at], ref.at[at], send_sem.at[c, 2 * digits - 1 - i], recv_sem.at[c, 2 * digits - 1 - i],
            device_id=peers[chunks[c][4][i]], device_id_type=pl.DeviceIdType.MESH,
        )

    def start(c, phase):
        if phase < digits:
            scatter(c, phase).start()
        elif phase < 2 * digits:
            gather(c, 2 * digits - 1 - phase).start()

    def arrive(c, phase):
        if phase < digits:
            scatter(c, phase).wait_recv()
            kept = regions[c][phase + 1]
            if phase == 0:
                source, at = inside(c, kept)
            else:
                source, at = work_ref, window(*kept)
            landed = landing(c, phase)
            value = source[at].astype(F32) + landed[...].astype(F32)
            if phase == digits - 1:
                target, at = total_at(c, kept)
            else:
                target, at = work_ref, window(*kept)
            target[at] = value.astype(BF16)
        else:
            gather(c, 2 * digits - 1 - phase).wait_recv()

    wide_ref[...] = widened(grad_ref)
    states = jnp.concatenate([states_ref[a, meta_ref[0, t]] for a in range(2) for t in range(main)], axis=0).astype(BF16)

    def pair_grads(p, first_pair):
        quarters = split_pair(outer_ref[:, pl.ds(aligned(p - first_pair, 16), 16), :])
        cols = pl.ds(aligned(p, 2 * LANES), 2 * LANES)
        quarters_ref[p] = quarters
        product = dot(quarters, states, TN)
        product = jnp.concatenate([product[:LANES], product[LANES:]], axis=1)
        grads_ref[:, cols] = (product + grads_over_ref[:, cols].astype(F32)).astype(BF16)

    def pair_rows(first, last):
        if first == 0:
            rows_ref[...] = jnp.zeros_like(rows_ref)

        def pair(p):
            weight = weight_ref[:, pl.ds(aligned(first + p, 2 * LANES), 2 * LANES)]
            weight = jnp.concatenate([weight[:, :LANES], weight[:, LANES:]], axis=0)
            rows_ref[...] += dot(quarters_ref[first + p], weight)

        tile_loop(last - first, pair, UNROLL_ROWS)

    def span_outer(g):
        first, last = spans[g]
        rows = pl.ds(first * 16, (last - first) * 16)

        def spread(t):
            _, _, within = tile_masks(tiles_ref[t, 17:18, :].astype(F32))
            spread_ref[t, rows, :] = keep_within(dot(wide_ref[rows, :], target_ref[t]), within)

        def outer(t):
            outer_ref[t, : (last - first) * 16, :] = dot(spread_ref[t, rows, :], hidden_ref[t], NT).astype(BF16)

        tile_loop(main, spread, UNROLL_SPAN)
        tile_loop(main, outer, UNROLL_SPAN)

    settled = {}

    def settle():
        if not settled:
            for fetch in fetch_late:
                fetch.wait()
            settled["first"] = extended_first(first_ref, first_bias_ref)
            settled["sums"] = dot(counts_ref[...], grad_ref[...], NT).astype(BF16)

    def fill_small():
        settle()
        small_ref[...] = jnp.zeros_like(small_ref)
        small_ref[:half_width, :LANES] = dot(settled["sums"], group_states(states_ref), TN).astype(BF16)
        small_ref[half_width + ROWS : half_width + ROWS + 16, : biases_ref.shape[1]] = jnp.concatenate(
            [biases_ref[...], jnp.zeros_like(biases_ref)], axis=0
        ).astype(BF16)
        small_ref[:, LANES : 4 * LANES] = weights_ref[...]

    def chunk_grads(c):
        if chunks[c][0] is grads_ref:
            first = chunks[c][2] // (2 * LANES)
            tile_loop(
                chunks[c][3] // (2 * LANES), lambda p: pair_grads(first + p, spans[chunks[c][5]][0]), UNROLL_PAIRS
            )
        else:
            fill_small()
        start(c, 0)

    span_outer(0)
    fetch_over.wait()
    pl.semaphore_wait(barrier, len(greeted))

    rows_copy = side(1, rows_send_ref, rows_land_ref, partner)
    rim_copy = side(2, rim_send_ref, rim_land_ref, before)
    feat_copy = side(3, feat_ref, feat_land_ref, partner)
    state_store = pltpu.make_async_copy(state_out_ref, state_hbm, late_sem.at[0])
    first_store = pltpu.make_async_copy(first_sum_ref, first_hbm, late_sem.at[1])
    feat_store = pltpu.make_async_copy(feat_out_ref, feat_hbm, late_sem.at[2])

    def source_rows():
        settle()
        rows = slot_ref[0:1, : 2 * main * HALF].astype(jnp.int32)
        hot = (iota((slots, 2 * main * HALF), 0) == rows).astype(F32).astype(BF16)
        source_ref[...] = dot(hot, rows_ref[...].astype(BF16)) + rows_over_ref[:slots, :]
        bias = dot(settled["sums"], second_bias_ref[...])
        for g in range(padded):
            for a in range(2):
                at = g * GROUP + a * HALF
                size = min(HALF, GROUP - a * HALF, slots - at)
                if size > 0:
                    source_ref[at : at + size, :] += bias[(a * padded + g) * HALF : (a * padded + g) * HALF + size]
        source_ref[border:, :] += partial_ref[...].T
        rows_send_ref[...] = source_ref[...].astype(BF16)
        rows_copy.start()

    def rim_rows():
        rows_copy.wait()
        source_ref[...] += rows_land_ref[...].astype(F32)
        rim_send_ref[...] = source_ref[:border, :].astype(BF16)
        rim_copy.start()

    def state_rows():
        rim_copy.wait()
        source_ref[slots - border :, :] += rim_land_ref[...].astype(F32)
        rows = source_ref[border:, :].T
        state_out_ref[...] = jnp.where(gate == 0, rows[:half_width], rows[half_width:]) + own_ref[...]
        state_store.start()

    table_ready = []

    def tile_grads(first, last):
        settle()
        if not table_ready:
            fetch_table.wait()
            table_ready.append(True)
            first_sum_ref[...] = first_over_ref[...]

        def tile(t):
            t = first + t
            held = tiles_ref[t]
            pre = dot(settled["first"], held, TN)
            logistic = jax.nn.sigmoid(pre)
            slope = logistic * (1.0 + pre * (1.0 - logistic))
            table = table_ref[meta_ref[0, t]]
            part, first_grad = hidden_slopes(held, table, spread_ref[t], slope, first_ref[...])
            part_ref[pl.ds(aligned(t, 16), 16), :] = part
            first_sum_ref[...] += first_grad

        tile_loop(last - first, tile, UNROLL_TILES)

    def first_copy(i):
        device = partner if i == 0 else peers[i - 1]
        return pltpu.make_async_remote_copy(
            first_land_ref.at[2 * i], first_land_ref.at[2 * i + 1], first_send.at[i], first_recv.at[i],
            device_id=device, device_id_type=pl.DeviceIdType.MESH,
        )

    def first_step(i):
        if i > 0:
            first_copy(i - 1).wait()
            first_sum_ref[...] = first_land_ref[2 * i - 2] + first_land_ref[2 * i - 1]
        if i <= digits:
            first_land_ref[2 * i] = first_sum_ref[...]
            first_copy(i).start()
        else:
            first_store.start()

    def back(first, last):
        def chunk(c):
            c = first + 2 * c
            lane = jnp.concatenate([lane_ref[c : c + 1, :], lane_ref[c + 1 : c + 2, :]], axis=1).astype(jnp.int32)
            hot = (iota((TILE, 2 * LANES), 0) == lane).astype(F32).astype(BF16)
            moved = dot(part_ref[...], hot)
            tile = jnp.concatenate([tile_ref[c : c + 1, :], tile_ref[c + 1 : c + 2, :]], axis=1)
            total = jnp.concatenate([feat_over_ref[c * 16 : (c + 1) * 16], feat_over_ref[(c + 1) * 16 : (c + 2) * 16]], axis=1)
            for t in range(main):
                total = total + jnp.where(tile == float(t), moved[t * 16 : (t + 1) * 16], 0.0)
            feat_ref[:, c * LANES : (c + 2) * LANES] = total

        for c in range((last - first) // 2):
            chunk(c)
        if last == chunk_count:
            feat_copy.start()

    def feat_total():
        feat_copy.wait()
        feat_out_ref[...] = feat_ref[...] + feat_land_ref[...]
        feat_store.start()

    batch = TILE_BATCH
    tile_batches = range(0, main, batch)
    back_batches = range(0, chunk_count, 8)
    row_batches = range(0, half_width // 2, 8)
    done = [0] * len(chunks)

    def go(c):
        arrive(c, done[c])
        start(c, done[c] + 1)
        done[c] += 1

    actions = {
        "span": span_outer,
        "chunk": chunk_grads,
        "go": go,
        "tiles": lambda i: tile_grads(tile_batches[i], min(tile_batches[i] + batch, main)),
        "first": first_step,
        "rows": lambda i: pair_rows(row_batches[i], row_batches[i] + 8),
        "back": lambda i: back(back_batches[i], min(back_batches[i] + 8, chunk_count)),
        "sources": lambda i: source_rows(),
        "rim": lambda i: rim_rows(),
        "state": lambda i: state_rows(),
        "feat": lambda i: feat_total(),
    }
    for name, i in event_order(members, digits, len(tile_batches), len(back_batches), len(row_batches)):
        actions[name](i)

    for c in range(len(chunks)):
        for phase in range(2 * digits):
            if phase < digits:
                scatter(c, phase).wait_send()
            else:
                gather(c, 2 * digits - 1 - phase).wait_send()
    for copy in (state_store, first_store, feat_store):
        copy.wait()


def emit_kernel(
    total_ref, small_ref, first_in_ref, new_in_ref, state_in_ref, feat_in_ref,
    new_ref, state_ref, feat_ref, first_ref, first_bias_ref, second_out, second_bias_ref, input_ref, hidden_ref,
    input_bias_ref, hidden_bias_ref,
    wide_ref, sems,
):
    blocks = sems.shape[0]
    size = wide_ref.shape[1] // blocks
    writes = []
    for i in range(blocks):
        cols = pl.ds(i * size, size)
        wide_ref[:, cols] = total_ref[:, cols].astype(F32)
        writes.append(pltpu.make_async_copy(wide_ref.at[:, cols], second_out.at[:, cols], sems.at[i]))
        writes[i].start()
    new_ref[...] = new_in_ref[...]
    state_ref[...] = state_in_ref[...]
    feat_ref[...] = feat_in_ref[...]
    small = small_ref[:, : 4 * LANES].astype(F32)
    half = second_bias_ref.shape[0]
    second_bias_ref[...] = small[:half, :LANES]
    first_ref[...] = first_in_ref[:16]
    first_bias_ref[...] = first_in_ref[18:19]
    part = input_ref.shape[1]
    at = half + ROWS
    input_bias_ref[...] = small[at : at + 3, :part]
    hidden_bias_ref[...] = small[at + 3 : at + 6, :part]
    for k in range(3):
        input_ref[k] = small[:part, LANES + k * LANES : LANES + (k + 1) * LANES]
        hidden_ref[k] = small[part:, LANES + k * LANES : LANES + (k + 1) * LANES]
    for copy in writes:
        copy.wait()


def per_device(
    node_state, edge_feat, source, target, edge_mask, node_mask, net_first, net_first_bias, net_second,
    net_second_bias, gru_input, gru_hidden, gru_input_bias, gru_hidden_bias, cotangent,
):
    node_count, half_width = node_state.shape
    edge_count = source.shape[0]
    width = 2 * half_width
    chunks = edge_count // LANES
    slots = BORDER + node_count
    groups = -(-slots // GROUP)
    padded = (groups + 1) // 2 * 2
    over = groups + edge_count // TILE - 1 - MAIN
    first_bias = net_first_bias.reshape(1, width)
    second_bias = net_second_bias.reshape(half_width, width)
    shape = jax.ShapeDtypeStruct
    vmem = pl.BlockSpec(memory_space=pltpu.VMEM)
    smem = pl.BlockSpec(memory_space=pltpu.SMEM)
    hbm = pl.BlockSpec(memory_space=pl.ANY)

    def local(mib):
        return pltpu.CompilerParams(vmem_limit_bytes=mib * MIB)

    def remote(collective_id, mib):
        return pltpu.CompilerParams(vmem_limit_bytes=mib * MIB, collective_id=collective_id, has_side_effects=True)

    state_t = node_state.T
    operands = in_hbm(
        source.reshape(chunks, LANES), target.reshape(chunks, LANES), edge_mask.reshape(chunks, LANES), edge_feat, state_t
    )
    body, specs, scratch = fetched(place_kernel, operands)
    weights = in_hbm(net_second, second_bias, net_first, first_bias)
    second_near, second_bias_near, first_near, first_bias_near, full_t, states, placed, values, tile_rows, lane_rows, meta, slot_rows = pl.pallas_call(
        body,
        out_shape=tuple(shape(x.shape, x.dtype) for x in weights)
        + (
            shape((width, node_count), BF16),
            shape((2, padded, HALF, width), F32),
            shape((MAIN, ROWS, TILE), BF16),
            shape((ROWS, edge_count), BF16),
            shape((chunks, LANES), F32),
            shape((chunks, LANES), F32),
            shape((8, LANES), jnp.int32),
            shape((8, -(-2 * MAIN * HALF // LANES) * LANES), F32),
        ),
        in_specs=specs + [hbm] * 4,
        out_specs=(vmem,) * 12,
        scratch_shapes=[
            pltpu.VMEM((chunks * ROWS, LANES), BF16),
            pltpu.VMEM((MAIN * 16 + 3 * ROWS, edge_count), BF16),
            pltpu.VMEM((TILE, edge_count), BF16),
            pltpu.VMEM((half_width, node_count), BF16),
            pltpu.VMEM((2, half_width, LANES), BF16),
            pltpu.SemaphoreType.DMA((3,)),
            pltpu.SemaphoreType.DMA((3,)),
            pltpu.SemaphoreType.DMA((4,)),
        ]
        + scratch,
        compiler_params=remote(0, 20),
        name="place_edges",
    )(*operands, *weights)

    blank_shapes = (
        pltpu.HBM((width, half_width * width), BF16),
        pltpu.HBM((padded * GROUP + 16, width), F32),
        pltpu.HBM((chunks * 16, LANES), F32),
        pltpu.HBM((ROWS, width), F32),
    )
    incoming, over_tiles, counts, table, hidden, targets, *blanks = pl.pallas_call(
        forward_kernel,
        out_shape=(
            shape((half_width, node_count), BF16),
            pltpu.HBM((over, ROWS, TILE), BF16),
            shape((2 * padded * HALF, node_count), BF16),
            pltpu.HBM((padded, half_width * HALF, 2 * width), BF16),
            shape((MAIN, 2 * width, TILE), BF16),
            shape((MAIN, node_count, TILE), BF16),
        )
        + blank_shapes,
        in_specs=[vmem] * 4 + [smem, vmem] + [hbm] * 3 + [vmem],
        out_specs=(vmem, hbm, vmem, hbm, vmem, vmem) + (hbm,) * 4,
        scratch_shapes=[
            pltpu.VMEM((padded, 16, node_count), F32),
            pltpu.VMEM((padded, half_width * HALF, 2 * width), BF16),
            pltpu.VMEM((2 * width, TILE), BF16),
            pltpu.VMEM((node_count, TILE), BF16),
            pltpu.VMEM((TILE, edge_count), BF16),
            pltpu.VMEM((half_width * HALF, node_count), F32),
            pltpu.VMEM((width, half_width * width), BF16),
            pltpu.VMEM((max(padded * GROUP + 16, chunks * 16), width), F32),
            pltpu.VMEM((ROWS, edge_count), BF16),
            pltpu.VMEM((chunks, LANES), F32),
            pltpu.VMEM((chunks, LANES), F32),
            pltpu.VMEM((ROWS, TILE), BF16),
            pltpu.SemaphoreType.DMA((3,)),
            pltpu.SemaphoreType.DMA((4,)),
        ],
        compiler_params=local(28),
        name="forward_edges",
    )(first_near, first_bias_near, second_bias_near, second_near, meta, placed, values, tile_rows, lane_rows, states)

    operands = in_hbm(
        state_t, node_mask.reshape(node_count // LANES, LANES), gru_input.swapaxes(1, 2), gru_hidden.swapaxes(1, 2),
        gru_input_bias, gru_hidden_bias, cotangent.T
    )
    body, specs, scratch = fetched(node_kernel, operands)
    message_grad, new_state, grad_own, state_partial, weight_grads, bias_grads = pl.pallas_call(
        body,
        out_shape=(
            shape((half_width, node_count), BF16),
            shape((half_width, node_count), BF16),
            shape((half_width, node_count), F32),
            shape((width, node_count), F32),
            shape((width, 3 * width), BF16),
            shape((8, half_width), F32),
        ),
        in_specs=specs + [vmem] * 2,
        out_specs=(vmem,) * 6,
        scratch_shapes=[
            pltpu.VMEM((half_width, node_count), BF16),
            pltpu.VMEM((width, node_count), F32),
            pltpu.VMEM((half_width, node_count), F32),
            pltpu.SemaphoreType.DMA((2,)),
            pltpu.SemaphoreType.DMA((2,)),
        ]
        + scratch,
        compiler_params=remote(1, 6),
        name="node_update",
    )(*operands, incoming, full_t)

    grads_over, rows_over, feat_over, first_over = pl.pallas_call(
        overflow_kernel,
        out_shape=blank_shapes,
        in_specs=[smem] + [hbm] * 13,
        out_specs=(hbm,) * 4,
        scratch_shapes=[
            pltpu.VMEM((half_width, node_count), BF16),
            pltpu.VMEM((16, width), BF16),
            pltpu.VMEM((1, width), BF16),
            pltpu.VMEM((ROWS, TILE), BF16),
            pltpu.VMEM((2, padded, HALF, width), F32),
            pltpu.VMEM((padded * GROUP + 16, width), F32),
            pltpu.VMEM((over * 16, TILE), BF16),
            pltpu.VMEM((chunks * 16, LANES), F32),
            pltpu.VMEM((ROWS, width), F32),
            pltpu.VMEM((width, half_width * width), F32),
            pltpu.VMEM((width, half_width * width), BF16),
            pltpu.VMEM((1, half_width * HALF, 2 * width), BF16),
            pltpu.VMEM((half_width * HALF, 2 * width), BF16),
            pltpu.VMEM((chunks, LANES), F32),
            pltpu.VMEM((chunks, LANES), F32),
            pltpu.SemaphoreType.DMA,
        ],
        input_output_aliases={10 + i: i for i in range(4)},
        compiler_params=local(16),
        name="overflow_edges",
    )(meta, message_grad, *in_hbm(net_first, first_bias), *in_hbm(over_tiles, table), states, *in_hbm(net_second), tile_rows, lane_rows,
        *in_hbm(*blanks),
    )

    digits = (lax.axis_size("edge") - 1).bit_length()
    unit = LANES << (digits - 3)
    columns = half_width * width
    small_width = max(4 * LANES, unit)
    steps = min(columns // unit, len(SIZES)) + 1
    whole = columns + small_width
    plan, _ = chunk_plan(columns // unit, digits)
    span = max(sum(p[1] for p in plan if p[3] == g) for g in range(2)) * unit // (2 * LANES)
    late = (
        slot_rows, counts, *in_hbm(rows_over, feat_over, first_over), tile_rows, lane_rows, weight_grads, bias_grads,
        state_partial, grad_own,
    )
    total, small_total, grad_feat, grad_state, first_sum = pl.pallas_call(
        functools.partial(finish_kernel, digits),
        out_shape=(
            pltpu.VMEM((width, columns), BF16),
            pltpu.VMEM((width, small_width), BF16),
            shape((16, edge_count), F32),
            shape((half_width, node_count), F32),
            shape((ROWS, width), F32),
        ),
        in_specs=[vmem] * 4 + [smem] + [vmem] * 5 + [hbm] * 13,
        out_specs=(vmem, vmem, hbm, hbm, hbm),
        scratch_shapes=[
            [pltpu.VMEM(x.shape, x.dtype) for x in late],
            pltpu.SemaphoreType.DMA((len(late),)),
            pltpu.VMEM((16, edge_count), F32),
            pltpu.VMEM((half_width, node_count), F32),
            pltpu.VMEM((padded, half_width * HALF, 2 * width), BF16),
            pltpu.VMEM((width, columns), BF16),
            pltpu.VMEM((half_width * HALF, node_count), BF16),
            pltpu.VMEM((MAIN, half_width * HALF, TILE), BF16),
            pltpu.VMEM((MAIN, 16 * span, 2 * width), BF16),
            pltpu.VMEM((half_width // 2, 2 * MAIN * HALF, 2 * width), BF16),
            pltpu.VMEM((width, columns), BF16),
            pltpu.VMEM((width, whole), BF16),
            [pltpu.VMEM((max(16, width >> (i + 1)), whole >> max(0, i - 2)), BF16) for i in range(digits)],
            pltpu.VMEM((width, small_width), BF16),
            pltpu.VMEM((MAIN * 16, TILE), BF16),
            pltpu.VMEM((2 * MAIN * HALF, width), F32),
            pltpu.VMEM((slots, width), F32),
            pltpu.VMEM((ROWS, width), F32),
            pltpu.VMEM((2 * digits + 2, ROWS, width), F32),
            pltpu.VMEM((16, edge_count), F32),
            pltpu.VMEM((16, edge_count), F32),
            pltpu.VMEM((slots, width), BF16),
            pltpu.VMEM((slots, width), BF16),
            pltpu.VMEM((BORDER, width), BF16),
            pltpu.VMEM((BORDER, width), BF16),
            pltpu.SemaphoreType.DMA((steps, 2 * digits)),
            pltpu.SemaphoreType.DMA((steps, 2 * digits)),
            pltpu.SemaphoreType.DMA((4,)),
            pltpu.SemaphoreType.DMA((4,)),
            pltpu.SemaphoreType.DMA((digits + 1,)),
            pltpu.SemaphoreType.DMA((digits + 1,)),
            pltpu.SemaphoreType.DMA((3,)),
        ],
        compiler_params=remote(2, 38),
        name="finish_sums",
    )(
        first_near, first_bias_near, second_bias_near, second_near, meta, message_grad, states, placed, hidden, targets,
        *in_hbm(table, grads_over), *late,
    )

    blocks = 8
    outs = pl.pallas_call(
        emit_kernel,
        out_shape=(
            shape((half_width, node_count), BF16),
            shape((half_width, node_count), F32),
            shape((16, edge_count), F32),
            shape((16, width), F32),
            shape((1, width), F32),
            shape((width, columns), F32),
            shape((half_width, width), F32),
            shape((3, half_width, width), F32),
            shape((3, half_width, width), F32),
            shape((3, half_width), F32),
            shape((3, half_width), F32),
        ),
        in_specs=[vmem] * 6,
        out_specs=(vmem,) * 5 + (hbm,) + (vmem,) * 5,
        scratch_shapes=[
            pltpu.VMEM((width, columns), F32),
            pltpu.SemaphoreType.DMA((blocks,)),
        ],
        compiler_params=local(12),
        name="emit",
    )(total, small_total, first_sum, new_state, grad_state, grad_feat)
    outs = list(outs)
    outs[0], outs[1] = outs[0].T, outs[1].T
    outs[7], outs[8] = outs[7].swapaxes(1, 2), outs[8].swapaxes(1, 2)
    outs[4] = outs[4].reshape(width)
    outs[6] = outs[6].reshape(columns)
    return tuple(outs)


def solution(mesh):
    return jax.shard_map(
        per_device,
        mesh=mesh,
        in_specs=(
            P("edge", "gate"), P(None, "edge"), P("edge"), P("edge"), P("edge"), P("edge"), P(), P(), P(None, "gate"),
            P("gate"), P(None, None, "gate"), P(None, None, "gate"), P(None, "gate"), P(None, "gate"), P("edge", "gate"),
        ),
        out_specs=(
            P("edge", "gate"), P("edge", "gate"), P(None, "edge"), P(), P(), P(None, "gate"), P("gate"),
            P(None, None, "gate"), P(None, None, "gate"), P(None, "gate"), P(None, "gate"),
        ),
        check_vma=False,
    )
```

```python
import functools

import jax
import jax.numpy as jnp
from jax import lax
from jax.experimental import pallas as pl
from jax.experimental.pallas import tpu as pltpu
from jax.sharding import PartitionSpec as P

BORDER = 64
GROUP = 14
HALF = 8
TILE = 256
MAIN = 26
UNROLL_ROWS = 8
UNROLL_PAIRS = 99
UNROLL_SPAN = 26
UNROLL_TILES = 3
TILE_BATCH = 3
LANES = 128
ROWS = 32
MIB = 1024 * 1024

KINDS = ("span", "chunk", "go", "tiles", "first", "back", "sources", "rim", "state", "feat", "rows")
SIZES = (4, 7, 6, 5, 5, 5)
ORDERS = ((0, 2, 1), (1, 2, 0), (2, 1, 0), (2, 1, 0), (0, 1, 2), (0, 1, 2), (1, 0, 2))
FIRST_SPAN = 3
SCHEDULE = (
    17, 18, 16, 1, 20, 22, 19, 21, 32, 34, 56, 33, 55, 36, 54, 34, 50, 32, 35, 38, 36, 51, 34, 37, 33, 32, 160, 36,
    49, 38, 34, 33, 35, 37, 32, 36, 52, 38, 48, 35, 37, 161, 33, 32, 36, 38, 53, 64, 34, 35, 37, 32, 65, 33, 36, 162,
    163, 34, 35, 38, 37, 66, 33, 32, 81, 35, 38, 67, 36, 37, 34, 96, 33, 32, 80, 68, 35, 38, 37, 112, 82, 83, 69,
    128, 36, 33, 34, 144, 37, 35, 38,
)

NN = ((1,), (0,))
NT = ((1,), (1,))
TN = ((0,), (0,))
F32 = jnp.float32
BF16 = jnp.bfloat16


def dot(left, right, dims=NN):
    return lax.dot_general(left, right, (dims, ((), ())), preferred_element_type=F32)


def iota(shape, dim):
    return lax.broadcasted_iota(jnp.int32, shape, dim)


def extended_first(first_ref, bias_ref):
    extra = jnp.where(iota((ROWS - 16, LANES), 0) == 2, bias_ref[...].astype(F32), 0.0)
    return jnp.concatenate([first_ref[...].astype(F32), extra], axis=0).astype(BF16)


def tile_masks(slot_row):
    place = slot_row.astype(jnp.int32) - 1
    low = jnp.logical_and(place >= 0, place < HALF)
    high = place >= HALF
    within = jnp.where(high, place - HALF, place)
    return low, high, within


def halves(hidden, low, high):
    return jnp.concatenate(
        [jnp.where(low, hidden, 0.0), jnp.where(high, hidden, 0.0)], axis=0
    ).astype(BF16)


def keep_within(values, within):
    rows, width = values.shape
    match = iota((HALF, width), 0) == within
    kept = jnp.where(match[None], values.reshape(rows // HALF, HALF, width), 0.0)
    return kept.reshape(rows, width).astype(BF16)


def target_hot(target_row, node_count):
    width = target_row.shape[1]
    return (iota((node_count, width), 0) + 1 == target_row.astype(jnp.int32)).astype(F32).astype(BF16)


def lane_hot(lane_ref, out_ref):
    chunks = lane_ref.shape[0]
    for c in range(chunks):
        row = lane_ref[c : c + 1, :].astype(jnp.int32)
        out_ref[:, c * LANES : (c + 1) * LANES] = (
            (iota((TILE, LANES), 0) == row).astype(F32).astype(BF16)
        )


def aligned(index, unit):
    return index * unit if isinstance(index, int) else pl.multiple_of(index * unit, unit)


def tile_loop(count, body, step):
    def several(i, carry):
        for s in range(step):
            body(i * step + s)
        return carry

    whole = count // step if step < count else 0
    if whole:
        lax.fori_loop(0, whole, several, 0)
    for t in range(whole * step, count):
        body(t)


def fetched(kernel, operands):
    count = len(operands)

    def body(*refs):
        sources, others, targets, sem = refs[:count], refs[count : -count - 1], refs[-count - 1 : -1], refs[-1]
        copies = [pltpu.make_async_copy(sources[i], targets[i], sem.at[i]) for i in range(count)]
        for copy in copies:
            copy.start()

        def ready():
            for copy in copies:
                copy.wait()

        kernel(ready, *targets, *others)

    scratch = [pltpu.VMEM(x.shape, x.dtype) for x in operands] + [pltpu.SemaphoreType.DMA((count,))]
    return body, [pl.BlockSpec(memory_space=pl.ANY)] * count, scratch


def in_hbm(*arrays):
    return tuple(pltpu.with_memory_space_constraint(x, pltpu.HBM) for x in arrays)


def place_kernel(
    ready, source_ref, target_ref, mask_ref, feat_ref, state_ref, second_hbm, second_bias_hbm, first_hbm, first_bias_hbm,
    second_ref, second_bias_ref, first_ref, first_bias_ref, full_ref, states_ref, tiles_ref, values_ref, tile_ref, lane_ref, meta_ref, slot_ref,
    counts_ref, spread_ref, hot_ref, other_ref, rim_ref, send_sem, recv_sem, load_sem,
):
    chunks = source_ref.shape[0]
    half, node_count = state_ref.shape
    main = tiles_ref.shape[0]
    padded = states_ref.shape[1]
    groups = -(-(node_count + BORDER) // GROUP)
    edge, gate = lax.axis_index("edge"), lax.axis_index("gate")
    count = lax.axis_size("edge")
    first_node = edge * node_count
    partner = (edge, 1 - gate)
    after = lax.rem(edge + 1, count)
    before = lax.rem(edge + count - 1, count)
    mesh_signal(
        pltpu.get_barrier_semaphore(), [partner, (after, gate), (after, 1 - gate), (before, gate), (before, 1 - gate)]
    )

    def send(index, source, target, device):
        return pltpu.make_async_remote_copy(
            source, target, send_sem.at[index], recv_sem.at[index], device_id=device, device_id_type=pl.DeviceIdType.MESH
        )

    loads = [
        pltpu.make_async_copy(far, near, load_sem.at[i])
        for i, (far, near) in enumerate(
            [(first_hbm, first_ref), (first_bias_hbm, first_bias_ref), (second_bias_hbm, second_bias_ref), (second_hbm, second_ref)]
        )
    ]
    ready()
    for load in loads:
        load.start()
    rim = state_ref.at[:, pl.ds(node_count - LANES, LANES)]
    copies = [
        send(0, rim, rim_ref.at[0], (after, gate)),
        send(1, rim, rim_ref.at[1], (after, 1 - gate)),
        send(2, state_ref, other_ref, partner),
    ]
    for copy in copies:
        copy.start()

    group_rows = []
    slot_rows = []
    for c in range(chunks):
        slot = (source_ref[c : c + 1, :] - first_node + BORDER).astype(F32)
        group = jnp.floor((slot + 0.5) * (1.0 / GROUP))
        slot_rows.append(slot)
        group_rows.append(group)
        counts_ref[c * ROWS : (c + 1) * ROWS, :] = (
            (iota((ROWS, LANES), 0).astype(F32) == group).astype(F32).astype(BF16)
        )
    above = jnp.where(
        iota((LANES, 2 * LANES), 0) < iota((LANES, 2 * LANES), 1), 1.0, 0.0
    ).astype(BF16)
    sums = dot(counts_ref[...], above)
    running = jnp.zeros((ROWS, LANES), F32)
    ranks = []
    for c in range(chunks):
        hot = counts_ref[c * ROWS : (c + 1) * ROWS, :].astype(F32)
        part = sums[c * ROWS : (c + 1) * ROWS]
        ranks.append(jnp.sum(hot * (part[:, :LANES] + running), axis=0, keepdims=True))
        running = running + part[:, LANES:]
    owned = jnp.floor((running + (TILE - 1.0)) * (1.0 / TILE))
    earlier = (iota((ROWS, ROWS), 1) < iota((ROWS, ROWS), 0)).astype(F32).astype(BF16)
    start = dot(earlier, owned.astype(BF16))
    end = start + owned
    total = jnp.sum(owned, axis=0, keepdims=True)

    def group_of(tile):
        return jnp.minimum(jnp.sum((end <= tile).astype(F32), axis=0, keepdims=True), groups - 1.0)

    row8 = iota((8, LANES), 0)
    lane = iota((1, LANES), 1).astype(F32)
    meta_ref[...] = jnp.where(row8 == 0, group_of(lane), jnp.where(row8 == 1, total, 0.0)).astype(jnp.int32)
    for c in range(slot_ref.shape[1] // LANES):
        row = lane + float(c * LANES)
        high = jnp.where(row >= main * HALF, 1.0, 0.0)
        row = row - high * (main * HALF)
        tile = jnp.floor((row + 0.5) * (1.0 / HALF))
        place = row - tile * HALF + high * HALF
        slot = group_of(tile) * GROUP + place
        slot = jnp.where(jnp.logical_and(place < GROUP, tile < jnp.minimum(total, float(main))), slot, -1.0)
        slot_ref[:, c * LANES : (c + 1) * LANES] = jnp.broadcast_to(slot, (8, LANES))

    row16 = iota((ROWS - 16, LANES), 0)
    for c in range(chunks):
        cols = slice(c * LANES, (c + 1) * LANES)
        hot = counts_ref[c * ROWS : (c + 1) * ROWS, :].astype(F32)
        over = jnp.floor(ranks[c] * (1.0 / TILE))
        tile = jnp.sum(hot * start, axis=0, keepdims=True) + over
        lane = ranks[c] - TILE * over
        tile_ref[c : c + 1, :] = tile
        lane_ref[c : c + 1, :] = lane
        hot_ref[:, cols] = (iota((TILE, LANES), 0).astype(F32) == lane).astype(F32).astype(BF16)
        place = slot_rows[c] - GROUP * group_rows[c] + 1.0
        target = jnp.where(
            mask_ref[c : c + 1, :] > 0, target_ref[c : c + 1, :] - first_node + 1, 0
        ).astype(F32)
        more = jnp.where(row16 == 0, target, jnp.where(row16 == 1, place, jnp.where(row16 == 2, 1.0, 0.0)))
        feats = feat_ref[:, cols].astype(F32)
        values_ref[:, cols] = jnp.concatenate([feats, more], axis=0).astype(BF16)
        for t in range(main):
            spread_ref[t * 16 : (t + 1) * 16, cols] = jnp.where(tile == float(t), feats, 0.0).astype(BF16)
        in_tile = iota((ROWS, LANES), 0).astype(F32) == tile
        for i, value in enumerate((target, place, 1.0)):
            at = main * 16 + i * ROWS
            spread_ref[at : at + ROWS, cols] = jnp.where(in_tile, value, 0.0).astype(BF16)
    moved = dot(spread_ref[...], hot_ref[...], NT)
    blank = jnp.zeros((13, TILE), F32)
    for t in range(main):
        tiles_ref[t, :16, :] = moved[t * 16 : (t + 1) * 16].astype(BF16)
        more = [moved[main * 16 + i * ROWS + t : main * 16 + i * ROWS + t + 1] for i in range(3)]
        tiles_ref[t, 16:, :] = jnp.concatenate(more + [blank], axis=0).astype(BF16)

    for copy in copies:
        copy.wait()
    is_first = gate == 0
    mine, other = state_ref[...], other_ref[...]
    full = jnp.concatenate([jnp.where(is_first, mine, other), jnp.where(is_first, other, mine)], axis=0)
    full_ref[...] = full
    own, swapped = rim_ref[0], rim_ref[1]
    rims = jnp.concatenate([jnp.where(is_first, own, swapped), jnp.where(is_first, swapped, own)], axis=0)
    rows = jnp.concatenate(
        [rims.astype(F32).T[LANES - BORDER :], full.astype(F32).T], axis=0
    )
    spare = padded * GROUP + 16 - rows.shape[0]
    rows = jnp.concatenate([rows, jnp.zeros((spare, 2 * half), F32)], axis=0)
    for load in loads:
        load.wait()
    for g in range(padded):
        for a in range(2):
            states_ref[a, g] = rows[g * GROUP + a * HALF : g * GROUP + (a + 1) * HALF]


def group_states(states_ref):
    _, padded, half, width = states_ref.shape
    return jnp.concatenate([states_ref[a].reshape(padded * half, width) for a in range(2)], axis=0).astype(BF16)


def group_counts(counts_ref):
    padded, _, node_count = counts_ref.shape
    return jnp.concatenate(
        [counts_ref[:, a * HALF : (a + 1) * HALF, :].reshape(padded * HALF, node_count) for a in range(2)], axis=0
    ).astype(BF16)


def forward_kernel(
    first_ref, first_bias_ref, second_bias_ref, second_ref, meta_ref, tiles_ref, values_hbm, tile_hbm, lane_hbm, states_ref,
    incoming_ref, over_hbm, counts_out_ref, table_out_ref, hidden_ref, targets_ref, *rest,
):
    blank_refs, rest = rest[:4], rest[4:]
    counts_ref, table_ref, hidden_over_ref, targets_over_ref, hot_ref, total_ref, narrow_ref, zeros_ref = rest[:8]
    values_ref, tile_ref, lane_ref, held_ref, sems, blank_sems = rest[8:]
    chunks = tile_ref.shape[0]
    half_width, node_count = incoming_ref.shape
    main = tiles_ref.shape[0]
    padded = table_ref.shape[0]
    over_total = jnp.maximum(meta_ref[1, 0] - main, 0)
    narrow_ref[...] = jnp.zeros_like(narrow_ref)
    zeros_ref[...] = jnp.zeros_like(zeros_ref)
    blanks = []
    for i, blank_ref in enumerate(blank_refs):
        rows, cols = blank_ref.shape
        zeros = narrow_ref if blank_ref.dtype == BF16 else zeros_ref
        blanks.append(pltpu.make_async_copy(zeros.at[pl.ds(0, rows), pl.ds(0, cols)], blank_ref, blank_sems.at[i]))
        blanks[i].start()
    first_t = extended_first(first_ref, first_bias_ref)

    def expand(held):
        low, high, _ = tile_masks(held[17:18, :].astype(F32))
        pre = dot(first_t, held, TN)
        return halves(pre * jax.nn.sigmoid(pre), low, high), target_hot(held[16:17, :].astype(F32), node_count)

    def expand_main(t):
        hidden_ref[t], targets_ref[t] = expand(tiles_ref[t])


    states = group_states(states_ref)

    def table_pair(p):
        pair = second_ref[:, pl.ds(pl.multiple_of(p * 2 * LANES, 2 * LANES), 2 * LANES)]
        both = jnp.concatenate([pair[:, :LANES], pair[:, LANES:]], axis=0)
        product = dot(states, both, NT).reshape(2, padded, HALF, 2 * LANES)
        for a in range(2):
            rows = jnp.concatenate([product[a, :, :, :LANES], product[a, :, :, LANES:]], axis=1)
            table_ref[:, pl.ds(pl.multiple_of(p * 16, 16), 16), a * LANES : (a + 1) * LANES] = rows.astype(BF16)

    pairs = half_width // 2
    shared = min(main, pairs) // 4 * 4

    def both(i):
        expand_main(i)
        table_pair(i)

    tile_loop(shared, both, shared // 2)
    for t in range(shared, main):
        expand_main(t)
    for p in range(shared, pairs):
        table_pair(p)
    keep = pltpu.make_async_copy(table_ref, table_out_ref, sems.at[1])
    keep.start()

    def messages(hidden, targets, group, held):
        _, _, within = tile_masks(held[17:18, :].astype(F32))
        message = keep_within(dot(table_ref[group], hidden), within)
        place = held[17:18, :].astype(jnp.int32) - 1
        places = (iota((16, TILE), 0) == place).astype(F32).astype(BF16)
        sums = dot(jnp.concatenate([message, places], axis=0), targets, NT)
        total_ref[...] += sums[: half_width * HALF]
        counts_ref[group] += sums[half_width * HALF :]

    total_ref[...] = jnp.zeros_like(total_ref)
    counts_ref[...] = jnp.zeros_like(counts_ref)
    tile_loop(main, lambda t: messages(hidden_ref[t], targets_ref[t], meta_ref[0, t], tiles_ref[t]), 13)

    @pl.when(over_total > 0)
    def _():
        for source, target in [(values_hbm, values_ref), (tile_hbm, tile_ref), (lane_hbm, lane_ref)]:
            load = pltpu.make_async_copy(source, target, sems.at[2])
            load.start()
            load.wait()
        lane_hot(lane_ref, hot_ref)

    def over_messages(u, carry):
        wanted = (main + u).astype(F32)
        pieces = []
        for c in range(chunks):
            values = values_ref[:, c * LANES : (c + 1) * LANES].astype(F32)
            pieces.append(jnp.where(tile_ref[c : c + 1, :] == wanted, values, 0.0).astype(BF16))
        held = dot(jnp.concatenate(pieces, axis=1), hot_ref[...], NT).astype(BF16)
        held_ref[...] = held
        save = pltpu.make_async_copy(held_ref, over_hbm.at[u], sems.at[2])
        save.start()
        save.wait()
        hidden_over_ref[...], targets_over_ref[...] = expand(held)
        messages(hidden_over_ref[...], targets_over_ref[...], meta_ref[0, main + u], held)
        return carry

    lax.fori_loop(0, over_total, over_messages, 0)
    bias = dot(second_bias_ref[...], states, NT)
    summed = jnp.sum(total_ref[...].reshape(half_width, HALF, node_count), axis=1)
    counts = group_counts(counts_ref)
    counts_out_ref[...] = counts
    incoming_ref[...] = (summed + dot(bias.astype(BF16), counts)).astype(BF16)
    keep.wait()
    for blank in blanks:
        blank.wait()


def expand_tile(held, first_t, wide, node_count):
    low, high, within = tile_masks(held[17:18, :].astype(F32))
    pre = dot(first_t, held, TN)
    logistic = jax.nn.sigmoid(pre)
    hidden = halves(pre * logistic, low, high)
    slope = logistic * (1.0 + pre * (1.0 - logistic))
    spread = keep_within(dot(wide, target_hot(held[16:17, :].astype(F32), node_count)), within)
    return hidden, slope, spread


def widened(grad_ref):
    half_width, node_count = grad_ref.shape
    wide = jnp.broadcast_to(grad_ref[...].astype(F32)[:, None, :], (half_width, HALF, node_count))
    return wide.reshape(half_width * HALF, node_count).astype(BF16)


def hidden_slopes(held, table, spread, slope, first):
    low, _, _ = tile_masks(held[17:18, :].astype(F32))
    grad_hidden = dot(table, spread, TN)
    grad_hidden = jnp.where(low, grad_hidden[:LANES], grad_hidden[LANES:])
    grad_pre = (grad_hidden * slope).astype(BF16)
    return dot(first, grad_pre).astype(BF16), dot(held, grad_pre, NT)


def split_pair(held):
    tiles = held.shape[0]
    held = held.astype(F32)
    parts = []
    for q in range(2):
        rows = held[:, q * HALF : (q + 1) * HALF, :].reshape(tiles * HALF, 2 * LANES).astype(BF16)
        parts.append(jnp.concatenate([rows[:, :LANES], rows[:, LANES:]], axis=0))
    return jnp.concatenate(parts, axis=1)


def overflow_kernel(
    meta_ref, grad_hbm, first_hbm, first_bias_hbm, over_hbm, table_hbm, states_hbm, second_hbm, tile_hbm, lane_hbm,
    _grads, _rows, _feat, _first,
    grads_hbm, rows_hbm, feat_hbm, first_grad_hbm,
    grad_ref, first_ref, first_bias_ref, over_ref, states_ref, rows_ref, part_ref, feat_ref, first_grad_ref,
    grads_ref, weight_ref, outer_ref, table_ref, tile_ref, lane_ref, sem,
):
    total = jnp.maximum(meta_ref[1, 0] - MAIN, 0)

    def move(source, target):
        copy = pltpu.make_async_copy(source, target, sem)
        copy.start()
        copy.wait()

    @pl.when(total > 0)
    def _():
        half_width, node_count = grad_ref.shape
        move(grad_hbm, grad_ref)
        move(first_hbm, first_ref)
        move(first_bias_hbm, first_bias_ref)
        move(states_hbm, states_ref)
        move(second_hbm, weight_ref)
        move(tile_hbm, tile_ref)
        move(lane_hbm, lane_ref)
        first_grad_ref[...] = jnp.zeros_like(first_grad_ref)
        part_ref[...] = jnp.zeros_like(part_ref)
        rows_ref[...] = jnp.zeros_like(rows_ref)
        grads_ref[...] = jnp.zeros_like(grads_ref)
        first_t = extended_first(first_ref, first_bias_ref)
        wide = widened(grad_ref)

        def tile_work(u, carry):
            group = meta_ref[0, MAIN + u]
            move(table_hbm.at[group], table_ref)
            move(over_hbm.at[u], over_ref)
            held = over_ref[...]
            hidden, slope, spread = expand_tile(held, first_t, wide, node_count)
            outer_ref[0] = dot(spread, hidden, NT).astype(BF16)
            part, first_grad = hidden_slopes(held, table_ref[...], spread, slope, first_ref[...])
            part_ref[pl.ds(pl.multiple_of(u * 16, 16), 16), :] = part
            first_grad_ref[...] += first_grad
            states = jnp.concatenate([states_ref[0, group], states_ref[1, group]], axis=0).astype(BF16)

            def pair_work(p, carry):
                cols = pl.ds(pl.multiple_of(p * 2 * LANES, 2 * LANES), 2 * LANES)
                quarters = split_pair(outer_ref[:, pl.ds(pl.multiple_of(p * 16, 16), 16), :])
                product = dot(quarters, states, TN)
                grads_ref[:, cols] += jnp.concatenate([product[:LANES], product[LANES:]], axis=1)
                pair = weight_ref[:, cols]
                return carry + dot(quarters, jnp.concatenate([pair[:, :LANES], pair[:, LANES:]], axis=0))

            rows = lax.fori_loop(0, half_width // 2, pair_work, jnp.zeros((2 * HALF, LANES), F32))
            at = group * GROUP
            rows_ref[pl.ds(at, HALF), :] += rows[:HALF]
            rows_ref[pl.ds(at + HALF, HALF), :] += rows[HALF:]
            return carry

        lax.fori_loop(0, total, tile_work, 0)
        weight_ref[...] = grads_ref[...].astype(BF16)
        move(weight_ref, grads_hbm)
        move(rows_ref, rows_hbm)
        for c in range(tile_ref.shape[0]):
            hot = (iota((TILE, LANES), 0) == lane_ref[c : c + 1, :].astype(jnp.int32)).astype(F32).astype(BF16)
            moved = dot(part_ref[...], hot)
            tile = tile_ref[c : c + 1, :]
            part = jnp.zeros((16, LANES), F32)
            for u in range(part_ref.shape[0] // 16):
                part = part + jnp.where(tile == float(MAIN + u), moved[u * 16 : (u + 1) * 16], 0.0)
            feat_ref[c * 16 : (c + 1) * 16, :] = part
        move(feat_ref, feat_hbm)
        move(first_grad_ref, first_grad_hbm)


def mesh_signal(sem, peers):
    for peer in peers:
        pl.semaphore_signal(sem, inc=1, device_id=peer, device_id_type=pl.DeviceIdType.MESH)
    pl.semaphore_wait(sem, len(peers))


def node_kernel(
    ready, state_ref, mask_ref, input_ref, hidden_ref, input_bias_ref, hidden_bias_ref, cotangent_ref, incoming_ref, full_ref,
    message_grad_ref, new_ref, own_ref, partial_ref, weights_ref, biases_ref,
    other_ref, onto_ref, back_ref, send_sem, recv_sem,
):
    edge, gate = lax.axis_index("edge"), lax.axis_index("gate")
    partner = (edge, 1 - gate)
    half = state_ref.shape[0]
    mesh_signal(pltpu.get_barrier_semaphore(), [partner])
    swap = pltpu.make_async_remote_copy(
        incoming_ref, other_ref, send_sem.at[0], recv_sem.at[0], device_id=partner, device_id_type=pl.DeviceIdType.MESH
    )
    swap.start()
    ready()
    full = full_ref[...]
    biases = jnp.concatenate(
        [input_bias_ref[...].astype(F32), hidden_bias_ref[...].astype(F32), jnp.zeros((2, half), F32)], axis=0
    ).T
    hidden_pre = [dot(hidden_ref[k], full) + biases[:, 3 + k : 4 + k] for k in range(3)]
    keep = jnp.concatenate([mask_ref[c : c + 1, :] for c in range(mask_ref.shape[0])], axis=1).astype(F32)
    own = state_ref[...].astype(F32)
    grad_output = cotangent_ref[...].astype(F32) * keep
    mine = incoming_ref[...]
    swap.wait()
    other = other_ref[...]
    is_first = gate == 0
    message = jnp.concatenate(
        [jnp.where(is_first, mine, other), jnp.where(is_first, other, mine)], axis=0
    )
    input_pre = [dot(input_ref[k], message) + biases[:, k : k + 1] for k in range(3)]
    reset = jax.nn.sigmoid(input_pre[0] + hidden_pre[0])
    update = jax.nn.sigmoid(input_pre[1] + hidden_pre[1])
    candidate = jnp.tanh(input_pre[2] + reset * hidden_pre[2])
    grad_cand = grad_output * (1.0 - update) * (1.0 - candidate * candidate)
    grad_update = grad_output * (own - candidate) * update * (1.0 - update)
    grad_reset = grad_cand * hidden_pre[2] * reset * (1.0 - reset)
    grad_input = [grad_reset.astype(BF16), grad_update.astype(BF16), grad_cand.astype(BF16)]
    grad_hidden = [grad_input[0], grad_input[1], (grad_cand * reset).astype(BF16)]
    onto_ref[...] = sum(dot(input_ref[k], grad_input[k], TN) for k in range(3))
    back = pltpu.make_async_remote_copy(
        onto_ref.at[pl.ds(pl.multiple_of((1 - gate) * half, half), half)], back_ref, send_sem.at[1], recv_sem.at[1],
        device_id=partner, device_id_type=pl.DeviceIdType.MESH,
    )
    back.start()
    new_ref[...] = (keep * ((1.0 - update) * candidate + update * own)).astype(BF16)
    own_ref[...] = grad_output * update
    partial_ref[...] = sum(dot(hidden_ref[k], grad_hidden[k], TN) for k in range(3))
    for k in range(3):
        weights_ref[:, k * LANES : (k + 1) * LANES] = jnp.concatenate(
            [dot(grad_input[k], message, NT), dot(grad_hidden[k], full, NT)], axis=0
        ).astype(BF16)
    lane = iota((half, LANES), 1)
    sums = jnp.zeros((half, LANES), F32)
    for k, grad in enumerate(grad_input + grad_hidden):
        sums = jnp.where(lane == k, jnp.sum(grad.astype(F32), axis=1, keepdims=True), sums)
    biases_ref[...] = sums.T[:8]
    back.wait()
    kept = onto_ref[pl.ds(pl.multiple_of(gate * half, half), half), :]
    message_grad_ref[...] = (kept + back_ref[...]).astype(BF16)


def chunk_plan(units, digits):
    orders = [list(order) + list(range(3, digits)) for order in ORDERS]
    count = len(SIZES)
    sizes = SIZES
    if units != sum(SIZES):
        count = min(units, count)
        sizes = [units // count + (1 if i < units % count else 0) for i in range(count)]
    plan = [(sum(sizes[:i]), sizes[i], orders[i], 0 if i < FIRST_SPAN else 1) for i in range(count)]
    return plan, orders[-1]


def event_order(members, digits, tiles, backs, rows):
    if digits == 4 and len(members) == 2:
        return [(KINDS[code // 16], code % 16) for code in SCHEDULE]
    parts = len(members)
    steps = [[] for _ in range(parts + 2 * digits + 4)]
    for g in range(parts):
        if g > 0:
            steps[g].append(("span", g))
        steps[g] += [("chunk", c) for c in members[g]]
        for phase in range(2 * digits):
            steps[g + phase + 1] += [("go", c) for c in members[g]]
    at = parts
    steps[at] += [("rows", i) for i in range(rows)]
    steps[at].append(("sources", 0))
    for i in range(tiles):
        steps[at + i // 2].append(("tiles", i))
    steps[at + 1].append(("rim", 0))
    steps[at + 3].append(("state", 0))
    at += (tiles + 1) // 2
    for i in range(digits + 2):
        steps[min(at + i, len(steps) - 1)].append(("first", i))
    for i in range(backs):
        steps[min(at + i, len(steps) - 1)].append(("back", i))
    steps[min(at + backs, len(steps) - 1)].append(("feat", 0))
    return [event for step in steps for event in step]


def finish_kernel(
    digits, first_ref, first_bias_ref, second_bias_ref, weight_ref, meta_ref, grad_ref, states_ref, tiles_ref, hidden_ref,
    target_ref, table_hbm, grads_over_hbm, *rest,
):
    late_hbms, rest = rest[:11], rest[11:]
    total_ref, small_total_ref, feat_hbm, state_hbm, first_hbm, late_refs, *rest = rest
    finish_body(
        digits, meta_ref, grad_ref, states_ref, first_ref, first_bias_ref, second_bias_ref, weight_ref, tiles_ref, hidden_ref,
        target_ref, table_hbm, grads_over_hbm, late_hbms, total_ref, small_total_ref, feat_hbm, state_hbm, first_hbm, late_refs, *rest,
    )


def finish_body(
    digits, meta_ref, grad_ref, states_ref, first_ref, first_bias_ref, second_bias_ref, weight_ref, tiles_ref, hidden_ref,
    target_ref, table_hbm, grads_over_hbm, late_hbms, total_ref, small_total_ref, feat_hbm, state_hbm, first_hbm, late_refs, late_sem,
    feat_out_ref, state_out_ref,
    table_ref, grads_over_ref, wide_ref, spread_ref, outer_ref, quarters_ref, grads_ref,
    work_ref, land_refs, small_ref, part_ref, rows_ref, source_ref, first_sum_ref,
    first_land_ref, feat_ref, feat_land_ref, rows_send_ref, rows_land_ref, rim_send_ref, rim_land_ref,
    send_sem, recv_sem, side_send, side_recv, first_send, first_recv, fetch_sem,
):
    (
        slot_ref, counts_ref, rows_over_ref, feat_over_ref, first_over_ref, tile_ref, lane_ref, weights_ref,
        biases_ref, partial_ref, own_ref,
    ) = late_refs
    edge, gate = lax.axis_index("edge"), lax.axis_index("gate")
    count = 1 << digits
    half_width, node_count = grad_ref.shape
    main = tiles_ref.shape[0]
    padded = states_ref.shape[1]
    chunk_count = tile_ref.shape[0]
    slots = source_ref.shape[0]
    border = slots - node_count
    width = grads_ref.shape[1]
    partner = (edge, 1 - gate)
    before = (lax.rem(edge + count - 1, count), gate)
    after = (lax.rem(edge + 1, count), gate)
    peers = [(edge ^ (1 << d), gate) for d in range(digits)]
    bits = [lax.rem(lax.shift_right_logical(edge, d), 2) for d in range(digits)]
    greeted = peers + [partner, before, after]
    barrier = pltpu.get_barrier_semaphore()
    for peer in greeted:
        pl.semaphore_signal(barrier, inc=1, device_id=peer, device_id_type=pl.DeviceIdType.MESH)

    unit = LANES << (digits - 3)
    plan, small_order = chunk_plan(width // unit, digits)
    chunks = [
        (grads_ref, start * unit, start * unit, size * unit, order, group) for start, size, order, group in plan
    ]
    parts = chunks[-1][5] + 1
    chunks.append((small_ref, 0, width, small_ref.shape[1], small_order, parts - 1))
    members = [[c for c in range(len(chunks)) if chunks[c][5] == g] for g in range(parts)]
    spans = []
    for g in range(parts):
        ours = [chunks[c] for c in members[g] if chunks[c][0] is grads_ref]
        spans.append((ours[0][2] // (2 * LANES), (ours[-1][2] + ours[-1][3]) // (2 * LANES)))

    fetch_over = pltpu.make_async_copy(grads_over_hbm, grads_over_ref, fetch_sem.at[1])
    fetch_table = pltpu.make_async_copy(table_hbm, table_ref, fetch_sem.at[2])
    fetch_over.start()
    fetch_late = [
        pltpu.make_async_copy(source, target, late_sem.at[i])
        for i, (source, target) in enumerate(zip(late_hbms, late_refs))
    ]
    for fetch in fetch_late:
        fetch.start()

    def side(index, source, target, device):
        return pltpu.make_async_remote_copy(
            source, target, side_send.at[index], side_recv.at[index], device_id=device, device_id_type=pl.DeviceIdType.MESH
        )

    regions = []
    for _, _, place, lanes, order, _ in chunks:
        row, rows, lane = 0, 128, place
        levels = [(row, rows, lane, lanes)]
        for i, d in enumerate(order):
            if i < 3:
                rows //= 2
                row = row + bits[d] * rows
            else:
                lanes //= 2
                lane = lane + bits[d] * lanes
            levels.append((row, rows, lane, lanes))
        regions.append(levels)

    def window(row, rows, lane, lanes):
        if not isinstance(row, int):
            row = pl.multiple_of(row, 16)
        if not isinstance(lane, int):
            lane = pl.multiple_of(lane, LANES)
        return (pl.ds(row, rows), pl.ds(lane, lanes))

    def sibling(c, i):
        row, rows, lane, lanes = regions[c][i]
        d = chunks[c][4][i]
        if i < 3:
            return (row + (1 - bits[d]) * (rows // 2), rows // 2, lane, lanes)
        return (row, rows, lane + (1 - bits[d]) * (lanes // 2), lanes // 2)

    def landing(c, i):
        _, rows, _, lanes = regions[c][i + 1]
        return land_refs[i].at[pl.ds(0, rows), pl.ds(chunks[c][2] >> max(0, i - 2), lanes)]

    def inside(c, window_):
        source, at, place = chunks[c][:3]
        row, rows, lane, lanes = window_
        return source, window(row, rows, lane - place + at, lanes)

    def total_at(c, window_):
        row, rows, lane, lanes = window_
        if chunks[c][0] is small_ref:
            return small_total_ref, window(row, rows, lane - width, lanes)
        return total_ref, window(row, rows, lane, lanes)

    def scatter(c, i):
        if i == 0:
            source, at = inside(c, sibling(c, i))
            source = source.at[at]
        else:
            source = work_ref.at[window(*sibling(c, i))]
        return pltpu.make_async_remote_copy(
            source, landing(c, i), send_sem.at[c, i], recv_sem.at[c, i],
            device_id=peers[chunks[c][4][i]], device_id_type=pl.DeviceIdType.MESH,
        )

    def gather(c, i):
        ref, at = total_at(c, regions[c][i + 1])
        return pltpu.make_async_remote_copy(
            ref.at[at], ref.at[at], send_sem.at[c, 2 * digits - 1 - i], recv_sem.at[c, 2 * digits - 1 - i],
            device_id=peers[chunks[c][4][i]], device_id_type=pl.DeviceIdType.MESH,
        )

    def start(c, phase):
        if phase < digits:
            scatter(c, phase).start()
        elif phase < 2 * digits:
            gather(c, 2 * digits - 1 - phase).start()

    def arrive(c, phase):
        if phase < digits:
            scatter(c, phase).wait_recv()
            kept = regions[c][phase + 1]
            if phase == 0:
                source, at = inside(c, kept)
            else:
                source, at = work_ref, window(*kept)
            landed = landing(c, phase)
            value = source[at].astype(F32) + landed[...].astype(F32)
            if phase == digits - 1:
                target, at = total_at(c, kept)
            else:
                target, at = work_ref, window(*kept)
            target[at] = value.astype(BF16)
        else:
            gather(c, 2 * digits - 1 - phase).wait_recv()

    wide_ref[...] = widened(grad_ref)
    states = jnp.concatenate([states_ref[a, meta_ref[0, t]] for a in range(2) for t in range(main)], axis=0).astype(BF16)

    def pair_grads(p, first_pair):
        quarters = split_pair(outer_ref[:, pl.ds(aligned(p - first_pair, 16), 16), :])
        cols = pl.ds(aligned(p, 2 * LANES), 2 * LANES)
        quarters_ref[p] = quarters
        product = dot(quarters, states, TN)
        product = jnp.concatenate([product[:LANES], product[LANES:]], axis=1)
        grads_ref[:, cols] = (product + grads_over_ref[:, cols].astype(F32)).astype(BF16)

    def pair_rows(first, last):
        if first == 0:
            rows_ref[...] = jnp.zeros_like(rows_ref)

        def pair(p):
            weight = weight_ref[:, pl.ds(aligned(first + p, 2 * LANES), 2 * LANES)]
            weight = jnp.concatenate([weight[:, :LANES], weight[:, LANES:]], axis=0)
            rows_ref[...] += dot(quarters_ref[first + p], weight)

        tile_loop(last - first, pair, UNROLL_ROWS)

    def span_outer(g):
        first, last = spans[g]
        rows = pl.ds(first * 16, (last - first) * 16)

        def spread(t):
            _, _, within = tile_masks(tiles_ref[t, 17:18, :].astype(F32))
            spread_ref[t, rows, :] = keep_within(dot(wide_ref[rows, :], target_ref[t]), within)

        def outer(t):
            outer_ref[t, : (last - first) * 16, :] = dot(spread_ref[t, rows, :], hidden_ref[t], NT).astype(BF16)

        tile_loop(main, spread, UNROLL_SPAN)
        tile_loop(main, outer, UNROLL_SPAN)

    settled = {}

    def settle():
        if not settled:
            for fetch in fetch_late:
                fetch.wait()
            settled["first"] = extended_first(first_ref, first_bias_ref)
            settled["sums"] = dot(counts_ref[...], grad_ref[...], NT).astype(BF16)

    def fill_small():
        settle()
        small_ref[...] = jnp.zeros_like(small_ref)
        small_ref[:half_width, :LANES] = dot(settled["sums"], group_states(states_ref), TN).astype(BF16)
        small_ref[half_width + ROWS : half_width + ROWS + 16, : biases_ref.shape[1]] = jnp.concatenate(
            [biases_ref[...], jnp.zeros_like(biases_ref)], axis=0
        ).astype(BF16)
        small_ref[:, LANES : 4 * LANES] = weights_ref[...]

    def chunk_grads(c):
        if chunks[c][0] is grads_ref:
            first = chunks[c][2] // (2 * LANES)
            tile_loop(
                chunks[c][3] // (2 * LANES), lambda p: pair_grads(first + p, spans[chunks[c][5]][0]), UNROLL_PAIRS
            )
        else:
            fill_small()
        start(c, 0)

    span_outer(0)
    fetch_over.wait()
    fetch_table.start()
    pl.semaphore_wait(barrier, len(greeted))

    rows_copy = side(1, rows_send_ref, rows_land_ref, partner)
    rim_copy = side(2, rim_send_ref, rim_land_ref, before)
    feat_copy = side(3, feat_ref, feat_land_ref, partner)
    state_store = pltpu.make_async_copy(state_out_ref, state_hbm, late_sem.at[0])
    first_store = pltpu.make_async_copy(first_sum_ref, first_hbm, late_sem.at[1])
    feat_store = pltpu.make_async_copy(feat_out_ref, feat_hbm, late_sem.at[2])

    def source_rows():
        settle()
        rows = slot_ref[0:1, : 2 * main * HALF].astype(jnp.int32)
        hot = (iota((slots, 2 * main * HALF), 0) == rows).astype(F32).astype(BF16)
        source_ref[...] = dot(hot, rows_ref[...].astype(BF16)) + rows_over_ref[:slots, :]
        bias = dot(settled["sums"], second_bias_ref[...])
        for g in range(padded):
            for a in range(2):
                at = g * GROUP + a * HALF
                size = min(HALF, GROUP - a * HALF, slots - at)
                if size > 0:
                    source_ref[at : at + size, :] += bias[(a * padded + g) * HALF : (a * padded + g) * HALF + size]
        source_ref[border:, :] += partial_ref[...].T
        rows_send_ref[...] = source_ref[...].astype(BF16)
        rows_copy.start()

    def rim_rows():
        rows_copy.wait()
        source_ref[...] += rows_land_ref[...].astype(F32)
        rim_send_ref[...] = source_ref[:border, :].astype(BF16)
        rim_copy.start()

    def state_rows():
        rim_copy.wait()
        source_ref[slots - border :, :] += rim_land_ref[...].astype(F32)
        rows = source_ref[border:, :].T
        state_out_ref[...] = jnp.where(gate == 0, rows[:half_width], rows[half_width:]) + own_ref[...]
        state_store.start()

    table_ready = []

    def tile_grads(first, last):
        settle()
        if not table_ready:
            fetch_table.wait()
            table_ready.append(True)
            first_sum_ref[...] = first_over_ref[...]

        def tile(t):
            t = first + t
            held = tiles_ref[t]
            pre = dot(settled["first"], held, TN)
            logistic = jax.nn.sigmoid(pre)
            slope = logistic * (1.0 + pre * (1.0 - logistic))
            table = table_ref[meta_ref[0, t]]
            part, first_grad = hidden_slopes(held, table, spread_ref[t], slope, first_ref[...])
            part_ref[pl.ds(aligned(t, 16), 16), :] = part
            first_sum_ref[...] += first_grad

        tile_loop(last - first, tile, UNROLL_TILES)

    def first_copy(i):
        device = partner if i == 0 else peers[i - 1]
        return pltpu.make_async_remote_copy(
            first_land_ref.at[2 * i], first_land_ref.at[2 * i + 1], first_send.at[i], first_recv.at[i],
            device_id=device, device_id_type=pl.DeviceIdType.MESH,
        )

    def first_step(i):
        if i > 0:
            first_copy(i - 1).wait()
            first_sum_ref[...] = first_land_ref[2 * i - 2] + first_land_ref[2 * i - 1]
        if i <= digits:
            first_land_ref[2 * i] = first_sum_ref[...]
            first_copy(i).start()
        else:
            first_store.start()

    def back(first, last):
        def chunk(c):
            c = first + 2 * c
            lane = jnp.concatenate([lane_ref[c : c + 1, :], lane_ref[c + 1 : c + 2, :]], axis=1).astype(jnp.int32)
            hot = (iota((TILE, 2 * LANES), 0) == lane).astype(F32).astype(BF16)
            moved = dot(part_ref[...], hot)
            tile = jnp.concatenate([tile_ref[c : c + 1, :], tile_ref[c + 1 : c + 2, :]], axis=1)
            total = jnp.concatenate([feat_over_ref[c * 16 : (c + 1) * 16], feat_over_ref[(c + 1) * 16 : (c + 2) * 16]], axis=1)
            for t in range(main):
                total = total + jnp.where(tile == float(t), moved[t * 16 : (t + 1) * 16], 0.0)
            feat_ref[:, c * LANES : (c + 2) * LANES] = total

        for c in range((last - first) // 2):
            chunk(c)
        if last == chunk_count:
            feat_copy.start()

    def feat_total():
        feat_copy.wait()
        feat_out_ref[...] = feat_ref[...] + feat_land_ref[...]
        feat_store.start()

    batch = TILE_BATCH
    tile_batches = range(0, main, batch)
    back_batches = range(0, chunk_count, 8)
    row_batches = range(0, half_width // 2, 8)
    done = [0] * len(chunks)

    def go(c):
        arrive(c, done[c])
        start(c, done[c] + 1)
        done[c] += 1

    actions = {
        "span": span_outer,
        "chunk": chunk_grads,
        "go": go,
        "tiles": lambda i: tile_grads(tile_batches[i], min(tile_batches[i] + batch, main)),
        "first": first_step,
        "rows": lambda i: pair_rows(row_batches[i], row_batches[i] + 8),
        "back": lambda i: back(back_batches[i], min(back_batches[i] + 8, chunk_count)),
        "sources": lambda i: source_rows(),
        "rim": lambda i: rim_rows(),
        "state": lambda i: state_rows(),
        "feat": lambda i: feat_total(),
    }
    for name, i in event_order(members, digits, len(tile_batches), len(back_batches), len(row_batches)):
        actions[name](i)

    for c in range(len(chunks)):
        for phase in range(2 * digits):
            if phase < digits:
                scatter(c, phase).wait_send()
            else:
                gather(c, 2 * digits - 1 - phase).wait_send()
    for copy in (state_store, first_store, feat_store):
        copy.wait()


def emit_kernel(
    total_ref, small_ref, first_in_ref, new_in_ref, state_in_ref, feat_in_ref,
    new_ref, state_ref, feat_ref, first_ref, first_bias_ref, second_out, second_bias_ref, input_ref, hidden_ref,
    input_bias_ref, hidden_bias_ref,
    wide_ref, sems,
):
    blocks = sems.shape[0]
    size = wide_ref.shape[1] // blocks
    writes = []
    for i in range(blocks):
        cols = pl.ds(i * size, size)
        wide_ref[:, cols] = total_ref[:, cols].astype(F32)
        writes.append(pltpu.make_async_copy(wide_ref.at[:, cols], second_out.at[:, cols], sems.at[i]))
        writes[i].start()
    new_ref[...] = new_in_ref[...]
    state_ref[...] = state_in_ref[...]
    feat_ref[...] = feat_in_ref[...]
    small = small_ref[:, : 4 * LANES].astype(F32)
    half = second_bias_ref.shape[0]
    second_bias_ref[...] = small[:half, :LANES]
    first_ref[...] = first_in_ref[:16]
    first_bias_ref[...] = first_in_ref[18:19]
    part = input_ref.shape[1]
    at = half + ROWS
    input_bias_ref[...] = small[at : at + 3, :part]
    hidden_bias_ref[...] = small[at + 3 : at + 6, :part]
    for k in range(3):
        input_ref[k] = small[:part, LANES + k * LANES : LANES + (k + 1) * LANES]
        hidden_ref[k] = small[part:, LANES + k * LANES : LANES + (k + 1) * LANES]
    for copy in writes:
        copy.wait()


def per_device(
    node_state, edge_feat, source, target, edge_mask, node_mask, net_first, net_first_bias, net_second,
    net_second_bias, gru_input, gru_hidden, gru_input_bias, gru_hidden_bias, cotangent,
):
    node_count, half_width = node_state.shape
    edge_count = source.shape[0]
    width = 2 * half_width
    chunks = edge_count // LANES
    slots = BORDER + node_count
    groups = -(-slots // GROUP)
    padded = (groups + 1) // 2 * 2
    over = groups + edge_count // TILE - 1 - MAIN
    first_bias = net_first_bias.reshape(1, width)
    second_bias = net_second_bias.reshape(half_width, width)
    shape = jax.ShapeDtypeStruct
    vmem = pl.BlockSpec(memory_space=pltpu.VMEM)
    smem = pl.BlockSpec(memory_space=pltpu.SMEM)
    hbm = pl.BlockSpec(memory_space=pl.ANY)

    def local(mib):
        return pltpu.CompilerParams(vmem_limit_bytes=mib * MIB)

    def remote(collective_id, mib):
        return pltpu.CompilerParams(vmem_limit_bytes=mib * MIB, collective_id=collective_id, has_side_effects=True)

    state_t = node_state.T
    operands = in_hbm(
        source.reshape(chunks, LANES), target.reshape(chunks, LANES), edge_mask.reshape(chunks, LANES), edge_feat, state_t
    )
    body, specs, scratch = fetched(place_kernel, operands)
    weights = in_hbm(net_second, second_bias, net_first, first_bias)
    second_near, second_bias_near, first_near, first_bias_near, full_t, states, placed, values, tile_rows, lane_rows, meta, slot_rows = pl.pallas_call(
        body,
        out_shape=tuple(shape(x.shape, x.dtype) for x in weights)
        + (
            shape((width, node_count), BF16),
            shape((2, padded, HALF, width), F32),
            shape((MAIN, ROWS, TILE), BF16),
            shape((ROWS, edge_count), BF16),
            shape((chunks, LANES), F32),
            shape((chunks, LANES), F32),
            shape((8, LANES), jnp.int32),
            shape((8, -(-2 * MAIN * HALF // LANES) * LANES), F32),
        ),
        in_specs=specs + [hbm] * 4,
        out_specs=(vmem,) * 12,
        scratch_shapes=[
            pltpu.VMEM((chunks * ROWS, LANES), BF16),
            pltpu.VMEM((MAIN * 16 + 3 * ROWS, edge_count), BF16),
            pltpu.VMEM((TILE, edge_count), BF16),
            pltpu.VMEM((half_width, node_count), BF16),
            pltpu.VMEM((2, half_width, LANES), BF16),
            pltpu.SemaphoreType.DMA((3,)),
            pltpu.SemaphoreType.DMA((3,)),
            pltpu.SemaphoreType.DMA((4,)),
        ]
        + scratch,
        compiler_params=remote(0, 20),
        name="place_edges",
    )(*operands, *weights)

    blank_shapes = (
        pltpu.HBM((width, half_width * width), BF16),
        pltpu.HBM((padded * GROUP + 16, width), F32),
        pltpu.HBM((chunks * 16, LANES), F32),
        pltpu.HBM((ROWS, width), F32),
    )
    incoming, over_tiles, counts, table, hidden, targets, *blanks = pl.pallas_call(
        forward_kernel,
        out_shape=(
            shape((half_width, node_count), BF16),
            pltpu.HBM((over, ROWS, TILE), BF16),
            shape((2 * padded * HALF, node_count), BF16),
            pltpu.HBM((padded, half_width * HALF, 2 * width), BF16),
            shape((MAIN, 2 * width, TILE), BF16),
            shape((MAIN, node_count, TILE), BF16),
        )
        + blank_shapes,
        in_specs=[vmem] * 4 + [smem, vmem] + [hbm] * 3 + [vmem],
        out_specs=(vmem, hbm, vmem, hbm, vmem, vmem) + (hbm,) * 4,
        scratch_shapes=[
            pltpu.VMEM((padded, 16, node_count), F32),
            pltpu.VMEM((padded, half_width * HALF, 2 * width), BF16),
            pltpu.VMEM((2 * width, TILE), BF16),
            pltpu.VMEM((node_count, TILE), BF16),
            pltpu.VMEM((TILE, edge_count), BF16),
            pltpu.VMEM((half_width * HALF, node_count), F32),
            pltpu.VMEM((width, half_width * width), BF16),
            pltpu.VMEM((max(padded * GROUP + 16, chunks * 16), width), F32),
            pltpu.VMEM((ROWS, edge_count), BF16),
            pltpu.VMEM((chunks, LANES), F32),
            pltpu.VMEM((chunks, LANES), F32),
            pltpu.VMEM((ROWS, TILE), BF16),
            pltpu.SemaphoreType.DMA((3,)),
            pltpu.SemaphoreType.DMA((4,)),
        ],
        compiler_params=local(28),
        name="forward_edges",
    )(first_near, first_bias_near, second_bias_near, second_near, meta, placed, values, tile_rows, lane_rows, states)

    operands = in_hbm(
        state_t, node_mask.reshape(node_count // LANES, LANES), gru_input.swapaxes(1, 2), gru_hidden.swapaxes(1, 2),
        gru_input_bias, gru_hidden_bias, cotangent.T
    )
    body, specs, scratch = fetched(node_kernel, operands)
    message_grad, new_state, grad_own, state_partial, weight_grads, bias_grads = pl.pallas_call(
        body,
        out_shape=(
            shape((half_width, node_count), BF16),
            shape((half_width, node_count), BF16),
            shape((half_width, node_count), F32),
            shape((width, node_count), F32),
            shape((width, 3 * width), BF16),
            shape((8, half_width), F32),
        ),
        in_specs=specs + [vmem] * 2,
        out_specs=(vmem,) * 6,
        scratch_shapes=[
            pltpu.VMEM((half_width, node_count), BF16),
            pltpu.VMEM((width, node_count), F32),
            pltpu.VMEM((half_width, node_count), F32),
            pltpu.SemaphoreType.DMA((2,)),
            pltpu.SemaphoreType.DMA((2,)),
        ]
        + scratch,
        compiler_params=remote(1, 6),
        name="node_update",
    )(*operands, incoming, full_t)

    grads_over, rows_over, feat_over, first_over = pl.pallas_call(
        overflow_kernel,
        out_shape=blank_shapes,
        in_specs=[smem] + [hbm] * 13,
        out_specs=(hbm,) * 4,
        scratch_shapes=[
            pltpu.VMEM((half_width, node_count), BF16),
            pltpu.VMEM((16, width), BF16),
            pltpu.VMEM((1, width), BF16),
            pltpu.VMEM((ROWS, TILE), BF16),
            pltpu.VMEM((2, padded, HALF, width), F32),
            pltpu.VMEM((padded * GROUP + 16, width), F32),
            pltpu.VMEM((over * 16, TILE), BF16),
            pltpu.VMEM((chunks * 16, LANES), F32),
            pltpu.VMEM((ROWS, width), F32),
            pltpu.VMEM((width, half_width * width), F32),
            pltpu.VMEM((width, half_width * width), BF16),
            pltpu.VMEM((1, half_width * HALF, 2 * width), BF16),
            pltpu.VMEM((half_width * HALF, 2 * width), BF16),
            pltpu.VMEM((chunks, LANES), F32),
            pltpu.VMEM((chunks, LANES), F32),
            pltpu.SemaphoreType.DMA,
        ],
        input_output_aliases={10 + i: i for i in range(4)},
        compiler_params=local(16),
        name="overflow_edges",
    )(meta, message_grad, *in_hbm(net_first, first_bias), *in_hbm(over_tiles, table), states, *in_hbm(net_second), tile_rows, lane_rows,
        *in_hbm(*blanks),
    )

    digits = (lax.axis_size("edge") - 1).bit_length()
    unit = LANES << (digits - 3)
    columns = half_width * width
    small_width = max(4 * LANES, unit)
    steps = min(columns // unit, len(SIZES)) + 1
    whole = columns + small_width
    plan, _ = chunk_plan(columns // unit, digits)
    span = max(sum(p[1] for p in plan if p[3] == g) for g in range(2)) * unit // (2 * LANES)
    late = (
        slot_rows, counts, *in_hbm(rows_over, feat_over, first_over), tile_rows, lane_rows, weight_grads, bias_grads,
        state_partial, grad_own,
    )
    total, small_total, grad_feat, grad_state, first_sum = pl.pallas_call(
        functools.partial(finish_kernel, digits),
        out_shape=(
            pltpu.VMEM((width, columns), BF16),
            pltpu.VMEM((width, small_width), BF16),
            shape((16, edge_count), F32),
            shape((half_width, node_count), F32),
            shape((ROWS, width), F32),
        ),
        in_specs=[vmem] * 4 + [smem] + [vmem] * 5 + [hbm] * 13,
        out_specs=(vmem, vmem, hbm, hbm, hbm),
        scratch_shapes=[
            [pltpu.VMEM(x.shape, x.dtype) for x in late],
            pltpu.SemaphoreType.DMA((len(late),)),
            pltpu.VMEM((16, edge_count), F32),
            pltpu.VMEM((half_width, node_count), F32),
            pltpu.VMEM((padded, half_width * HALF, 2 * width), BF16),
            pltpu.VMEM((width, columns), BF16),
            pltpu.VMEM((half_width * HALF, node_count), BF16),
            pltpu.VMEM((MAIN, half_width * HALF, TILE), BF16),
            pltpu.VMEM((MAIN, 16 * span, 2 * width), BF16),
            pltpu.VMEM((half_width // 2, 2 * MAIN * HALF, 2 * width), BF16),
            pltpu.VMEM((width, columns), BF16),
            pltpu.VMEM((width, whole), BF16),
            [pltpu.VMEM((max(16, width >> (i + 1)), whole >> max(0, i - 2)), BF16) for i in range(digits)],
            pltpu.VMEM((width, small_width), BF16),
            pltpu.VMEM((MAIN * 16, TILE), BF16),
            pltpu.VMEM((2 * MAIN * HALF, width), F32),
            pltpu.VMEM((slots, width), F32),
            pltpu.VMEM((ROWS, width), F32),
            pltpu.VMEM((2 * digits + 2, ROWS, width), F32),
            pltpu.VMEM((16, edge_count), F32),
            pltpu.VMEM((16, edge_count), F32),
            pltpu.VMEM((slots, width), BF16),
            pltpu.VMEM((slots, width), BF16),
            pltpu.VMEM((BORDER, width), BF16),
            pltpu.VMEM((BORDER, width), BF16),
            pltpu.SemaphoreType.DMA((steps, 2 * digits)),
            pltpu.SemaphoreType.DMA((steps, 2 * digits)),
            pltpu.SemaphoreType.DMA((4,)),
            pltpu.SemaphoreType.DMA((4,)),
            pltpu.SemaphoreType.DMA((digits + 1,)),
            pltpu.SemaphoreType.DMA((digits + 1,)),
            pltpu.SemaphoreType.DMA((3,)),
        ],
        compiler_params=remote(2, 38),
        name="finish_sums",
    )(
        first_near, first_bias_near, second_bias_near, second_near, meta, message_grad, states, placed, hidden, targets,
        *in_hbm(table, grads_over), *late,
    )

    blocks = 8
    outs = pl.pallas_call(
        emit_kernel,
        out_shape=(
            shape((half_width, node_count), BF16),
            shape((half_width, node_count), F32),
            shape((16, edge_count), F32),
            shape((16, width), F32),
            shape((1, width), F32),
            shape((width, columns), F32),
            shape((half_width, width), F32),
            shape((3, half_width, width), F32),
            shape((3, half_width, width), F32),
            shape((3, half_width), F32),
            shape((3, half_width), F32),
        ),
        in_specs=[vmem] * 6,
        out_specs=(vmem,) * 5 + (hbm,) + (vmem,) * 5,
        scratch_shapes=[
            pltpu.VMEM((width, columns), F32),
            pltpu.SemaphoreType.DMA((blocks,)),
        ],
        compiler_params=local(12),
        name="emit",
    )(total, small_total, first_sum, new_state, grad_state, grad_feat)
    outs = list(outs)
    outs[0], outs[1] = outs[0].T, outs[1].T
    outs[7], outs[8] = outs[7].swapaxes(1, 2), outs[8].swapaxes(1, 2)
    outs[4] = outs[4].reshape(width)
    outs[6] = outs[6].reshape(columns)
    return tuple(outs)


def solution(mesh):
    return jax.shard_map(
        per_device,
        mesh=mesh,
        in_specs=(
            P("edge", "gate"), P(None, "edge"), P("edge"), P("edge"), P("edge"), P("edge"), P(), P(), P(None, "gate"),
            P("gate"), P(None, None, "gate"), P(None, None, "gate"), P(None, "gate"), P(None, "gate"), P("edge", "gate"),
        ),
        out_specs=(
            P("edge", "gate"), P("edge", "gate"), P(None, "edge"), P(), P(), P(None, "gate"), P("gate"),
            P(None, None, "gate"), P(None, None, "gate"), P(None, "gate"), P(None, "gate"),
        ),
        check_vma=False,
    )
```
